32 devices in a mesh: tm: 8 (over z, y), items: 4 (over x, core).
Axes of the slice: x: 2, y: 2, z: 4, core: 2. Of those that a mesh axis runs over, the one named last changes fastest.
Arguments:
- source_one: float32 [32, 128, 4096], P('items', None, 'tm')
- source_two: float32 [32, 128, 4096], P('items', None, 'tm')
- offsets: int32 [32], P('items'), may hold values from 1 to 512
- lengths: int32 [32], P('items'), may hold values from 3968 to 4096
- gain_one: float32 [128], replicated, may hold values from 0.5 to 1.5
- gain_two: float32 [128], replicated, may hold values from 0.5 to 1.5
- w_in: float32 [512, 128], replicated, may hold values from -0.5 to 0.5
- b_in: float32 [512], replicated, may hold values from -3 to 3
- slope_one: float32 [512], replicated, may hold values from 0.05 to 0.45
- first_norm_gain: float32 [512], replicated, may hold values from 0.5 to 1.5
- first_norm_bias: float32 [512], replicated, may hold values from -2 to 2
- depthwise_weight: float32 [512, 3], replicated, may hold values from -3.5 to 3.5
- depthwise_bias: float32 [512], replicated, may hold values from -2 to 2
- slope_two: float32 [512], replicated, may hold values from 0.05 to 0.45
- second_norm_gain: float32 [512], replicated, may hold values from 0.5 to 1.5
- second_norm_bias: float32 [512], replicated, may hold values from -2 to 2
- w_res: float32 [128, 512], replicated, may hold values from -0.5 to 0.5
- b_res: float32 [128], replicated, may hold values from -2 to 2
- w_skip: float32 [128, 512], replicated, may hold values from -0.25 to 0.25
- b_skip: float32 [128], replicated, may hold values from -2 to 2
- cot_res: float32 [32, 128, 4096], P('items', None, 'tm'), may hold values from -6 to 6
- cot_skip: float32 [32, 128, 4096], P('items', None, 'tm'), may hold values from -6 to 6
Outputs:
- residual_out: float32 [32, 128, 4096], P('items', None, 'tm')
- skip_out: float32 [32, 128, 4096], P('items', None, 'tm')
- grad_source_one: float32 [32, 128, 4096], P('items', None, 'tm')
- grad_source_two: float32 [32, 128, 4096], P('items', None, 'tm')
- grad_gain_one: float32 [128], replicated
- grad_gain_two: float32 [128], replicated
- grad_w_in: float32 [512, 128], replicated
- grad_b_in: float32 [512], replicated
- grad_slope_one: float32 [512], replicated
- grad_gamma_one: float32 [512], replicated
- grad_beta_one: float32 [512], replicated
- grad_w_depth: float32 [512, 3], replicated
- grad_b_depth: float32 [512], replicated
- grad_slope_two: float32 [512], replicated
- grad_gamma_two: float32 [512], replicated
- grad_beta_two: float32 [512], replicated
- grad_w_res: float32 [128, 512], replicated
- grad_b_res: float32 [128], replicated
- grad_w_skip: float32 [128, 512], replicated
- grad_b_skip: float32 [128], replicated
The draws below stay inside these ranges and needn't reach their ends.
All inputs are finite; a program needn't handle non-finite values.
Results may differ from the reference program's by a relative error of at most 0.0003.
Values sent between devices are 32-bit elements; how exact they have to be, the bound alone decides.
A program may use at most 128 MiB of HBM per device.

```python
import jax
import jax.numpy as jnp
from jax import lax

B = 128
H = 512
P_SIZE = 3
DILATION_RATE = 16
SPAN = 512
FRAMES = 4096
ITEMS = 32


def ramped(key):
    place = jnp.arange(FRAMES, dtype=jnp.float32) / (FRAMES - 1)
    base = jax.random.normal(key, (ITEMS, B, FRAMES), jnp.float32)
    rise = 1.0 + 2.0 * place
    return (base * rise).astype(jnp.float32)


def draw_source_one(key, part):
    key = jax.random.fold_in(key, 11)
    return ramped(key)


def draw_source_two(key, part):
    key = jax.random.fold_in(key, 23)
    return ramped(key)


def set_ends(array, rng, least, largest):
    longest = array.shape.index(max(array.shape))
    spots = []
    for shift in (0, 1):
        where = [jax.random.randint(jax.random.fold_in(rng, axis), (), 0, length) for axis, length in enumerate(array.shape)]
        where[longest] = (where[longest] + shift) % array.shape[longest]
        spots.append(tuple(where))
    return array.at[spots[0]].set(least).at[spots[1]].set(largest)


def block_scale(key, shape, split, low, top_value):
    factor_of = 1.0
    for position, shards_of in split:
        steps = jax.random.uniform(jax.random.fold_in(jax.random.fold_in(key, 6), position), (shards_of,), jnp.float32, low / len(split), top_value / len(split))
        factor_of = factor_of * jnp.repeat(jnp.exp(steps), shape[position] // shards_of).reshape((-1,) + (1,) * (len(shape) - 1 - position))
    return factor_of


def bell_draw(rng, shape, scale, reach, shards=(), kind=jnp.bfloat16):
    drawn = scale * jax.random.normal(rng, shape, jnp.float32)
    if shards:
        drawn = drawn * block_scale(rng, shape, shards, -0.22, 0.18)
    return jnp.clip(drawn, -reach, reach).astype(kind)


def setup_inputs(seed: int = 0) -> dict:
    seeds = jax.random.split(jax.random.key(seed), 23)
    source_one = draw_source_one(jax.random.fold_in(seeds[22], 71), 0)
    source_two = draw_source_two(jax.random.fold_in(seeds[22], 71), 0)
    offsets = set_ends(jax.random.randint(seeds[2], (ITEMS,), 1, SPAN + 1), jax.random.fold_in(seeds[2], 1), 1, SPAN).astype(jnp.int32)
    lengths = set_ends(jax.random.randint(seeds[3], (ITEMS,), FRAMES - FRAMES // 32, FRAMES + 1), jax.random.fold_in(seeds[3], 1), FRAMES - FRAMES // 32, FRAMES).astype(jnp.int32)
    gain_one = jnp.clip(1.0 + 0.1 * jax.random.normal(seeds[4], (B,), jnp.float32), 0.5, 1.5)
    gain_two = jnp.clip(1.0 + 0.1 * jax.random.normal(seeds[5], (B,), jnp.float32), 0.5, 1.5)
    w_in = bell_draw(seeds[6], (H, B), B ** -0.5, 0.5, (), jnp.float32)
    b_in = bell_draw(seeds[7], (H,), 0.5, 3.0, (), jnp.float32)
    slope_one = jnp.clip(jax.random.uniform(seeds[8], (H,), jnp.float32, 0.05, 0.45), 0.05, 0.45)
    first_norm_gain = jnp.clip(1.0 + 0.1 * jax.random.normal(seeds[9], (H,), jnp.float32), 0.5, 1.5)
    first_norm_bias = bell_draw(seeds[10], (H,), 0.3, 2.0, (), jnp.float32)
    depthwise_weight = bell_draw(seeds[11], (H, P_SIZE), P_SIZE ** -0.5, 3.5, (), jnp.float32)
    depthwise_bias = bell_draw(seeds[12], (H,), 0.3, 2.0, (), jnp.float32)
    slope_two = jnp.clip(jax.random.uniform(seeds[13], (H,), jnp.float32, 0.05, 0.45), 0.05, 0.45)
    second_norm_gain = jnp.clip(1.0 + 0.1 * jax.random.normal(seeds[14], (H,), jnp.float32), 0.5, 1.5)
    second_norm_bias = bell_draw(seeds[15], (H,), 0.3, 2.0, (), jnp.float32)
    w_res = bell_draw(seeds[16], (B, H), (H // 4) ** -0.5, 0.5, (), jnp.float32)
    b_res = bell_draw(seeds[17], (B,), 0.3, 2.0, (), jnp.float32)
    w_skip = bell_draw(seeds[18], (B, H), H ** -0.5, 0.25, (), jnp.float32)
    b_skip = bell_draw(seeds[19], (B,), 0.3, 2.0, (), jnp.float32)
    cot_res = bell_draw(seeds[20], (ITEMS, B, FRAMES), 1.0, 6.0, ((0, 4), (2, 8)), jnp.float32)
    cot_skip = bell_draw(seeds[21], (ITEMS, B, FRAMES), 1.0, 6.0, ((0, 4), (2, 8)), jnp.float32)
    return {"source_one": source_one, "source_two": source_two, "offsets": offsets, "lengths": lengths, "gain_one": gain_one, "gain_two": gain_two, "w_in": w_in, "b_in": b_in, "slope_one": slope_one, "first_norm_gain": first_norm_gain, "first_norm_bias": first_norm_bias, "depthwise_weight": depthwise_weight, "depthwise_bias": depthwise_bias, "slope_two": slope_two, "second_norm_gain": second_norm_gain, "second_norm_bias": second_norm_bias, "w_res": w_res, "b_res": b_res, "w_skip": w_skip, "b_skip": b_skip, "cot_res": cot_res, "cot_skip": cot_skip}


@jax.custom_vjp
def low(v):
    return lax.optimization_barrier(v.astype(jnp.bfloat16)).astype(jnp.float32)

@jax.custom_vjp
def low_back(v):
    return v

def low_keep(v):
    return (low(v), None)

def low_pass(kept, grad):
    return (grad,)

def back_keep(v):
    return (v, None)

def back_low(kept, grad):
    return (low(grad),)
low.defvjp(low_keep, low_pass)
low_back.defvjp(back_keep, back_low)

def soft_prelu(value_input, slope):
    return slope * value_input + (1.0 - slope) * jax.nn.softplus(value_input)

def global_norm(value_input, frame_mask, element_count, norm_gain, norm_shift):
    global_mean = jnp.sum(frame_mask * value_input) / element_count
    spread = jnp.sum(frame_mask * (value_input - global_mean) ** 2) / element_count
    return norm_gain[:, None] * ((value_input - global_mean) * lax.rsqrt(spread + 1e-05)) + norm_shift[:, None]

def one_item(src_one, src_two, delay, length, params):
    gain_one, gain_two, w_in, b_in, slope_one, first_norm_gain, first_norm_bias, depthwise_weight, depthwise_bias, slope_two, second_norm_gain, second_norm_bias, w_res, b_res, w_skip, b_skip = params
    frame_count = src_one.shape[1]
    frame_mask = (jnp.arange(frame_count, dtype=jnp.int32) < length).astype(jnp.float32)[None, :]
    element_count = length.astype(jnp.float32) * H
    wide = jnp.pad(src_two, ((0, 0), (frame_count, 0)))
    moved = lax.dynamic_slice_in_dim(wide, (frame_count - delay).astype(jnp.int32), frame_count, 1)
    mixed = frame_mask * (gain_one[:, None] * src_one + gain_two[:, None] * moved)
    pre_one = jnp.dot(w_in, mixed, precision=lax.Precision.HIGHEST) + b_in[:, None]
    first_activation = soft_prelu(pre_one, slope_one[:, None])
    first_norm_output = frame_mask * global_norm(first_activation, frame_mask, element_count, first_norm_gain, first_norm_bias)
    padded_input = jnp.pad(first_norm_output, ((0, 0), (DILATION_RATE, DILATION_RATE)))
    conv_output = depthwise_weight[:, 0:1] * padded_input[:, :frame_count] + depthwise_weight[:, 1:2] * padded_input[:, DILATION_RATE:DILATION_RATE + frame_count] + depthwise_weight[:, 2:3] * padded_input[:, 2 * DILATION_RATE:] + depthwise_bias[:, None]
    second_activation = soft_prelu(conv_output, slope_two[:, None])
    second_norm_output = global_norm(second_activation, frame_mask, element_count, second_norm_gain, second_norm_bias)
    residual_out = frame_mask * (mixed + jnp.dot(w_res, second_norm_output, precision=lax.Precision.HIGHEST) + b_res[:, None])
    skip_out = frame_mask * (jnp.dot(w_skip, second_norm_output, precision=lax.Precision.HIGHEST) + b_skip[:, None])
    return (residual_out, skip_out)

def reference(source_one, source_two, offsets, lengths, gain_one, gain_two, w_in, b_in, slope_one, first_norm_gain, first_norm_bias, depthwise_weight, depthwise_bias, slope_two, second_norm_gain, second_norm_bias, w_res, b_res, w_skip, b_skip, cot_res, cot_skip):

    def forward(src_one, src_two, params):
        return jax.vmap(lambda a, b, c, d: one_item(a, b, c, d, params))(src_one, src_two, offsets, lengths)
    params = (gain_one, gain_two, w_in, b_in, slope_one, first_norm_gain, first_norm_bias, depthwise_weight, depthwise_bias, slope_two, second_norm_gain, second_norm_bias, w_res, b_res, w_skip, b_skip)
    outputs, pullback = jax.vjp(forward, source_one, source_two, params)
    grad_one, grad_two, grads = pullback((cot_res, cot_skip))
    return (outputs[0], outputs[1], grad_one, grad_two, grads[0], grads[1], grads[2], grads[3], grads[4], grads[5], grads[6], grads[7], grads[8], grads[9], grads[10], grads[11], grads[12], grads[13], grads[14], grads[15])
```

```python
import functools

import jax
import jax.numpy as jnp
from jax import lax
from jax.experimental import pallas as pl
from jax.experimental.pallas import tpu as pltpu
from jax.sharding import PartitionSpec as P

DILATION_RATE = 16
EPS = 1e-05
LANES = 128
F32 = jnp.float32
BF16 = jnp.bfloat16
MESH = pl.DeviceIdType.MESH
CHUNK = 64

B_IN, SLOPE_ONE, GAMMA_ONE, BETA_ONE, TAP, B_DEPTH, SLOPE_TWO, GAMMA_TWO, BETA_TWO, NARROW = (
    0, 1, 2, 3, 4, 7, 8, 9, 10, 11,
)
SUM_ROWS = 16


def halves(value):
    high = value.astype(BF16)
    return high, (value - high.astype(F32)).astype(BF16)


def dot(left, right, over_left, over_right):
    return lax.dot_general(
        left, right, (((over_left,), (over_right,)), ((), ())), preferred_element_type=F32
    )


def fold_rows(value):
    return jnp.sum(value.reshape(value.shape[0] // 8, 8, value.shape[1]), axis=0)


def fold_lanes(value):
    total = value[:, :LANES]
    for start in range(LANES, value.shape[1], LANES):
        total = total + value[:, start : start + LANES]
    return total


def column(row):
    return jnp.broadcast_to(row, (LANES, LANES)).T


def wide(tile, width):
    return jnp.concatenate([tile] * (width // LANES), axis=1)


def rounded(size, step):
    return -(-size // step) * step


class Plan:
    def __init__(self, mesh, items, chans, frames, units):
        self.n_tm = mesh.shape["tm"]
        self.n_it = mesh.shape["items"]
        self.items, self.chans, self.frames, self.units = items, chans, frames, units
        whole = frames * self.n_tm
        self.tail = min(frames, rounded(whole // 32, CHUNK))
        step = 8 * self.n_tm * self.n_it
        self.seg = (
            rounded(2 * chans * units // LANES, step),
            rounded((chans + SUM_ROWS) * units // LANES, step),
        )


def kernel(plan, *refs):
    n_tm, n_it = plan.n_tm, plan.n_it
    items, chans, frames, units = plan.items, plan.chans, plan.frames, plan.units
    wing = DILATION_RATE
    blocks = units // LANES
    (
        offs, lens, s1_h, s2t_h, cr_h, cs_h,
        gain1, gain2, w_in, b_in, slope1, gamma1, beta1, taps_in, b_depth, slope2, gamma2, beta2,
        w_res, b_res, w_skip, b_skip,
        res_h, skip_h, gs1_h, gs2_h, total_h,
        s1, s2t, cr, cs, from_left, gbuf, from_right, out_res, out_skip, out_gs1, out_gs2, cat,
        moved_s, mixed_s, mcat, a1, pre1, conv, act2, d2, e2, high, low, raw, grad_a, gconv,
        gp_high, gp_low, gcat, halo_a, halo_g, stats, coef,
        w_t, wg_high, wg_low, wg, cols, x_acc, gw_acc, gb_acc, y_acc, gain_acc, sums, tap_rows,
        gall, rs_it, part, rs_tm, quarter, done,
        in_sem, out_sem, left_send, left_recv, right_send, right_recv,
        halo_send, halo_recv, stat_send, stat_recv, ar_send, ar_recv,
    ) = refs
    tm = lax.axis_index("tm")
    it = lax.axis_index("items")
    first, last = tm == 0, tm == n_tm - 1
    base = tm * frames
    whole = frames * n_tm

    def remote(src, dst, send, recv, axis, peer):
        return pltpu.make_async_remote_copy(
            src_ref=src, dst_ref=dst, send_sem=send, recv_sem=recv,
            device_id={axis: peer}, device_id_type=MESH,
        )

    def others(axis, count, mine, act):
        def turn(step, carry):
            act(lax.rem(mine + step, count))
            return carry

        lax.fori_loop(1, count, turn, 0)

    def load(kind, item):
        src, dst = ((s2t_h, s2t), (s1_h, s1), (cr_h, cr), (cs_h, cs))[kind]
        return pltpu.make_async_copy(src.at[item], dst.at[item], in_sem.at[kind, item])

    def start_loads(item, carry):
        for kind in range(4):
            load(kind, item).start()
        return carry

    lax.fori_loop(0, items, start_loads, 0)

    barrier = pltpu.get_barrier_semaphore()

    def greet(axis):
        def act(peer):
            pl.semaphore_signal(barrier, inc=1, device_id={axis: peer}, device_id_type=MESH)

        return act

    others("tm", n_tm, tm, greet("tm"))
    others("items", n_it, it, greet("items"))
    pl.semaphore_wait(barrier, n_tm + n_it - 2)

    def to_next(item):
        return remote(
            s2t_h.at[item], from_left.at[item], left_send.at[item], left_recv.at[item],
            "tm", jnp.minimum(tm + 1, n_tm - 1),
        )

    def to_previous(item):
        return remote(
            gbuf.at[item], from_right.at[item], right_send.at[item], right_recv.at[item],
            "tm", jnp.maximum(tm - 1, 0),
        )

    def start_to_next(item):
        @pl.when((item < items) & jnp.logical_not(last))
        def _():
            to_next(item).start()

    start_to_next(0)
    start_to_next(1)

    w_high, w_low = halves(w_in[...].T)
    w_t[0:chans] = w_high
    w_t[chans : 2 * chans] = w_low
    w_t[2 * chans :] = w_high
    wg[0:chans] = w_res[...] * gamma2[...]
    wg[chans:] = w_skip[...] * gamma2[...]
    high_part, low_part = halves(wg[...])
    wg_high[...] = high_part
    wg_low[...] = low_part
    tap_rows[...] = taps_in[...].T
    cols[0] = column(gain1[...])
    cols[1] = column(gain2[...])
    for side, (weight, bias) in enumerate(((w_res, b_res), (w_skip, b_skip))):
        weight_sum = jnp.sum(wg[side * chans : (side + 1) * chans], axis=1, keepdims=True)
        shift = jnp.sum(weight[...] * beta2[...], axis=1, keepdims=True)
        cols[2 + side] = jnp.broadcast_to(weight_sum, (chans, LANES))
        cols[4 + side] = jnp.broadcast_to(shift, (chans, LANES)) + column(bias[...])
    x_acc[...] = jnp.zeros_like(x_acc)
    gw_acc[...] = jnp.zeros_like(gw_acc)
    gb_acc[...] = jnp.zeros_like(gb_acc)
    y_acc[...] = jnp.zeros_like(y_acc)
    gain_acc[...] = jnp.zeros_like(gain_acc)
    sums[...] = jnp.zeros_like(sums)

    main = (frames - plan.tail) // CHUNK
    chunks = frames // CHUNK

    def by_lanes(act, init):
        return lax.fori_loop(0, blocks, lambda b, c: act(pl.multiple_of(b * LANES, LANES), c), init)

    def by_rows(act, init):
        def at(masked):
            return lambda c, carry: act(pl.multiple_of(c * CHUNK, CHUNK), masked, carry)

        carry = lax.fori_loop(0, main, at(False), init)
        return lax.fori_loop(main, chunks, at(True), carry)

    def valid_rows(row, count, length):
        index = lax.broadcasted_iota(jnp.int32, (count, LANES), 0)
        return (index + (base + row)) < length

    def lane_mask(length):
        return (lax.broadcasted_iota(jnp.int32, (8, frames), 1) + base) < length

    def add_sum(row, lanes, value):
        sums[pl.ds(row, 1), pl.ds(lanes, LANES)] += value

    def send_stats(phase, item):
        mine = stats.at[phase, item, tm]
        others("tm", n_tm, tm, lambda peer: remote(
            mine, mine, stat_send.at[phase, item], stat_recv.at[phase, item], "tm", peer).start())

    def wait_stats(phase, item, sem):
        if n_tm > 1:
            block = stats.at[phase, item, pl.ds(0, n_tm - 1)]
            pltpu.make_async_copy(block, block, sem.at[phase, item]).wait()

    def read_stats(phase, item):
        wait_stats(phase, item, stat_recv)
        total = stats[phase, item, 0]
        for peer in range(1, n_tm):
            total = total + stats[phase, item, peer]
        return jnp.sum(total, axis=1, keepdims=True)

    def halo_copies(kind, item, source, slot, halo):
        down = remote(
            source.at[slot, pl.ds(wing, wing)], halo.at[item, 1],
            halo_send.at[kind, item, 0], halo_recv.at[kind, item, 1], "tm", jnp.maximum(tm - 1, 0))
        up = remote(
            source.at[slot, pl.ds(frames, wing)], halo.at[item, 0],
            halo_send.at[kind, item, 1], halo_recv.at[kind, item, 0], "tm",
            jnp.minimum(tm + 1, n_tm - 1))
        return down, up

    def send_halo(kind, item, source, slot, halo):
        down, up = halo_copies(kind, item, source, slot, halo)
        pl.when(jnp.logical_not(first))(down.start)
        pl.when(jnp.logical_not(last))(up.start)

    def wait_halo(kind, item, source, slot, halo):
        down, up = halo_copies(kind, item, source, slot, halo)

        @pl.when(jnp.logical_not(first))
        def _():
            down.wait_send()
            up.wait_recv()

        @pl.when(jnp.logical_not(last))
        def _():
            up.wait_send()
            down.wait_recv()

    def phase_a(item):
        slot = lax.rem(item, 4)
        length = lens[item]
        load(0, item).wait()
        load(1, item).wait()
        pl.when(jnp.logical_not(first))(to_next(item).wait_recv)
        pl.when(jnp.logical_not(last))(to_next(item).wait_send)
        start_to_next(item + 2)
        cat[0:frames] = jnp.where(first, 0.0, from_left[item])
        cat[frames:] = s2t[item]
        moved = cat[pl.ds(frames - offs[item], frames), :].T
        moved_s[slot] = moved
        mixed = wide(cols[0], frames) * s1[item] + wide(cols[1], frames) * moved
        mixed = jnp.where(lane_mask(length)[0:1], mixed, 0.0)
        mixed_s[slot] = mixed
        mix_high, mix_low = halves(mixed)
        mcat[slot, 0:chans] = mix_high
        mcat[slot, chans:] = mix_low
        left = jnp.concatenate([mix_high, mix_high, mix_low], axis=0)
        pre1[slot] = dot(left, w_t[...], 0, 0)

        def lanes_step(lanes, carry):
            cut = pl.ds(lanes, LANES)
            bias, slope = b_in[:, cut], slope1[:, cut]

            def rows_step(row, masked, carry):
                rows = pl.ds(row, CHUNK)
                x = pre1[slot, rows, cut] + bias
                half = jnp.tanh(0.5 * x)
                act = jnp.maximum(x, slope * x) - (1.0 - slope) * jnp.log(
                    0.5 + 0.5 * jnp.abs(half))
                pre1[slot, rows, cut] = x
                a1[slot, pl.ds(pl.multiple_of(row + wing, 8), CHUNK), cut] = act
                if masked:
                    act = jnp.where(valid_rows(row, CHUNK, length), act, 0.0)
                return carry[0] + fold_rows(act), carry[1] + fold_rows(act * act)

            return by_rows(rows_step, carry)

        zero = jnp.zeros((8, LANES), F32)
        one, two = by_lanes(lanes_step, (zero, zero))
        stats[0, item, tm] = jnp.concatenate(
            [jnp.sum(one, axis=0, keepdims=True), jnp.sum(two, axis=0, keepdims=True),
             jnp.zeros((6, LANES), F32)], axis=0)
        send_stats(0, item)
        send_halo(0, item, a1, slot, halo_a)

    def scales(totals, length):
        count = jnp.float32(units) * length.astype(F32)
        mean = totals[0:1] / count
        inverse = lax.rsqrt(totals[1:2] / count - mean * mean + EPS)
        return mean, inverse, count

    def phase_b(item):
        slot = lax.rem(item, 4)
        pair = lax.rem(item, 2)
        length = lens[item]
        wait_halo(0, item, a1, slot, halo_a)
        mean, inverse, _ = scales(read_stats(0, item), length)
        scale = gamma1[...] * inverse
        shift = beta1[...] - scale * mean
        outside = mean - beta1[...] / scale
        taps = [tap_rows[k : k + 1] for k in range(3)]
        coef[0:1] = taps[0] * scale
        coef[1:2] = taps[1] * scale
        coef[2:3] = taps[2] * scale
        coef[3:4] = b_depth[...] + shift * (taps[0] + taps[1] + taps[2])
        a1[slot, 0:wing] = jnp.where(first, outside, halo_a[item, 0])
        after = (lax.broadcasted_iota(jnp.int32, (wing, units), 0) + (base + frames)) < length
        a1[slot, frames + wing :] = jnp.where(after, halo_a[item, 1], outside)
        for row in range(frames - plan.tail, frames, CHUNK):
            keep = wide(valid_rows(row, CHUNK, length).astype(F32), units) > 0.5
            rows = slice(row + wing, row + wing + CHUNK)
            a1[slot, rows] = jnp.where(keep, a1[slot, rows], outside)

        def lanes_step(lanes, carry):
            cut = pl.ds(lanes, LANES)
            slope = slope2[:, cut]
            w0, w1, w2, const = (coef[k : k + 1, cut] for k in range(4))

            def rows_step(row, masked, carry):
                rows = pl.ds(row, CHUNK)
                x = const + w0 * a1[slot, rows, cut]
                x += w1 * a1[slot, pl.ds(pl.multiple_of(row + wing, 8), CHUNK), cut]
                x += w2 * a1[slot, pl.ds(pl.multiple_of(row + 2 * wing, 8), CHUNK), cut]
                half = jnp.tanh(0.5 * x)
                act = jnp.maximum(x, slope * x) - (1.0 - slope) * jnp.log(
                    0.5 + 0.5 * jnp.abs(half))
                conv[pair, rows, cut] = x
                act2[pair, rows, cut] = act
                d2[pair, rows, cut] = (0.5 + 0.5 * slope) + (0.5 - 0.5 * slope) * half
                act_high, act_low = halves(act)
                high[rows, cut] = act_high
                low[rows, cut] = act_low
                if masked:
                    act = jnp.where(valid_rows(row, CHUNK, length), act, 0.0)
                return carry[0] + fold_rows(act), carry[1] + fold_rows(act * act)

            return by_rows(rows_step, carry)

        zero = jnp.zeros((8, LANES), F32)
        one, two = by_lanes(lanes_step, (zero, zero))
        load(2, item).wait()
        load(3, item).wait()
        keep = lane_mask(length)[0:1]
        in_sums = []
        for side, source in enumerate((cr, cs)):
            cot = jnp.where(keep, source[item], 0.0)
            cot_high, cot_low = halves(cot)
            gcat[pair, side * chans : (side + 1) * chans] = cot_high
            gcat[pair, (2 + side) * chans : (3 + side) * chans] = cot_low
            partial = fold_lanes(cot)
            coef_rows = pl.ds(side * chans, chans)
            gb_acc[1, coef_rows] = partial
            gb_acc[0, coef_rows] += partial
            in_sums.append(cols[2 + side] * partial)
        act_h, act_l = high[...], low[...]
        left = jnp.concatenate([wg_high[...], wg_high[...], wg_low[...]], axis=1)
        right = jnp.concatenate([act_h, act_l, act_h], axis=1)
        raw[pair] = dot(left, right, 1, 1)
        cot_high, cot_low = gcat[pair, 0 : 2 * chans], gcat[pair, 2 * chans :]
        left = jnp.concatenate([cot_high, cot_high, cot_low], axis=1)
        right = jnp.concatenate([act_h, act_l, act_h], axis=0)
        grad_a[pair] = dot(left, right, 1, 0)
        y_acc[1 + pair] = gb_acc[1]
        cross = fold_lanes(fold_rows(wg[...] * grad_a[pair]))
        stats[1, item, tm] = jnp.concatenate(
            [jnp.sum(one, axis=0, keepdims=True), jnp.sum(two, axis=0, keepdims=True),
             jnp.sum(in_sums[0] + in_sums[1], axis=0, keepdims=True),
             jnp.sum(cross, axis=0, keepdims=True), jnp.zeros((4, LANES), F32)], axis=0)
        send_stats(1, item)

    def phase_c(item):
        slot = lax.rem(item, 4)
        pair = lax.rem(item, 2)
        length = lens[item]
        left = jnp.concatenate([gcat[pair], gcat[pair, 0 : 2 * chans]], axis=0)
        right = jnp.concatenate([wg_high[...], wg_high[...], wg_low[...]], axis=0)
        e2[...] = dot(left, right, 0, 0)
        totals = read_stats(1, item)
        mean, inverse, count = scales(totals, length)
        sum_e, sum_ea = totals[2:3], totals[3:4]
        mean_e = sum_e / count
        mean_ex = inverse * (sum_ea - mean * sum_e) / count
        by_act = -inverse * inverse * mean_ex
        by_one = -inverse * mean_e - by_act * mean
        first_totals = read_only_stats(0, item)
        mean_1, inverse_1, _ = scales(first_totals, length)
        scale_1 = gamma1[...] * inverse_1
        shift_1 = beta1[...] - scale_1 * mean_1
        taps = [tap_rows[k : k + 1] for k in range(3)]
        coef[4:5] = scale_1
        coef[5:6] = shift_1
        keep = lane_mask(length)[0:1]

        @pl.when(item >= 2)
        def _():
            for copy in out_copies(item - 2):
                copy.wait()

        out = inverse * raw[pair, 0:chans] + wide(cols[4] - (inverse * mean) * cols[2], frames)
        out_res[pair] = jnp.where(keep, mixed_s[slot] + out, 0.0)
        out = inverse * raw[pair, chans:] + wide(cols[5] - (inverse * mean) * cols[3], frames)
        out_skip[pair] = jnp.where(keep, out, 0.0)
        for copy in out_copies(item):
            copy.start()
        x_acc[...] += inverse * grad_a[pair]
        y_acc[0] += (inverse * mean) * y_acc[1 + pair]

        by_act_row = jnp.broadcast_to(by_act, (8, LANES))
        by_one_row = jnp.broadcast_to(by_one, (8, LANES))
        inverse_row = jnp.broadcast_to(inverse, (8, LANES))
        edge_rows = min(frames, plan.tail + CHUNK)

        def lanes_step(lanes, carry):
            cut = pl.ds(lanes, LANES)
            inv_e, by_a, by_1 = inverse_row[0:1], by_act_row[0:1], by_one_row[0:1]

            def rows_step(row, masked, carry):
                rows = pl.ds(row, CHUNK)
                middle = pl.ds(pl.multiple_of(row + wing, 8), CHUNK)
                behind = pl.ds(pl.multiple_of(row + 2 * wing, 8), CHUNK)
                act = act2[pair, rows, cut]
                g = inv_e * e2[rows, cut] + by_a * act + by_1
                if masked:
                    g = jnp.where(valid_rows(row, CHUNK, length), g, 0.0)
                gc = g * d2[pair, rows, cut]
                gconv[pair, middle, cut] = gc
                parts = (
                    g * (conv[pair, rows, cut] - act), gc, gc * a1[slot, rows, cut],
                    gc * a1[slot, middle, cut], gc * a1[slot, behind, cut],
                )
                return tuple(c + fold_rows(p) for c, p in zip(carry, parts))

            zero = jnp.zeros((8, LANES), F32)
            found = by_rows(rows_step, (zero,) * 5)
            slope_sum, total, n0, n1, n2 = (jnp.sum(f, axis=0, keepdims=True) for f in found)

            def edge_step(c, carry):
                row = pl.multiple_of(c * CHUNK, CHUNK)
                gc = gconv[pair, pl.ds(pl.multiple_of(row + wing, 8), CHUNK), cut]
                inside = valid_rows(row + wing, CHUNK, length)
                return carry + fold_rows(jnp.where(inside, 0.0, gc))

            late = lax.fori_loop((frames - edge_rows) // CHUNK, chunks, edge_step, zero)
            late = jnp.sum(late, axis=0, keepdims=True)
            early = jnp.sum(gconv[pair, wing : 2 * wing, cut], axis=0, keepdims=True)
            early = jnp.where(first, early, 0.0)
            scale, shift = coef[4:5, cut], coef[5:6, cut]
            gains, bias = gamma1[:, cut], beta1[:, cut]
            reach = (total - early, total, total - late)
            by_beta = jnp.zeros((1, LANES), F32)
            by_gamma = jnp.zeros((1, LANES), F32)
            for k, (n_k, b_k) in enumerate(zip((n0, n1, n2), reach)):
                tap = tap_rows[k : k + 1, cut]
                n_k = scale * n_k + shift * total
                add_sum(TAP + k, lanes, n_k)
                by_beta += tap * b_k
                by_gamma += tap * (n_k - bias * b_k)
            add_sum(SLOPE_TWO, lanes, slope_sum)
            add_sum(B_DEPTH, lanes, total)
            add_sum(BETA_ONE, lanes, by_beta)
            add_sum(GAMMA_ONE, lanes, by_gamma)
            return carry[0] + gains * by_beta, carry[1] + by_gamma

        zero = jnp.zeros((1, LANES), F32)
        sum_e1, sum_ex1 = by_lanes(lanes_step, (zero, zero))
        stats[2, item, tm] = jnp.concatenate(
            [sum_e1, sum_ex1, jnp.zeros((6, LANES), F32)], axis=0)
        send_stats(2, item)
        send_halo(1, item, gconv, pair, halo_g)

    def out_copies(item):
        pair = lax.rem(item, 2)
        return (
            pltpu.make_async_copy(out_res.at[pair], res_h.at[item], out_sem.at[0, item]),
            pltpu.make_async_copy(out_skip.at[pair], skip_h.at[item], out_sem.at[1, item]),
        )

    def gs1_copy(item):
        return pltpu.make_async_copy(
            out_gs1.at[lax.rem(item, 2)], gs1_h.at[item], out_sem.at[2, item])

    def gs2_copy(item):
        return pltpu.make_async_copy(out_gs2.at[item], gs2_h.at[item], out_sem.at[3, item])

    def read_only_stats(phase, item):
        total = stats[phase, item, 0]
        for peer in range(1, n_tm):
            total = total + stats[phase, item, peer]
        return jnp.sum(total, axis=1, keepdims=True)

    def phase_d(item):
        slot = lax.rem(item, 4)
        pair = lax.rem(item, 2)
        length = lens[item]
        wait_halo(1, item, gconv, pair, halo_g)
        totals = read_stats(2, item)
        mean, inverse, count = scales(read_only_stats(0, item), length)
        mean_e, mean_ex = totals[0:1] / count, totals[1:2] / count
        by_act = -inverse * inverse * mean_ex
        by_one = -inverse * mean_e - by_act * mean
        for k in range(3):
            coef[6 + k : 7 + k] = tap_rows[k : k + 1] * gamma1[...] * inverse
        gconv[pair, 0:wing] = jnp.where(first, 0.0, halo_g[item, 0])
        gconv[pair, frames + wing :] = jnp.where(last, 0.0, halo_g[item, 1])
        by_act_row = jnp.broadcast_to(by_act, (8, LANES))
        by_one_row = jnp.broadcast_to(by_one, (8, LANES))

        def lanes_step(lanes, carry):
            cut = pl.ds(lanes, LANES)
            slope = slope1[:, cut]
            by_a, by_1 = by_act_row[0:1], by_one_row[0:1]
            u0, u1, u2 = (coef[6 + k : 7 + k, cut] for k in range(3))

            def rows_step(row, masked, carry):
                rows = pl.ds(row, CHUNK)
                middle = pl.ds(pl.multiple_of(row + wing, 8), CHUNK)
                behind = pl.ds(pl.multiple_of(row + 2 * wing, 8), CHUNK)
                act, x = a1[slot, middle, cut], pre1[slot, rows, cut]
                g = by_a * act + by_1 + u0 * gconv[pair, behind, cut]
                g += u1 * gconv[pair, middle, cut] + u2 * gconv[pair, rows, cut]
                if masked:
                    g = jnp.where(valid_rows(row, CHUNK, length), g, 0.0)
                half = jnp.tanh(0.5 * x)
                gp = g * ((0.5 + 0.5 * slope) + (0.5 - 0.5 * slope) * half)
                gp_h, gp_l = halves(gp)
                gp_high[rows, cut] = gp_h
                gp_low[rows, cut] = gp_l
                return carry[0] + fold_rows(g * (x - act)), carry[1] + fold_rows(gp)

            zero = jnp.zeros((8, LANES), F32)
            slope_sum, bias_sum = by_rows(rows_step, (zero, zero))
            add_sum(SLOPE_ONE, lanes, jnp.sum(slope_sum, axis=0, keepdims=True))
            add_sum(B_IN, lanes, jnp.sum(bias_sum, axis=0, keepdims=True))
            return carry

        by_lanes(lanes_step, 0)
        g_h, g_l = gp_high[...], gp_low[...]
        gw_acc[...] += dot(mcat[slot], g_h, 1, 0)
        gw_acc[0:chans] += dot(mcat[slot, 0:chans], g_l, 1, 0)
        both = dot(w_t[0 : 2 * chans], g_h, 1, 1)
        g_mixed = both[0:chans] + both[chans:] + dot(w_t[0:chans], g_l, 1, 1)
        g_mixed = jnp.where(lane_mask(length)[0:1], cr[item] + g_mixed, 0.0)
        pl.when(item >= 2)(gs1_copy(item - 2).wait)
        out_gs1[pair] = wide(cols[0], frames) * g_mixed
        gs1_copy(item).start()
        gain_acc[0] += fold_lanes(g_mixed * s1[item])
        gain_acc[1] += fold_lanes(g_mixed * moved_s[slot])
        gbuf[item] = (wide(cols[1], frames) * g_mixed).T
        pl.when(jnp.logical_not(first))(to_previous(item).start)

    def segment(seg):
        start = 0 if seg == 0 else plan.seg[0]
        size = plan.seg[seg]
        return start, size // n_it, size // n_it // n_tm

    def stage_copies(seg, stage):
        start, big, small = segment(seg)
        offset = start // n_it
        send, recv = ar_send.at[seg, stage], ar_recv.at[seg, stage]
        if stage == 0:
            return "items", n_it, it, lambda peer: remote(
                gall.at[pl.ds(start + peer * big, big)], rs_it.at[it, pl.ds(offset, big)],
                send, recv, "items", peer)
        if stage == 1:
            return "tm", n_tm, tm, lambda peer: remote(
                part.at[pl.ds(offset + peer * small, small)],
                rs_tm.at[tm, pl.ds(offset // n_tm, small)], send, recv, "tm", peer)
        if stage == 2:
            mine = quarter.at[pl.ds(offset + tm * small, small)]
            return "tm", n_tm, tm, lambda peer: remote(mine, mine, send, recv, "tm", peer)
        mine = done.at[pl.ds(start + it * big, big)]
        return "items", n_it, it, lambda peer: remote(mine, mine, send, recv, "items", peer)

    def stage_start(seg, stage):
        axis, count, mine, copy = stage_copies(seg, stage)
        others(axis, count, mine, lambda peer: copy(peer).start())

    def stage_wait(seg, stage, sem):
        start, big, small = segment(seg)
        count, rows = ((n_it, big), (n_tm, small), (n_tm, small), (n_it, big))[stage]
        if count > 1:
            block = gall.at[pl.ds(0, (count - 1) * rows)]
            pltpu.make_async_copy(block, block, sem.at[seg, stage]).wait()

    def added(ref, count, rows):
        total = ref[0, rows]
        for peer in range(1, count):
            total = total + ref[peer, rows]
        return total

    def stage_zero(seg):
        start, big, _ = segment(seg)
        rs_it[it, pl.ds(start // n_it, big)] = gall[pl.ds(start + it * big, big)]
        stage_start(seg, 0)

    def stage_one(seg):
        start, big, small = segment(seg)
        offset = start // n_it
        stage_wait(seg, 0, ar_recv)
        part[pl.ds(offset, big)] = added(rs_it, n_it, pl.ds(offset, big))
        rs_tm[tm, pl.ds(offset // n_tm, small)] = part[pl.ds(offset + tm * small, small)]
        stage_start(seg, 1)

    def stage_two(seg):
        start, big, small = segment(seg)
        offset = start // n_it
        stage_wait(seg, 1, ar_recv)
        quarter[pl.ds(offset + tm * small, small)] = added(
            rs_tm, n_tm, pl.ds(offset // n_tm, small))
        stage_start(seg, 2)

    def stage_three(seg):
        start, big, _ = segment(seg)
        offset = start // n_it
        stage_wait(seg, 2, ar_recv)
        done[pl.ds(start + it * big, big)] = quarter[pl.ds(offset, big)]
        stage_start(seg, 3)

    def weights_sum():
        for side, weight in enumerate((w_res, w_skip)):
            rows = slice(side * chans, (side + 1) * chans)
            ones = jnp.sum(gb_acc[0, rows], axis=1, keepdims=True)
            centred = x_acc[rows] - jnp.sum(y_acc[0, rows], axis=1, keepdims=True)
            grad = gamma2[...] * centred + beta2[...] * ones
            for b in range(blocks):
                gall[b * 2 * chans + side * chans : b * 2 * chans + (side + 1) * chans] = grad[
                    :, b * LANES : (b + 1) * LANES]
            sums[GAMMA_TWO : GAMMA_TWO + 1] += jnp.sum(
                weight[...] * centred, axis=0, keepdims=True)
            sums[BETA_TWO : BETA_TWO + 1] += jnp.sum(weight[...] * ones, axis=0, keepdims=True)
            sums[NARROW : NARROW + 1, (2 + side) * LANES : (3 + side) * LANES] = jnp.sum(
                gb_acc[0, rows].T, axis=0, keepdims=True)

    def rest_sum():
        start = plan.seg[0]
        grad = gw_acc[0:chans] + gw_acc[chans:]
        for side in range(2):
            sums[NARROW : NARROW + 1, side * LANES : (side + 1) * LANES] = jnp.sum(
                gain_acc[side].T, axis=0, keepdims=True)
        sums[SLOPE_ONE : SLOPE_ONE + 1] = sums[SLOPE_ONE : SLOPE_ONE + 1] / (1.0 - slope1[...])
        sums[SLOPE_TWO : SLOPE_TWO + 1] = sums[SLOPE_TWO : SLOPE_TWO + 1] / (1.0 - slope2[...])
        sums[GAMMA_ONE : GAMMA_ONE + 1] = sums[GAMMA_ONE : GAMMA_ONE + 1] / gamma1[...]
        for b in range(blocks):
            cut = slice(b * LANES, (b + 1) * LANES)
            gall[start + b * chans : start + (b + 1) * chans] = grad[:, cut]
            row = start + blocks * chans + b * SUM_ROWS
            gall[row : row + SUM_ROWS] = sums[:, cut]
        used = start + blocks * (chans + SUM_ROWS)
        if used < gall.shape[0]:
            gall[used:] = jnp.zeros((gall.shape[0] - used, LANES), F32)

    def step(index, carry):
        @pl.when(index < items)
        def _():
            phase_a(index)

        @pl.when((index >= 1) & (index < items + 1))
        def _():
            phase_b(index - 1)

        @pl.when((index >= 2) & (index < items + 2))
        def _():
            phase_c(index - 2)

        @pl.when(index == items + 1)
        def _():
            weights_sum()
            stage_zero(0)

        @pl.when(index == items + 2)
        def _():
            stage_one(0)

        @pl.when(index >= 3)
        def _():
            phase_d(index - 3)

        return carry

    lax.fori_loop(0, items + 3, step, 0)
    rest_sum()
    stage_zero(1)
    stage_two(0)

    def place(item, carry):
        pl.when(jnp.logical_not(last))(to_previous(item).wait_recv)
        cat[0:frames] = gbuf[item]
        cat[frames:] = jnp.where(last, 0.0, from_right[item])
        out_gs2[item] = cat[pl.ds(offs[item], frames), :].T
        gs2_copy(item).start()
        return carry

    stage_one(1)
    stage_three(0)
    lax.fori_loop(0, items - 1, place, 0)
    stage_two(1)
    lax.fori_loop(items - 1, items, place, 0)
    stage_three(1)
    stage_wait(0, 3, ar_recv)
    stage_wait(1, 3, ar_recv)
    total_copy = pltpu.make_async_copy(done, total_h, out_sem.at[0, 0])
    total_copy.start()

    def finish(item, carry):
        pl.when(jnp.logical_not(first))(to_previous(item).wait_send)
        for phase in range(3):
            wait_stats(phase, item, stat_send)
        gs2_copy(item).wait()
        return carry

    lax.fori_loop(0, items, finish, 0)
    for item in range(max(0, items - 2), items):
        for copy in out_copies(item):
            copy.wait()
        gs1_copy(item).wait()
    for seg in range(2):
        for stage in range(4):
            stage_wait(seg, stage, ar_send)
    total_copy.wait()


def per_device(
    mesh, source_one, source_two, offsets, lengths, gain_one, gain_two, w_in, b_in, slope_one,
    first_norm_gain, first_norm_bias, depthwise_weight, depthwise_bias, slope_two,
    second_norm_gain, second_norm_bias, w_res, b_res, w_skip, b_skip, cot_res, cot_skip,
):
    items, chans, frames = source_one.shape
    units = w_in.shape[0]
    plan = Plan(mesh, items, chans, frames, units)
    n_tm, n_it, wing = plan.n_tm, plan.n_it, DILATION_RATE
    s2t = jnp.swapaxes(source_two, 1, 2)

    def row(value):
        return value.reshape(1, -1)

    smem = pl.BlockSpec(memory_space=pltpu.SMEM)
    hbm = pl.BlockSpec(memory_space=pl.ANY)
    vmem = pl.BlockSpec(memory_space=pltpu.VMEM)
    rows = sum(plan.seg)

    def floats(*shape):
        return pltpu.VMEM(shape, F32)

    def shorts(*shape):
        return pltpu.VMEM(shape, BF16)

    big = jax.ShapeDtypeStruct((items, chans, frames), F32)
    sem = pltpu.SemaphoreType.DMA
    res, skip, gs1, gs2, total = pl.pallas_call(
        functools.partial(kernel, plan),
        out_shape=(big, big, big, big, jax.ShapeDtypeStruct((rows, LANES), F32)),
        in_specs=[smem] * 2 + [hbm] * 4 + [vmem] * 16,
        out_specs=[hbm] * 5,
        scratch_shapes=[
            floats(items, chans, frames), floats(items, frames, chans),
            floats(items, chans, frames), floats(items, chans, frames),
            floats(items, frames, chans), floats(items, frames, chans),
            floats(items, frames, chans),
            floats(2, chans, frames), floats(2, chans, frames), floats(2, chans, frames),
            floats(items, chans, frames), floats(2 * frames, chans),
            floats(4, chans, frames), floats(4, chans, frames), shorts(4, 2 * chans, frames),
            floats(4, frames + 2 * wing, units), floats(4, frames, units),
            floats(2, frames, units), floats(2, frames, units), floats(2, frames, units),
            floats(frames, units), shorts(frames, units), shorts(frames, units),
            floats(2, 2 * chans, frames), floats(2, 2 * chans, units),
            floats(2, frames + 2 * wing, units), shorts(frames, units), shorts(frames, units),
            shorts(2, 4 * chans, frames),
            floats(items, 2, wing, units), floats(items, 2, wing, units),
            floats(3, items, n_tm, 8, LANES), floats(16, units),
            shorts(3 * chans, units), shorts(2 * chans, units), shorts(2 * chans, units),
            floats(2 * chans, units), floats(6, chans, LANES),
            floats(2 * chans, units), floats(2 * chans, units),
            floats(2, 2 * chans, LANES), floats(3, 2 * chans, LANES), floats(2, chans, LANES),
            floats(SUM_ROWS, units), floats(3, units),
            floats(rows, LANES), floats(n_it, rows // n_it, LANES), floats(rows // n_it, LANES),
            floats(n_tm, rows // n_it // n_tm, LANES), floats(rows // n_it, LANES),
            floats(rows, LANES),
            sem((4, items)), sem((4, items)), sem((items,)), sem((items,)), sem((items,)),
            sem((items,)), sem((2, items, 2)), sem((2, items, 2)), sem((3, items)),
            sem((3, items)), sem((2, 4)), sem((2, 4)),
        ],
        compiler_params=pltpu.CompilerParams(
            collective_id=0, has_side_effects=True, vmem_limit_bytes=62 * 2**20),
        name="tcn_block",
    )(
        offsets, lengths, source_one, s2t, cot_res, cot_skip,
        row(gain_one), row(gain_two), w_in, row(b_in), row(slope_one), row(first_norm_gain),
        row(first_norm_bias), depthwise_weight, row(depthwise_bias), row(slope_two),
        row(second_norm_gain), row(second_norm_bias), w_res, row(b_res), w_skip, row(b_skip),
    )
    blocks = units // LANES
    w_pair = total[: blocks * 2 * chans].reshape(blocks, 2, chans, LANES)
    g_res, g_skip = (
        jnp.swapaxes(w_pair[:, side], 0, 1).reshape(chans, units) for side in range(2))
    start = plan.seg[0]
    g_in = jnp.swapaxes(
        total[start : start + blocks * chans].reshape(blocks, chans, LANES), 1, 2
    ).reshape(units, chans)
    start += blocks * chans
    sums = jnp.swapaxes(
        total[start : start + blocks * SUM_ROWS].reshape(blocks, SUM_ROWS, LANES), 0, 1
    ).reshape(SUM_ROWS, units)
    narrow = sums[NARROW].reshape(4, chans)
    return (
        res, skip, gs1, gs2, narrow[0], narrow[1], g_in, sums[B_IN], sums[SLOPE_ONE],
        sums[GAMMA_ONE], sums[BETA_ONE], sums[TAP : TAP + 3].T, sums[B_DEPTH], sums[SLOPE_TWO],
        sums[GAMMA_TWO], sums[BETA_TWO], g_res, narrow[2], g_skip, narrow[3],
    )


def solution(mesh):
    split = P("items", None, "tm")
    in_specs = (split, split, P("items"), P("items")) + (P(),) * 16 + (split, split)
    out_specs = (split,) * 4 + (P(),) * 16
    return jax.shard_map(
        functools.partial(per_device, mesh), mesh=mesh, in_specs=in_specs, out_specs=out_specs,
        check_vma=False,
    )
```

```python
import functools

import jax
import jax.numpy as jnp
from jax import lax
from jax.experimental import pallas as pl
from jax.experimental.pallas import tpu as pltpu
from jax.sharding import PartitionSpec as P

DILATION_RATE = 16
EPS = 1e-05
LANES = 128
F32 = jnp.float32
BF16 = jnp.bfloat16
MESH = pl.DeviceIdType.MESH
CHUNK = 64

B_IN, SLOPE_ONE, GAMMA_ONE, BETA_ONE, TAP, B_DEPTH, SLOPE_TWO, GAMMA_TWO, BETA_TWO, NARROW = (
    0, 1, 2, 3, 4, 7, 8, 9, 10, 11,
)
SUM_ROWS = 16


def halves(value):
    high = value.astype(BF16)
    return high, (value - high.astype(F32)).astype(BF16)


def dot(left, right, over_left, over_right):
    return lax.dot_general(
        left, right, (((over_left,), (over_right,)), ((), ())), preferred_element_type=F32
    )


def fold_rows(value):
    return jnp.sum(value.reshape(value.shape[0] // 8, 8, value.shape[1]), axis=0)


def fold_lanes(value):
    total = value[:, :LANES]
    for start in range(LANES, value.shape[1], LANES):
        total = total + value[:, start : start + LANES]
    return total


def column(row):
    return jnp.broadcast_to(row, (LANES, LANES)).T


def wide(tile, width):
    return jnp.concatenate([tile] * (width // LANES), axis=1)


def rounded(size, step):
    return -(-size // step) * step


class Plan:
    def __init__(self, mesh, items, chans, frames, units):
        self.n_tm = mesh.shape["tm"]
        self.n_it = mesh.shape["items"]
        self.items, self.chans, self.frames, self.units = items, chans, frames, units
        whole = frames * self.n_tm
        self.tail = min(frames, rounded(whole // 32, CHUNK))
        self.chunk = frames // 2
        step = 8 * self.n_tm * self.n_it
        self.seg = (
            rounded(2 * chans * units // LANES, step),
            rounded((chans + SUM_ROWS) * units // LANES, step),
        )


def kernel(plan, rows_sent, *refs):
    n_tm, n_it = plan.n_tm, plan.n_it
    items, chans, frames, units = plan.items, plan.chans, plan.frames, plan.units
    wing = DILATION_RATE
    blocks = units // LANES
    (
        offs, lens, pack, window, s1_h, s2t_h, packed_h, cr_h, cs_h,
        gain1, gain2, w_in, b_in, slope1, gamma1, beta1, taps_in, b_depth, slope2, gamma2, beta2,
        w_res, b_res, w_skip, b_skip,
        res_h, skip_h, gs1_h, gmoved_h, from_right_h, total_h,
        s1, s2t, cr, cs, from_left, staged, gbuf, gpack, out_res, out_skip, out_gs1, cat,
        moved_s, mixed_s, mcat, a1, pre1, conv, act2, d2, e2, high, low, raw, grad_a, gconv,
        gp_high, gp_low, gcat, halo_a, halo_g, stats, coef,
        w_t, wg_high, wg_low, wg, cols, x_acc, gw_acc, gb_acc, y_acc, gain_acc, sums, tap_rows,
        gall, rs_it, part, rs_tm, quarter, done,
        in_sem, out_sem, left_send, left_recv, right_send, right_recv,
        halo_send, halo_recv, stat_send, stat_recv, ar_send, ar_recv,
    ) = refs
    size = plan.chunk
    per_item = frames // size
    count_chunks = rows_sent // size
    tm = lax.axis_index("tm")
    it = lax.axis_index("items")
    first, last = tm == 0, tm == n_tm - 1
    base = tm * frames
    whole = frames * n_tm

    def remote(src, dst, send, recv, axis, peer):
        return pltpu.make_async_remote_copy(
            src_ref=src, dst_ref=dst, send_sem=send, recv_sem=recv,
            device_id={axis: peer}, device_id_type=MESH,
        )

    def others(axis, count, mine, act):
        def turn(step, carry):
            act(lax.rem(mine + step, count))
            return carry

        lax.fori_loop(1, count, turn, 0)

    def load(kind, item):
        src, dst = ((s2t_h, s2t), (s1_h, s1), (cr_h, cr), (cs_h, cs))[kind]
        return pltpu.make_async_copy(src.at[item], dst.at[item], in_sem.at[kind, item])

    def start_loads(item, carry):
        for kind in range(4):
            load(kind, item).start()
        return carry

    lax.fori_loop(0, items, start_loads, 0)

    barrier = pltpu.get_barrier_semaphore()

    def greet(axis):
        def act(peer):
            pl.semaphore_signal(barrier, inc=1, device_id={axis: peer}, device_id_type=MESH)

        return act

    others("tm", n_tm, tm, greet("tm"))
    others("items", n_it, it, greet("items"))
    pl.semaphore_wait(barrier, n_tm + n_it - 2)

    def to_next(chunk):
        cut = pl.ds(chunk * size, size)
        return remote(
            packed_h.at[pl.ds(frames + chunk * size, size)], from_left.at[cut], left_send.at[chunk], left_recv.at[chunk],
            "tm", jnp.minimum(tm + 1, n_tm - 1),
        )

    def to_previous(chunk):
        cut = pl.ds(chunk * size, size)
        return remote(
            gpack.at[cut], from_right_h.at[cut], right_send.at[chunk], right_recv.at[chunk],
            "tm", jnp.maximum(tm - 1, 0),
        )

    def start_to_next(chunk):
        @pl.when((chunk < count_chunks) & jnp.logical_not(last))
        def _():
            to_next(chunk).start()

    for chunk in range(min(2 * per_item, count_chunks)):
        start_to_next(chunk)

    def arrived(chunk):
        @pl.when((chunk < count_chunks) & jnp.logical_not(first))
        def _():
            to_next(chunk).wait_recv()
            staged[pl.ds(pl.multiple_of(frames + chunk * size, 8), size)] = from_left[
                pl.ds(pl.multiple_of(chunk * size, 8), size)]

    def send_back(chunk):
        @pl.when(chunk >= 0)
        def _():
            def turn(group, carry):
                for part_of in range(8):
                    block = chunk * (size // 8) + group * 8 + part_of
                    source = pack[block] * 8
                    gpack[pl.ds(pl.multiple_of(block * 8, 8), 8)] = gbuf[pl.ds(source, 8)]
                return carry

            lax.fori_loop(0, size // 64, turn, 0)
            pl.when(jnp.logical_not(first))(to_previous(chunk).start)

    w_high, w_low = halves(w_in[...].T)
    w_t[0:chans] = w_high
    w_t[chans : 2 * chans] = w_low
    w_t[2 * chans :] = w_high
    wg[0:chans] = w_res[...] * gamma2[...]
    wg[chans:] = w_skip[...] * gamma2[...]
    high_part, low_part = halves(wg[...])
    wg_high[...] = high_part
    wg_low[...] = low_part
    tap_rows[...] = taps_in[...].T
    cols[0] = column(gain1[...])
    cols[1] = column(gain2[...])
    for side, (weight, bias) in enumerate(((w_res, b_res), (w_skip, b_skip))):
        weight_sum = jnp.sum(wg[side * chans : (side + 1) * chans], axis=1, keepdims=True)
        shift = jnp.sum(weight[...] * beta2[...], axis=1, keepdims=True)
        cols[2 + side] = jnp.broadcast_to(weight_sum, (chans, LANES))
        cols[4 + side] = jnp.broadcast_to(shift, (chans, LANES)) + column(bias[...])
    x_acc[...] = jnp.zeros_like(x_acc)
    gw_acc[...] = jnp.zeros_like(gw_acc)
    gb_acc[...] = jnp.zeros_like(gb_acc)
    y_acc[...] = jnp.zeros_like(y_acc)
    gain_acc[...] = jnp.zeros_like(gain_acc)
    sums[...] = jnp.zeros_like(sums)

    main = (frames - plan.tail) // CHUNK
    chunks = frames // CHUNK

    def by_lanes(act, init):
        for b in range(blocks):
            init = act(b * LANES, init)
        return init

    def by_rows(act, init):
        def at(masked):
            return lambda c, carry: act(pl.multiple_of(c * CHUNK, CHUNK), masked, carry)

        carry = init
        for c in range(chunks):
            carry = act(c * CHUNK, c >= main, carry)
        return carry

    def valid_rows(row, count, length):
        index = lax.broadcasted_iota(jnp.int32, (count, LANES), 0)
        return (index + (base + row)) < length

    def lane_mask(length):
        return (lax.broadcasted_iota(jnp.int32, (8, frames), 1) + base) < length

    def add_sum(row, lanes, value):
        sums[pl.ds(row, 1), pl.ds(lanes, LANES)] += value

    def send_stats(phase, item):
        mine = stats.at[phase, item, tm]
        others("tm", n_tm, tm, lambda peer: remote(
            mine, mine, stat_send.at[phase, item], stat_recv.at[phase, item], "tm", peer).start())

    def wait_stats(phase, item, sem):
        if n_tm > 1:
            block = stats.at[phase, item, pl.ds(0, n_tm - 1)]
            pltpu.make_async_copy(block, block, sem.at[phase, item]).wait()

    def read_stats(phase, item, wait=True):
        if wait:
            wait_stats(phase, item, stat_recv)
        total = stats[phase, item, 0]
        for peer in range(1, n_tm):
            total = total + stats[phase, item, peer]
        return [total[:, k : k + 1] for k in range(4)]

    def put_stats(phase, item, rows):
        rows = jnp.concatenate(
            list(rows) + [jnp.zeros((8 - len(rows), LANES), F32)], axis=0)
        totals = jnp.broadcast_to(jnp.sum(rows, axis=1, keepdims=True), (8, LANES))
        shape = (8, LANES)
        own = lax.broadcasted_iota(jnp.int32, shape, 0) == lax.broadcasted_iota(
            jnp.int32, shape, 1)
        stats[phase, item, tm] = jnp.sum(jnp.where(own, totals, 0.0), axis=0, keepdims=True)
        send_stats(phase, item)

    def halo_copies(kind, item, source, slot, halo):
        down = remote(
            source.at[slot, pl.ds(wing, wing)], halo.at[item, 1],
            halo_send.at[kind, item, 0], halo_recv.at[kind, item, 1], "tm", jnp.maximum(tm - 1, 0))
        up = remote(
            source.at[slot, pl.ds(frames, wing)], halo.at[item, 0],
            halo_send.at[kind, item, 1], halo_recv.at[kind, item, 0], "tm",
            jnp.minimum(tm + 1, n_tm - 1))
        return down, up

    def send_halo(kind, item, source, slot, halo):
        down, up = halo_copies(kind, item, source, slot, halo)
        pl.when(jnp.logical_not(first))(down.start)
        pl.when(jnp.logical_not(last))(up.start)

    def wait_halo(kind, item, source, slot, halo):
        down, up = halo_copies(kind, item, source, slot, halo)

        @pl.when(jnp.logical_not(first))
        def _():
            down.wait_send()
            up.wait_recv()

        @pl.when(jnp.logical_not(last))
        def _():
            up.wait_send()
            down.wait_recv()

    def phase_a(item):
        slot = lax.rem(item, 4)
        length = lens[item]
        load(0, item).wait()
        load(1, item).wait()
        for chunk in range(per_item):
            arrived(item * per_item + chunk)
        before = staged[pl.ds(window[item] * 8, frames)]
        cat[0:frames] = jnp.where(first, 0.0, before)
        cat[frames:] = s2t[item]
        moved = cat[pl.ds(frames - offs[item], frames), :].T
        moved_s[slot] = moved
        mixed = wide(cols[0], frames) * s1[item] + wide(cols[1], frames) * moved
        mixed = jnp.where(lane_mask(length)[0:1], mixed, 0.0)
        mixed_s[slot] = mixed
        mix_high, mix_low = halves(mixed)
        mcat[slot, 0:chans] = mix_high
        mcat[slot, chans:] = mix_low
        left = jnp.concatenate([mix_high, mix_high, mix_low], axis=0)
        pre1[slot] = dot(left, w_t[...], 0, 0)

        def lanes_step(lanes, carry):
            cut = pl.ds(lanes, LANES)
            bias, slope = b_in[:, cut], slope1[:, cut]

            def rows_step(row, masked, carry):
                rows = pl.ds(row, CHUNK)
                x = pre1[slot, rows, cut] + bias
                half = jnp.tanh(0.5 * x)
                act = jnp.maximum(x, slope * x) - (1.0 - slope) * jnp.log(
                    0.5 + 0.5 * jnp.abs(half))
                pre1[slot, rows, cut] = x
                a1[slot, pl.ds(row + wing, CHUNK), cut] = act
                if masked:
                    act = jnp.where(valid_rows(row, CHUNK, length), act, 0.0)
                return carry[0] + fold_rows(act), carry[1] + fold_rows(act * act)

            return by_rows(rows_step, carry)

        zero = jnp.zeros((8, LANES), F32)
        one, two = by_lanes(lanes_step, (zero, zero))
        put_stats(
            0, item, (jnp.sum(one, axis=0, keepdims=True), jnp.sum(two, axis=0, keepdims=True)))
        send_halo(0, item, a1, slot, halo_a)

    def scales(totals, length):
        count = jnp.float32(units) * length.astype(F32)
        mean = totals[0] / count
        inverse = lax.rsqrt(totals[1] / count - mean * mean + EPS)
        return mean, inverse, count

    def phase_b(item):
        slot = lax.rem(item, 4)
        pair = lax.rem(item, 2)
        length = lens[item]
        wait_halo(0, item, a1, slot, halo_a)
        mean, inverse, _ = scales(read_stats(0, item), length)
        scale = gamma1[...] * inverse
        shift = beta1[...] - scale * mean
        outside = mean - beta1[...] / scale
        taps = [tap_rows[k : k + 1] for k in range(3)]
        coef[0:1] = taps[0] * scale
        coef[1:2] = taps[1] * scale
        coef[2:3] = taps[2] * scale
        coef[3:4] = b_depth[...] + shift * (taps[0] + taps[1] + taps[2])
        a1[slot, 0:wing] = jnp.where(first, outside, halo_a[item, 0])
        after = (lax.broadcasted_iota(jnp.int32, (wing, units), 0) + (base + frames)) < length
        a1[slot, frames + wing :] = jnp.where(after, halo_a[item, 1], outside)
        for row in range(frames - plan.tail, frames, CHUNK):
            keep = wide(valid_rows(row, CHUNK, length).astype(F32), units) > 0.5
            rows = slice(row + wing, row + wing + CHUNK)
            a1[slot, rows] = jnp.where(keep, a1[slot, rows], outside)

        def lanes_step(lanes, carry):
            cut = pl.ds(lanes, LANES)
            slope = slope2[:, cut]
            w0, w1, w2, const = (coef[k : k + 1, cut] for k in range(4))

            def rows_step(row, masked, carry):
                rows = pl.ds(row, CHUNK)
                x = const + w0 * a1[slot, rows, cut]
                x += w1 * a1[slot, pl.ds(row + wing, CHUNK), cut]
                x += w2 * a1[slot, pl.ds(row + 2 * wing, CHUNK), cut]
                half = jnp.tanh(0.5 * x)
                act = jnp.maximum(x, slope * x) - (1.0 - slope) * jnp.log(
                    0.5 + 0.5 * jnp.abs(half))
                conv[pair, rows, cut] = x
                act2[pair, rows, cut] = act
                d2[pair, rows, cut] = (0.5 + 0.5 * slope) + (0.5 - 0.5 * slope) * half
                act_high, act_low = halves(act)
                high[rows, cut] = act_high
                low[rows, cut] = act_low
                if masked:
                    act = jnp.where(valid_rows(row, CHUNK, length), act, 0.0)
                return carry[0] + fold_rows(act), carry[1] + fold_rows(act * act)

            return by_rows(rows_step, carry)

        zero = jnp.zeros((8, LANES), F32)
        one, two = by_lanes(lanes_step, (zero, zero))
        load(2, item).wait()
        load(3, item).wait()
        keep = lane_mask(length)[0:1]
        in_sums = []
        for side, source in enumerate((cr, cs)):
            cot = jnp.where(keep, source[item], 0.0)
            cot_high, cot_low = halves(cot)
            gcat[pair, side * chans : (side + 1) * chans] = cot_high
            gcat[pair, (2 + side) * chans : (3 + side) * chans] = cot_low
            partial = fold_lanes(cot)
            coef_rows = pl.ds(side * chans, chans)
            gb_acc[1, coef_rows] = partial
            gb_acc[0, coef_rows] += partial
            in_sums.append(cols[2 + side] * partial)
        act_h, act_l = high[...], low[...]
        left = jnp.concatenate([wg_high[...], wg_high[...], wg_low[...]], axis=1)
        right = jnp.concatenate([act_h, act_l, act_h], axis=1)
        raw[pair] = dot(left, right, 1, 1)
        cot_high, cot_low = gcat[pair, 0 : 2 * chans], gcat[pair, 2 * chans :]
        left = jnp.concatenate([cot_high, cot_high, cot_low], axis=1)
        right = jnp.concatenate([act_h, act_l, act_h], axis=0)
        grad_a[pair] = dot(left, right, 1, 0)
        y_acc[1 + pair] = gb_acc[1]
        cross = fold_lanes(fold_rows(wg[...] * grad_a[pair]))
        put_stats(
            1, item, (jnp.sum(one, axis=0, keepdims=True), jnp.sum(two, axis=0, keepdims=True),
                      jnp.sum(in_sums[0] + in_sums[1], axis=0, keepdims=True),
                      jnp.sum(cross, axis=0, keepdims=True)))

    def phase_c(item):
        slot = lax.rem(item, 4)
        pair = lax.rem(item, 2)
        length = lens[item]
        left = jnp.concatenate([gcat[pair], gcat[pair, 0 : 2 * chans]], axis=0)
        right = jnp.concatenate([wg_high[...], wg_high[...], wg_low[...]], axis=0)
        e2[...] = dot(left, right, 0, 0)
        totals = read_stats(1, item)
        mean, inverse, count = scales(totals, length)
        sum_e, sum_ea = totals[2], totals[3]
        mean_e = sum_e / count
        mean_ex = inverse * (sum_ea - mean * sum_e) / count
        by_act = -inverse * inverse * mean_ex
        by_one = -inverse * mean_e - by_act * mean
        first_totals = read_stats(0, item, wait=False)
        mean_1, inverse_1, _ = scales(first_totals, length)
        scale_1 = gamma1[...] * inverse_1
        shift_1 = beta1[...] - scale_1 * mean_1
        taps = [tap_rows[k : k + 1] for k in range(3)]
        coef[4:5] = scale_1
        coef[5:6] = shift_1
        keep = lane_mask(length)[0:1]

        @pl.when(item >= 2)
        def _():
            for copy in out_copies(item - 2):
                copy.wait()

        out = inverse * raw[pair, 0:chans] + wide(cols[4] - (inverse * mean) * cols[2], frames)
        out_res[pair] = jnp.where(keep, mixed_s[slot] + out, 0.0)
        out = inverse * raw[pair, chans:] + wide(cols[5] - (inverse * mean) * cols[3], frames)
        out_skip[pair] = jnp.where(keep, out, 0.0)
        for copy in out_copies(item):
            copy.start()
        x_acc[...] += inverse * grad_a[pair]
        y_acc[0] += (inverse * mean) * y_acc[1 + pair]

        by_act_row = jnp.broadcast_to(by_act, (8, LANES))
        by_one_row = jnp.broadcast_to(by_one, (8, LANES))
        inverse_row = jnp.broadcast_to(inverse, (8, LANES))
        edge_rows = min(frames, plan.tail + CHUNK)

        def lanes_step(lanes, carry):
            cut = pl.ds(lanes, LANES)
            inv_e, by_a, by_1 = inverse_row[0:1], by_act_row[0:1], by_one_row[0:1]

            def rows_step(row, masked, carry):
                rows = pl.ds(row, CHUNK)
                middle = pl.ds(row + wing, CHUNK)
                behind = pl.ds(row + 2 * wing, CHUNK)
                act = act2[pair, rows, cut]
                g = inv_e * e2[rows, cut] + by_a * act + by_1
                if masked:
                    g = jnp.where(valid_rows(row, CHUNK, length), g, 0.0)
                gc = g * d2[pair, rows, cut]
                gconv[pair, middle, cut] = gc
                parts = (
                    g * (conv[pair, rows, cut] - act), gc, gc * a1[slot, rows, cut],
                    gc * a1[slot, middle, cut], gc * a1[slot, behind, cut],
                )
                return tuple(c + fold_rows(p) for c, p in zip(carry, parts))

            zero = jnp.zeros((8, LANES), F32)
            found = by_rows(rows_step, (zero,) * 5)
            slope_sum, total, n0, n1, n2 = (jnp.sum(f, axis=0, keepdims=True) for f in found)

            def edge_step(c, carry):
                row = c * CHUNK
                gc = gconv[pair, pl.ds(row + wing, CHUNK), cut]
                inside = valid_rows(row + wing, CHUNK, length)
                return carry + fold_rows(jnp.where(inside, 0.0, gc))

            late = zero
            for c in range((frames - edge_rows) // CHUNK, chunks):
                late = edge_step(c, late)
            late = jnp.sum(late, axis=0, keepdims=True)
            early = jnp.sum(gconv[pair, wing : 2 * wing, cut], axis=0, keepdims=True)
            early = jnp.where(first, early, 0.0)
            scale, shift = coef[4:5, cut], coef[5:6, cut]
            gains, bias = gamma1[:, cut], beta1[:, cut]
            reach = (total - early, total, total - late)
            by_beta = jnp.zeros((1, LANES), F32)
            by_gamma = jnp.zeros((1, LANES), F32)
            for k, (n_k, b_k) in enumerate(zip((n0, n1, n2), reach)):
                tap = tap_rows[k : k + 1, cut]
                n_k = scale * n_k + shift * total
                add_sum(TAP + k, lanes, n_k)
                by_beta += tap * b_k
                by_gamma += tap * (n_k - bias * b_k)
            add_sum(SLOPE_TWO, lanes, slope_sum)
            add_sum(B_DEPTH, lanes, total)
            add_sum(BETA_ONE, lanes, by_beta)
            add_sum(GAMMA_ONE, lanes, by_gamma)
            return carry[0] + gains * by_beta, carry[1] + by_gamma

        zero = jnp.zeros((1, LANES), F32)
        sum_e1, sum_ex1 = by_lanes(lanes_step, (zero, zero))
        put_stats(2, item, (sum_e1, sum_ex1))
        send_halo(1, item, gconv, pair, halo_g)

    def out_copies(item):
        pair = lax.rem(item, 2)
        return (
            pltpu.make_async_copy(out_res.at[pair], res_h.at[item], out_sem.at[0, item]),
            pltpu.make_async_copy(out_skip.at[pair], skip_h.at[item], out_sem.at[1, item]),
        )

    def gs1_copy(item):
        return pltpu.make_async_copy(
            out_gs1.at[lax.rem(item, 2)], gs1_h.at[item], out_sem.at[2, item])

    def gmoved_copy(item):
        return pltpu.make_async_copy(
            gbuf.at[pl.ds(item * frames, frames)], gmoved_h.at[item], out_sem.at[3, item])

    def phase_d(item):
        slot = lax.rem(item, 4)
        pair = lax.rem(item, 2)
        length = lens[item]
        wait_halo(1, item, gconv, pair, halo_g)
        totals = read_stats(2, item)
        mean, inverse, count = scales(read_stats(0, item, wait=False), length)
        mean_e, mean_ex = totals[0] / count, totals[1] / count
        by_act = -inverse * inverse * mean_ex
        by_one = -inverse * mean_e - by_act * mean
        for k in range(3):
            coef[6 + k : 7 + k] = tap_rows[k : k + 1] * gamma1[...] * inverse
        gconv[pair, 0:wing] = jnp.where(first, 0.0, halo_g[item, 0])
        gconv[pair, frames + wing :] = jnp.where(last, 0.0, halo_g[item, 1])
        by_act_row = jnp.broadcast_to(by_act, (8, LANES))
        by_one_row = jnp.broadcast_to(by_one, (8, LANES))

        def lanes_step(lanes, carry):
            cut = pl.ds(lanes, LANES)
            slope = slope1[:, cut]
            by_a, by_1 = by_act_row[0:1], by_one_row[0:1]
            u0, u1, u2 = (coef[6 + k : 7 + k, cut] for k in range(3))

            def rows_step(row, masked, carry):
                rows = pl.ds(row, CHUNK)
                middle = pl.ds(row + wing, CHUNK)
                behind = pl.ds(row + 2 * wing, CHUNK)
                act, x = a1[slot, middle, cut], pre1[slot, rows, cut]
                g = by_a * act + by_1 + u0 * gconv[pair, behind, cut]
                g += u1 * gconv[pair, middle, cut] + u2 * gconv[pair, rows, cut]
                if masked:
                    g = jnp.where(valid_rows(row, CHUNK, length), g, 0.0)
                half = jnp.tanh(0.5 * x)
                gp = g * ((0.5 + 0.5 * slope) + (0.5 - 0.5 * slope) * half)
                gp_h, gp_l = halves(gp)
                gp_high[rows, cut] = gp_h
                gp_low[rows, cut] = gp_l
                return carry[0] + fold_rows(g * (x - act)), carry[1] + fold_rows(gp)

            zero = jnp.zeros((8, LANES), F32)
            slope_sum, bias_sum = by_rows(rows_step, (zero, zero))
            add_sum(SLOPE_ONE, lanes, jnp.sum(slope_sum, axis=0, keepdims=True))
            add_sum(B_IN, lanes, jnp.sum(bias_sum, axis=0, keepdims=True))
            return carry

        by_lanes(lanes_step, 0)
        g_h, g_l = gp_high[...], gp_low[...]
        gw_acc[...] += dot(mcat[slot], g_h, 1, 0)
        gw_acc[0:chans] += dot(mcat[slot, 0:chans], g_l, 1, 0)
        both = dot(w_t[0 : 2 * chans], g_h, 1, 1)
        g_mixed = both[0:chans] + both[chans:] + dot(w_t[0:chans], g_l, 1, 1)
        g_mixed = jnp.where(lane_mask(length)[0:1], cr[item] + g_mixed, 0.0)
        pl.when(item >= 2)(gs1_copy(item - 2).wait)
        out_gs1[pair] = wide(cols[0], frames) * g_mixed
        gs1_copy(item).start()
        gain_acc[0] += fold_lanes(g_mixed * s1[item])
        gain_acc[1] += fold_lanes(g_mixed * moved_s[slot])
        gbuf[pl.ds(pl.multiple_of(item * frames, 8), frames)] = (
            wide(cols[1], frames) * g_mixed).T
        gmoved_copy(item).start()
        for chunk in range(per_item):
            send_back(count_chunks - per_item * (items - item) + chunk)

    def segment(seg):
        start = 0 if seg == 0 else plan.seg[0]
        size = plan.seg[seg]
        return start, size // n_it, size // n_it // n_tm

    def stage_copies(seg, stage):
        start, big, small = segment(seg)
        offset = start // n_it
        send, recv = ar_send.at[seg, stage], ar_recv.at[seg, stage]
        if stage == 0:
            return "items", n_it, it, lambda peer: remote(
                gall.at[pl.ds(start + peer * big, big)], rs_it.at[it, pl.ds(offset, big)],
                send, recv, "items", peer)
        if stage == 1:
            return "tm", n_tm, tm, lambda peer: remote(
                part.at[pl.ds(offset + peer * small, small)],
                rs_tm.at[tm, pl.ds(offset // n_tm, small)], send, recv, "tm", peer)
        if stage == 2:
            mine = quarter.at[pl.ds(offset + tm * small, small)]
            return "tm", n_tm, tm, lambda peer: remote(mine, mine, send, recv, "tm", peer)
        mine = done.at[pl.ds(start + it * big, big)]
        return "items", n_it, it, lambda peer: remote(mine, mine, send, recv, "items", peer)

    def stage_start(seg, stage):
        axis, count, mine, copy = stage_copies(seg, stage)
        others(axis, count, mine, lambda peer: copy(peer).start())

    def stage_wait(seg, stage, sem):
        start, big, small = segment(seg)
        count, rows = ((n_it, big), (n_tm, small), (n_tm, small), (n_it, big))[stage]
        if count > 1:
            block = gall.at[pl.ds(0, (count - 1) * rows)]
            pltpu.make_async_copy(block, block, sem.at[seg, stage]).wait()

    def added(ref, count, rows):
        total = ref[0, rows]
        for peer in range(1, count):
            total = total + ref[peer, rows]
        return total

    def stage_zero(seg):
        start, big, _ = segment(seg)
        rs_it[it, pl.ds(start // n_it, big)] = gall[pl.ds(start + it * big, big)]
        stage_start(seg, 0)

    def stage_one(seg):
        start, big, small = segment(seg)
        offset = start // n_it
        stage_wait(seg, 0, ar_recv)
        part[pl.ds(offset, big)] = added(rs_it, n_it, pl.ds(offset, big))
        rs_tm[tm, pl.ds(offset // n_tm, small)] = part[pl.ds(offset + tm * small, small)]
        stage_start(seg, 1)

    def stage_two(seg):
        start, big, small = segment(seg)
        offset = start // n_it
        stage_wait(seg, 1, ar_recv)
        quarter[pl.ds(offset + tm * small, small)] = added(
            rs_tm, n_tm, pl.ds(offset // n_tm, small))
        stage_start(seg, 2)

    def stage_three(seg):
        start, big, _ = segment(seg)
        offset = start // n_it
        stage_wait(seg, 2, ar_recv)
        done[pl.ds(start + it * big, big)] = quarter[pl.ds(offset, big)]
        stage_start(seg, 3)

    def weights_sum():
        for side, weight in enumerate((w_res, w_skip)):
            rows = slice(side * chans, (side + 1) * chans)
            ones = jnp.sum(gb_acc[0, rows], axis=1, keepdims=True)
            centred = x_acc[rows] - jnp.sum(y_acc[0, rows], axis=1, keepdims=True)
            grad = gamma2[...] * centred + beta2[...] * ones
            for b in range(blocks):
                gall[b * 2 * chans + side * chans : b * 2 * chans + (side + 1) * chans] = grad[
                    :, b * LANES : (b + 1) * LANES]
            sums[GAMMA_TWO : GAMMA_TWO + 1] += jnp.sum(
                weight[...] * centred, axis=0, keepdims=True)
            sums[BETA_TWO : BETA_TWO + 1] += jnp.sum(weight[...] * ones, axis=0, keepdims=True)
            sums[NARROW : NARROW + 1, (2 + side) * LANES : (3 + side) * LANES] = jnp.sum(
                gb_acc[0, rows].T, axis=0, keepdims=True)

    def rest_sum():
        start = plan.seg[0]
        grad = gw_acc[0:chans] + gw_acc[chans:]
        for side in range(2):
            sums[NARROW : NARROW + 1, side * LANES : (side + 1) * LANES] = jnp.sum(
                gain_acc[side].T, axis=0, keepdims=True)
        sums[SLOPE_ONE : SLOPE_ONE + 1] = sums[SLOPE_ONE : SLOPE_ONE + 1] / (1.0 - slope1[...])
        sums[SLOPE_TWO : SLOPE_TWO + 1] = sums[SLOPE_TWO : SLOPE_TWO + 1] / (1.0 - slope2[...])
        sums[GAMMA_ONE : GAMMA_ONE + 1] = sums[GAMMA_ONE : GAMMA_ONE + 1] / gamma1[...]
        for b in range(blocks):
            cut = slice(b * LANES, (b + 1) * LANES)
            gall[start + b * chans : start + (b + 1) * chans] = grad[:, cut]
            row = start + blocks * chans + b * SUM_ROWS
            gall[row : row + SUM_ROWS] = sums[:, cut]
        used = start + blocks * (chans + SUM_ROWS)
        if used < gall.shape[0]:
            gall[used:] = jnp.zeros((gall.shape[0] - used, LANES), F32)

    def step(index, carry):
        @pl.when(index < items)
        def _():
            phase_a(index)

        start_to_next((index + 2) * per_item)

        @pl.when((index >= 1) & (index < items + 1))
        def _():
            phase_b(index - 1)

        @pl.when((index >= 2) & (index < items + 2))
        def _():
            phase_c(index - 2)

        for chunk in range(1, per_item):
            start_to_next((index + 2) * per_item + chunk)

        @pl.when(index == items + 1)
        def _():
            weights_sum()
            stage_zero(0)

        @pl.when(index == items + 2)
        def _():
            stage_one(0)

        @pl.when(index >= 3)
        def _():
            phase_d(index - 3)

        return carry

    lax.fori_loop(0, items + 3, step, 0)
    rest_sum()
    stage_zero(1)
    stage_two(0)

    stage_one(1)
    stage_three(0)
    stage_two(1)
    stage_three(1)
    stage_wait(0, 3, ar_recv)
    stage_wait(1, 3, ar_recv)
    total_copy = pltpu.make_async_copy(done, total_h, out_sem.at[0, 0])
    total_copy.start()

    def finish(item, carry):
        for phase in range(3):
            wait_stats(phase, item, stat_send)
        gmoved_copy(item).wait()
        return carry

    def finish_chunk(chunk, carry):
        @pl.when(jnp.logical_not(first))
        def _():
            to_previous(chunk).wait_send()

        @pl.when(jnp.logical_not(last))
        def _():
            to_next(chunk).wait_send()
            to_previous(chunk).wait_recv()

        return carry

    lax.fori_loop(0, items, finish, 0)
    lax.fori_loop(0, count_chunks, finish_chunk, 0)
    for item in range(max(0, items - 2), items):
        for copy in out_copies(item):
            copy.wait()
        gs1_copy(item).wait()
    for seg in range(2):
        for stage in range(4):
            stage_wait(seg, stage, ar_send)
    total_copy.wait()


def most_needed(plan, caps):
    def body(offs, out, held, send, recv):
        n_it = plan.n_it
        it = lax.axis_index("items")
        barrier = pltpu.get_barrier_semaphore()

        def peers(act):
            def turn(step, carry):
                act(lax.rem(it + step, n_it))
                return carry

            lax.fori_loop(1, n_it, turn, 0)

        def copy(peer):
            return pltpu.make_async_remote_copy(
                src_ref=held.at[it], dst_ref=held.at[it], send_sem=send, recv_sem=recv,
                device_id={"items": peer}, device_id_type=MESH)

        peers(lambda peer: pl.semaphore_signal(
            barrier, inc=1, device_id={"items": peer}, device_id_type=MESH))
        need = jnp.int32(0)
        for item in range(plan.items):
            need += (offs[item] + 7) // 8 * 8
        held[it] = jnp.full((1, LANES), need, jnp.int32)
        pl.semaphore_wait(barrier, n_it - 1)
        peers(lambda peer: copy(peer).start())
        if n_it > 1:
            block = held.at[pl.ds(0, n_it - 1)]
            pltpu.make_async_copy(block, block, recv).wait()
        most = held[0]
        for peer in range(1, n_it):
            most = jnp.maximum(most, held[peer])
        which = jnp.zeros((1, LANES), jnp.int32)
        for cap in caps[:-1]:
            which += (most > cap).astype(jnp.int32)
        out[0] = jnp.max(which)
        if n_it > 1:
            pltpu.make_async_copy(block, block, send).wait()

    return pl.pallas_call(
        body,
        out_shape=jax.ShapeDtypeStruct((1,), jnp.int32),
        in_specs=[pl.BlockSpec(memory_space=pltpu.SMEM)],
        out_specs=pl.BlockSpec(memory_space=pltpu.SMEM),
        scratch_shapes=[
            pltpu.VMEM((plan.n_it, 1, LANES), jnp.int32),
            pltpu.SemaphoreType.DMA, pltpu.SemaphoreType.DMA,
        ],
        compiler_params=pltpu.CompilerParams(collective_id=0, has_side_effects=True),
        name="most_needed",
    )


def packer(plan, caps):
    items, frames, chans = plan.items, plan.frames, plan.chans
    rows = items * frames

    def body(offs, which, s2, s2t, packed, pack, window, window_back):
        turn = pl.program_id(0)
        item = items - 1 - turn

        def rounded_up(i):
            return (offs[i] + 7) // 8 * 8

        rows_here = s2[0].T
        s2t[0] = rows_here
        end = lax.fori_loop(0, item + 1, lambda i, c: c + rounded_up(i), jnp.int32(0))
        packed[pl.ds(pl.multiple_of(end, 8), frames)] = rows_here
        window[item] = end // 8

        @pl.when(turn == 0)
        def _():
            sent = jnp.int32(caps[-1])
            for index, cap in enumerate(caps[:-1]):
                sent = jnp.where(which[0] == index, cap, sent)
            base = (sent - end) // 8

            def pad(block, carry):
                pack[block] = 0
                return carry

            lax.fori_loop(0, base, pad, 0)

            def per_item(i, base):
                window_back[i] = base
                blocks = rounded_up(i) // 8

                def fill(block, carry):
                    pack[base + block] = i * (frames // 8) + block
                    return carry

                lax.fori_loop(0, blocks, fill, 0)
                return base + blocks

            lax.fori_loop(0, items, per_item, base)

    smem = pl.BlockSpec(memory_space=pltpu.SMEM)
    return pl.pallas_call(
        body,
        grid=(items,),
        out_shape=(
            jax.ShapeDtypeStruct((items, frames, chans), F32),
            jax.ShapeDtypeStruct((rows + frames, chans), F32),
            jax.ShapeDtypeStruct((rows // 8,), jnp.int32),
            jax.ShapeDtypeStruct((items,), jnp.int32),
            jax.ShapeDtypeStruct((items,), jnp.int32),
        ),
        in_specs=[
            smem, smem, pl.BlockSpec((1, chans, frames), lambda turn: (items - 1 - turn, 0, 0))],
        out_specs=(
            pl.BlockSpec((1, frames, chans), lambda turn: (items - 1 - turn, 0, 0)),
            pl.BlockSpec((rows + frames, chans), lambda turn: (0, 0)),
            smem, smem, smem,
        ),
        compiler_params=pltpu.CompilerParams(vmem_limit_bytes=32 * 2**20),
        name="packer",
    )


def finisher(plan, rows):
    items, frames, chans, units = plan.items, plan.frames, plan.chans, plan.units
    blocks = units // LANES

    def body(offs, window, gmoved_h, from_right_h, total_h, res_h, skip_h, gs1_h, *rest):
        outs, scratch = rest[:20], rest[20:]
        cat, gs2, total, passed, in_sem, out_sem, pass_sem, total_sem = scratch
        out_res, out_skip, out_gs1, out_gs2 = outs[:4]
        last = lax.axis_index("tm") == plan.n_tm - 1
        def through(kind, item):
            src, dst = ((res_h, out_res), (skip_h, out_skip), (gs1_h, out_gs1))[kind]
            held = passed.at[kind, item]
            return (
                pltpu.make_async_copy(src.at[item], held, pass_sem.at[0, kind, item]),
                pltpu.make_async_copy(held, dst.at[item], pass_sem.at[1, kind, item]),
            )

        def loads(item):
            start = pl.multiple_of(window[item] * 8, 8)
            return (
                pltpu.make_async_copy(
                    gmoved_h.at[item], cat.at[item, pl.ds(0, frames)], in_sem.at[0, item]),
                pltpu.make_async_copy(
                    from_right_h.at[pl.ds(start, frames)], cat.at[item, pl.ds(frames, frames)],
                    in_sem.at[1, item]),
            )

        def store(item):
            return pltpu.make_async_copy(gs2.at[item], out_gs2.at[item], out_sem.at[item])

        def start(item, carry):
            for copy in loads(item):
                copy.start()
            for kind in range(3):
                through(kind, item)[0].start()
            return carry

        total_copy = pltpu.make_async_copy(total_h, total, total_sem)
        total_copy.start()
        lax.fori_loop(0, items, start, 0)

        def turn(item, carry):
            for copy in loads(item):
                copy.wait()
            for kind in range(3):
                arriving, leaving = through(kind, item)
                arriving.wait()
                leaving.start()

            @pl.when(last)
            def _():
                cat[item, frames:] = jnp.zeros((frames, chans), F32)

            gs2[item] = cat[item, pl.ds(offs[item], frames), :].T
            store(item).start()
            return carry

        lax.fori_loop(0, items, turn, 0)
        total_copy.wait()
        (
            gain_1, gain_2, g_in, gb_in, g_slope1, g_gamma1, g_beta1, g_taps, gb_depth, g_slope2,
            g_gamma2, g_beta2, g_res, gb_res, g_skip, gb_skip,
        ) = outs[4:]
        start_in = plan.seg[0]
        start_sums = start_in + blocks * chans
        for b in range(blocks):
            cut = slice(b * LANES, (b + 1) * LANES)
            g_res[:, cut] = total[2 * b * chans : (2 * b + 1) * chans]
            g_skip[:, cut] = total[(2 * b + 1) * chans : (2 * b + 2) * chans]
            g_in[cut] = total[start_in + b * chans : start_in + (b + 1) * chans].T
            sums = total[start_sums + b * SUM_ROWS : start_sums + (b + 1) * SUM_ROWS]
            for out, row in (
                (gb_in, B_IN), (g_slope1, SLOPE_ONE), (g_gamma1, GAMMA_ONE), (g_beta1, BETA_ONE),
                (gb_depth, B_DEPTH), (g_slope2, SLOPE_TWO), (g_gamma2, GAMMA_TWO),
                (g_beta2, BETA_TWO),
            ):
                out[:, cut] = sums[row : row + 1]
            g_taps[cut] = sums.T[:, TAP : TAP + 3]
            (gain_1, gain_2, gb_res, gb_skip)[b][...] = sums[NARROW : NARROW + 1]

        def end(item, carry):
            store(item).wait()
            for kind in range(3):
                through(kind, item)[1].wait()
            return carry

        lax.fori_loop(0, items, end, 0)

    smem = pl.BlockSpec(memory_space=pltpu.SMEM)
    hbm = pl.BlockSpec(memory_space=pl.ANY)
    vmem = pl.BlockSpec(memory_space=pltpu.VMEM)
    big = jax.ShapeDtypeStruct((items, chans, frames), F32)

    def array(*shape):
        return jax.ShapeDtypeStruct(shape, F32)

    narrow, per_unit = array(1, chans), array(1, units)
    sem = pltpu.SemaphoreType.DMA
    return pl.pallas_call(
        body,
        out_shape=(big,) * 4 + (
            narrow, narrow, array(units, chans), per_unit, per_unit, per_unit, per_unit,
            array(units, 3), per_unit, per_unit, per_unit, per_unit, array(chans, units), narrow,
            array(chans, units), narrow,
        ),
        in_specs=[smem, smem] + [hbm] * 6,
        out_specs=(hbm,) * 4 + (vmem,) * 16,
        scratch_shapes=[
            pltpu.VMEM((items, 2 * frames, chans), F32), pltpu.VMEM((items, chans, frames), F32),
            pltpu.VMEM((rows, LANES), F32), pltpu.VMEM((3, items, chans, frames), F32),
            sem((2, items)), sem((items,)), sem((2, 3, items)), sem,
        ],
        compiler_params=pltpu.CompilerParams(vmem_limit_bytes=32 * 2**20),
        name="finisher",
    )


def per_device(
    mesh, source_one, source_two, offsets, lengths, gain_one, gain_two, w_in, b_in, slope_one,
    first_norm_gain, first_norm_bias, depthwise_weight, depthwise_bias, slope_two,
    second_norm_gain, second_norm_bias, w_res, b_res, w_skip, b_skip, cot_res, cot_skip,
):
    items, chans, frames = source_one.shape
    units = w_in.shape[0]
    plan = Plan(mesh, items, chans, frames, units)
    n_tm, n_it, wing = plan.n_tm, plan.n_it, DILATION_RATE
    full = items * frames
    caps = tuple(full * part // 16 for part in (9, 10, 11, 12, 16))
    which = most_needed(plan, caps)(offsets)
    s2t, packed, pack, window, window_back = packer(plan, caps)(offsets, which, source_two)

    def row(value):
        return value.reshape(1, -1)

    smem = pl.BlockSpec(memory_space=pltpu.SMEM)
    hbm = pl.BlockSpec(memory_space=pl.ANY)
    vmem = pl.BlockSpec(memory_space=pltpu.VMEM)
    rows = sum(plan.seg)

    def floats(*shape):
        return pltpu.VMEM(shape, F32)

    def shorts(*shape):
        return pltpu.VMEM(shape, BF16)

    big = jax.ShapeDtypeStruct((items, chans, frames), F32)
    sem = pltpu.SemaphoreType.DMA
    def block(sent, index):
        chunks = sent // plan.chunk
        return pl.pallas_call(
            functools.partial(kernel, plan, sent),
            out_shape=(
                big, big, big, jax.ShapeDtypeStruct((items, frames, chans), F32),
                jax.ShapeDtypeStruct((full + frames, chans), F32),
                jax.ShapeDtypeStruct((rows, LANES), F32),
            ),
            in_specs=[smem] * 4 + [hbm] * 5 + [vmem] * 16,
            out_specs=[hbm] * 6,
            scratch_shapes=[
                floats(items, chans, frames), floats(items, frames, chans),
                floats(items, chans, frames), floats(items, chans, frames),
                floats(sent, chans), floats(frames + sent, chans), floats(full, chans),
                floats(sent, chans),
                floats(2, chans, frames), floats(2, chans, frames), floats(2, chans, frames),
                floats(2 * frames, chans),
                floats(4, chans, frames), floats(4, chans, frames), shorts(4, 2 * chans, frames),
                floats(4, frames + 2 * wing, units), floats(4, frames, units),
                floats(2, frames, units), floats(2, frames, units), floats(2, frames, units),
                floats(frames, units), shorts(frames, units), shorts(frames, units),
                floats(2, 2 * chans, frames), floats(2, 2 * chans, units),
                floats(2, frames + 2 * wing, units), shorts(frames, units), shorts(frames, units),
                shorts(2, 4 * chans, frames),
                floats(items, 2, wing, units), floats(items, 2, wing, units),
                floats(3, items, n_tm, 1, LANES), floats(16, units),
                shorts(3 * chans, units), shorts(2 * chans, units), shorts(2 * chans, units),
                floats(2 * chans, units), floats(6, chans, LANES),
                floats(2 * chans, units), floats(2 * chans, units),
                floats(2, 2 * chans, LANES), floats(3, 2 * chans, LANES), floats(2, chans, LANES),
                floats(SUM_ROWS, units), floats(3, units),
                floats(rows, LANES), floats(n_it, rows // n_it, LANES), floats(rows // n_it, LANES),
                floats(n_tm, rows // n_it // n_tm, LANES), floats(rows // n_it, LANES),
                floats(rows, LANES),
                sem((4, items)), sem((4, items)), sem((chunks,)), sem((chunks,)), sem((chunks,)),
                sem((chunks,)), sem((2, items, 2)), sem((2, items, 2)), sem((3, items)),
                sem((3, items)), sem((2, 4)), sem((2, 4)),
            ],
            compiler_params=pltpu.CompilerParams(
                collective_id=1 + index, has_side_effects=True,
                vmem_limit_bytes=62 * 2**20),
            name="tcn_block",
        )

    branches = [block(sent, index) for index, sent in enumerate(caps)]
    res, skip, gs1, gmoved, from_right, total = lax.switch(
        which[0], branches,
        offsets, lengths, pack, window, source_one, s2t, packed, cot_res, cot_skip,
        row(gain_one), row(gain_two), w_in, row(b_in), row(slope_one), row(first_norm_gain),
        row(first_norm_bias), depthwise_weight, row(depthwise_bias), row(slope_two),
        row(second_norm_gain), row(second_norm_bias), w_res, row(b_res), w_skip, row(b_skip),
    )
    outs = finisher(plan, rows)(
        offsets, window_back, gmoved, from_right, total, res, skip, gs1)
    return tuple(out.reshape(-1) if out.shape[0] == 1 else out for out in outs)


def solution(mesh):
    split = P("items", None, "tm")
    in_specs = (split, split, P("items"), P("items")) + (P(),) * 16 + (split, split)
    out_specs = (split,) * 4 + (P(),) * 16
    return jax.shard_map(
        functools.partial(per_device, mesh), mesh=mesh, in_specs=in_specs, out_specs=out_specs,
        check_vma=False,
    )
```

```python
import functools

import jax
import jax.numpy as jnp
from jax import lax
from jax.experimental import pallas as pl
from jax.experimental.pallas import tpu as pltpu
from jax.sharding import PartitionSpec as P

DILATION_RATE = 16
EPS = 1e-05
LANES = 128
F32 = jnp.float32
BF16 = jnp.bfloat16
MESH = pl.DeviceIdType.MESH
CHUNK = 64
GROUP = 16

B_IN, SLOPE_ONE, GAMMA_ONE, BETA_ONE, TAP, B_DEPTH, SLOPE_TWO, GAMMA_TWO, BETA_TWO, NARROW = (
    0, 1, 2, 3, 4, 7, 8, 9, 10, 11,
)
SUM_ROWS = 16


def halves(value):
    high = value.astype(BF16)
    return high, (value - high.astype(F32)).astype(BF16)


def dot(left, right, over_left, over_right):
    return lax.dot_general(
        left, right, (((over_left,), (over_right,)), ((), ())), preferred_element_type=F32
    )


def fold_rows(value):
    return jnp.sum(value.reshape(value.shape[0] // 8, 8, value.shape[1]), axis=0)


def fold_lanes(value):
    total = value[:, :LANES]
    for start in range(LANES, value.shape[1], LANES):
        total = total + value[:, start : start + LANES]
    return total


def column(row):
    return jnp.broadcast_to(row, (LANES, LANES)).T


def wide(tile, width):
    return jnp.concatenate([tile] * (width // LANES), axis=1)


def rounded(size, step):
    return -(-size // step) * step


class Plan:
    def __init__(self, mesh, items, chans, frames, units):
        self.n_tm = mesh.shape["tm"]
        self.n_it = mesh.shape["items"]
        self.items, self.chans, self.frames, self.units = items, chans, frames, units
        whole = frames * self.n_tm
        self.tail = min(frames, rounded(whole // 32, CHUNK))
        step = 8 * self.n_tm * self.n_it
        self.seg = step
        self.weight_segs = -(-(2 * chans * units // LANES) // step)
        self.segs = self.weight_segs + -(-(chans * units // LANES) // step)
        self.small = rounded(SUM_ROWS * units // LANES, 8 * self.n_tm)
        full = items * frames
        self.parts = 32
        self.caps = tuple(sorted({
            rounded(full * part // 16, GROUP * self.parts) for part in (9, 10, 11, 12, 16)}))
        if items == 8 and self.caps[0] >= 4 * frames:
            self.arrive = (4, 8, 12, 16, 24, 32, 32, 32)
            self.out = (8, ((2, 2), (3, 2), (3, 3), (3, 2), (4, 0)))
            self.back = {6: (2, 2), 7: (3, 3), 8: (3, 3), 9: (3, 3), 10: (5, 0), 11: (5, 0)}
        else:
            self.arrive = (self.parts,) * items
            self.out = (self.parts, ())
            self.back = {items + 3: (self.parts, 0)}


def kernel(plan, rows_sent, *refs):
    n_tm, n_it = plan.n_tm, plan.n_it
    items, chans, frames, units = plan.items, plan.chans, plan.frames, plan.units
    wing = DILATION_RATE
    blocks = units // LANES
    (
        order, offs, lens, window, pack, s1_h, s2t_h, packed_h, cr_h, cs_h,
        gain1, gain2, w_in, b_in, slope1, gamma1, beta1, tap_rows, b_depth, slope2, gamma2, beta2,
        w_res, b_res, w_skip, b_skip,
        res_h, skip_h, gs1_h, gmoved_h, from_right_h, total_h, small_h,
        s1, s2t, cr, cs, from_left, staged, gbuf, gpack, out_res, out_skip, out_gs1, cat,
        moved_s, mixed_s, mcat, pre_raw, a1, pre1, conv, act2, d2, e2, high, low, raw, grad_a,
        gconv, gp_high, gp_low, gcat, halo_a, halo_g, stats, act_sums, coef,
        w_t, wg_high, wg_low, wg, cols, x_acc, gw_acc, gb_acc, y_acc, gain_acc, sums,
        gall, rs_it, part, rs_tm, quarter, done, small, small_it, small_tm, small_done,
        in_sem, out_sem, left_send, left_recv, right_send, right_recv,
        halo_send, halo_recv, stat_send, stat_recv, ar_send, ar_recv,
    ) = refs
    size = rows_sent // plan.parts
    tm = lax.axis_index("tm")
    it = lax.axis_index("items")
    first, last = tm == 0, tm == n_tm - 1
    base = tm * frames
    whole = frames * n_tm

    def remote(src, dst, send, recv, axis, peer):
        return pltpu.make_async_remote_copy(
            src_ref=src, dst_ref=dst, send_sem=send, recv_sem=recv,
            device_id={axis: peer}, device_id_type=MESH,
        )

    def others(axis, count, mine, act):
        def turn(step, carry):
            act(lax.rem(mine + step, count))
            return carry

        lax.fori_loop(1, count, turn, 0)

    def load(kind):
        src, dst = ((s2t_h, s2t), (s1_h, s1), (cr_h, cr), (cs_h, cs))[kind]
        return pltpu.make_async_copy(src, dst, in_sem.at[kind])

    for kind in range(4):
        load(kind).start()

    barrier = pltpu.get_barrier_semaphore()

    def greet(axis):
        def act(peer):
            pl.semaphore_signal(barrier, inc=1, device_id={axis: peer}, device_id_type=MESH)

        return act

    others("tm", n_tm, tm, greet("tm"))
    others("items", n_it, it, greet("items"))
    pl.semaphore_wait(barrier, n_tm + n_it - 2)

    def to_next(chunk):
        cut = pl.ds(chunk * size, size)
        return remote(
            packed_h.at[cut], from_left.at[cut], left_send.at[chunk], left_recv.at[chunk],
            "tm", jnp.minimum(tm + 1, n_tm - 1),
        )

    def to_previous(chunk):
        cut = pl.ds(chunk * size, size)
        return remote(
            gpack.at[cut], from_right_h.at[cut], right_send.at[chunk], right_recv.at[chunk],
            "tm", jnp.maximum(tm - 1, 0),
        )

    def start_to_next(chunk):
        @pl.when((chunk < plan.parts) & jnp.logical_not(last))
        def _():
            to_next(chunk).start()

    for chunk in range(plan.out[0]):
        start_to_next(chunk)

    def arrived(place):
        def take(chunk, carry):
            @pl.when(jnp.logical_not(first))
            def _():
                to_next(chunk).wait_recv()
                staged[pl.ds(pl.multiple_of(frames + chunk * size, 8), size)] = from_left[
                    pl.ds(pl.multiple_of(chunk * size, 8), size)]

            return carry

        for k in range(items):
            low_end, high_end = (plan.arrive[k - 1] if k else 0), plan.arrive[k]
            if high_end > low_end:
                @pl.when(place == k)
                def _():
                    lax.fori_loop(low_end, high_end, take, 0)

    def send_back(low_end, high_end):
        def put(chunk, carry):
            def turn(block, carry):
                block = chunk * (size // GROUP) + block
                source = pack[block // LANES, block % LANES] * GROUP
                gpack[pl.ds(pl.multiple_of(block * GROUP, GROUP), GROUP)] = gbuf[
                    pl.ds(source, GROUP)]
                return carry

            lax.fori_loop(0, size // GROUP, turn, 0, unroll=True)
            pl.when(jnp.logical_not(first))(to_previous(chunk).start)
            return carry

        lax.fori_loop(low_end, high_end, put, 0)

    def bulk(index, point):
        sent = plan.out[0]
        for k, counts in enumerate(plan.out[1]):
            start, end = sent + point * counts[0], sent + counts[0] + point * counts[1]
            sent += sum(counts)
            if end > start:
                @pl.when(index == k)
                def _():
                    for chunk in range(start, end):
                        start_to_next(chunk)

        returned = 0
        for k, counts in plan.back.items():
            start = returned + point * counts[0]
            end = returned + counts[0] + point * counts[1]
            returned += sum(counts)
            if end > start:
                pl.when(index == k)(functools.partial(send_back, start, end))

    w_high, w_low = halves(w_in[...].T)
    w_t[0:chans] = w_high
    w_t[chans : 2 * chans] = w_low
    w_t[2 * chans :] = w_high
    wg[0:chans] = w_res[...] * gamma2[...]
    wg[chans:] = w_skip[...] * gamma2[...]
    high_part, low_part = halves(wg[...])
    wg_high[...] = high_part
    wg_low[...] = low_part
    cols[0] = column(gain1[...])
    cols[1] = column(gain2[...])
    for side, (weight, bias) in enumerate(((w_res, b_res), (w_skip, b_skip))):
        weight_sum = jnp.sum(wg[side * chans : (side + 1) * chans], axis=1, keepdims=True)
        shift = jnp.sum(weight[...] * beta2[...], axis=1, keepdims=True)
        cols[2 + side] = jnp.broadcast_to(weight_sum, (chans, LANES))
        cols[4 + side] = jnp.broadcast_to(shift, (chans, LANES)) + column(bias[...])
    x_acc[...] = jnp.zeros_like(x_acc)
    gw_acc[...] = jnp.zeros_like(gw_acc)
    gb_acc[...] = jnp.zeros_like(gb_acc)
    y_acc[...] = jnp.zeros_like(y_acc)
    gain_acc[...] = jnp.zeros_like(gain_acc)
    sums[...] = jnp.zeros_like(sums)

    main = (frames - plan.tail) // CHUNK
    chunks = frames // CHUNK

    def by_lanes(act, init, merged):
        if merged:
            for b in range(blocks):
                init = act(b * LANES, init)
            return init
        return lax.fori_loop(0, blocks, lambda b, c: act(pl.multiple_of(b * LANES, LANES), c), init)

    def side_by_side(index, together, parts):
        low_end, high_end = together
        all_due = (index >= low_end) & (index <= high_end)

        @pl.when(all_due)
        def _():
            for _, _, act in parts:
                act(True)

        for first_turn, last_turn, act in parts:
            due = (index >= first_turn) & (index <= last_turn) & jnp.logical_not(all_due)
            pl.when(due)(functools.partial(act, False))

    def by_rows(act, init):
        def at(masked):
            return lambda c, carry: act(pl.multiple_of(c * CHUNK, CHUNK), masked, carry)

        carry = init
        for c in range(chunks):
            carry = act(c * CHUNK, c >= main, carry)
        return carry

    def valid_rows(row, count, length):
        index = lax.broadcasted_iota(jnp.int32, (count, LANES), 0)
        return (index + (base + row)) < length

    def lane_mask(length):
        return (lax.broadcasted_iota(jnp.int32, (8, frames), 1) + base) < length

    def add_sum(row, lanes, value):
        sums[pl.ds(row, 1), pl.ds(lanes, LANES)] += value

    def send_stats(phase, item):
        mine = stats.at[phase, item, tm]
        others("tm", n_tm, tm, lambda peer: remote(
            mine, mine, stat_send.at[phase, item], stat_recv.at[phase, item], "tm", peer).start())

    def wait_stats(phase, item, sem):
        if n_tm > 1:
            block = stats.at[phase, item, pl.ds(0, n_tm - 1)]
            pltpu.make_async_copy(block, block, sem.at[phase, item]).wait()

    def read_stats(phase, item):
        total = stats[phase, item, 0]
        for peer in range(1, n_tm):
            total = total + stats[phase, item, peer]
        total = jnp.sum(total, axis=1, keepdims=True)
        return [total[k : k + 1] for k in range(4)]

    def put_stats(phase, item, rows):
        for k, row in enumerate(rows):
            stats[phase, item, tm, k : k + 1] = row
        for k in range(len(rows), 4):
            stats[phase, item, tm, k : k + 1] = jnp.zeros((1, LANES), F32)

    def halo_copies(kind, item, source, slot, halo):
        down = remote(
            source.at[slot, pl.ds(wing, wing)], halo.at[item, 1],
            halo_send.at[kind, item, 0], halo_recv.at[kind, item, 1], "tm", jnp.maximum(tm - 1, 0))
        up = remote(
            source.at[slot, pl.ds(frames, wing)], halo.at[item, 0],
            halo_send.at[kind, item, 1], halo_recv.at[kind, item, 0], "tm",
            jnp.minimum(tm + 1, n_tm - 1))
        return down, up

    def send_halo(kind, item, source, slot, halo):
        down, up = halo_copies(kind, item, source, slot, halo)
        pl.when(jnp.logical_not(first))(down.start)
        pl.when(jnp.logical_not(last))(up.start)

    def wait_halo(kind, item, source, slot, halo):
        down, up = halo_copies(kind, item, source, slot, halo)

        @pl.when(jnp.logical_not(first))
        def _():
            down.wait_send()
            up.wait_recv()

        @pl.when(jnp.logical_not(last))
        def _():
            up.wait_send()
            down.wait_recv()

    def mix(place):
        slot = lax.rem(place, 5)
        item = order[place]
        before = staged[pl.ds(window[place] * GROUP, frames)]
        cat[0:frames] = jnp.where(first, 0.0, before)
        cat[frames:] = s2t[place]
        moved = cat[pl.ds(frames - offs[place], frames), :].T
        moved_s[slot] = moved
        mixed = wide(cols[0], frames) * s1[item] + wide(cols[1], frames) * moved
        mixed = jnp.where(lane_mask(lens[place])[0:1], mixed, 0.0)
        mixed_s[slot] = mixed
        mix_high, mix_low = halves(mixed)
        mcat[slot, 0:chans] = mix_high
        mcat[slot, chans:] = mix_low

    def mix_product(place):
        slot = lax.rem(place, 5)
        left = jnp.concatenate([mcat[slot, 0:chans], mcat[slot]], axis=0)
        pre_raw[...] = dot(left, w_t[...], 0, 0)

    def phase_a(place, merged):
        slot = lax.rem(place, 4)
        length = lens[place]

        def lanes_step(lanes, carry):
            cut = pl.ds(lanes, LANES)
            bias, slope = b_in[:, cut], slope1[:, cut]

            def rows_step(row, masked, carry):
                rows = pl.ds(row, CHUNK)
                x = pre_raw[rows, cut] + bias
                half = jnp.tanh(0.5 * x)
                act = jnp.maximum(x, slope * x) - (1.0 - slope) * jnp.log(
                    0.5 + 0.5 * jnp.abs(half))
                pre1[slot, rows, cut] = x
                a1[slot, pl.ds(row + wing, CHUNK), cut] = act
                if masked:
                    act = jnp.where(valid_rows(row, CHUNK, length), act, 0.0)
                return carry[0] + fold_rows(act), carry[1] + fold_rows(act * act)

            return by_rows(rows_step, carry)

        zero = jnp.zeros((8, LANES), F32)
        carry = by_lanes(lanes_step, (zero, zero), merged)
        put_stats(0, place, [jnp.sum(c, axis=0, keepdims=True) for c in carry])

    def scales(totals, length):
        count = jnp.float32(units) * length.astype(F32)
        mean = totals[0] / count
        inverse = lax.rsqrt(totals[1] / count - mean * mean + EPS)
        return mean, inverse, count

    def before_b(place):
        slot = lax.rem(place, 4)
        length = lens[place]
        mean, inverse, _ = scales(read_stats(0, place), length)
        scale = gamma1[...] * inverse
        shift = beta1[...] - scale * mean
        outside = mean - beta1[...] / scale
        taps = [tap_rows[k : k + 1] for k in range(3)]
        coef[0:1] = taps[0] * scale
        coef[1:2] = taps[1] * scale
        coef[2:3] = taps[2] * scale
        coef[3:4] = b_depth[...] + shift * (taps[0] + taps[1] + taps[2])
        a1[slot, 0:wing] = jnp.where(first, outside, halo_a[place, 0])
        after = (lax.broadcasted_iota(jnp.int32, (wing, units), 0) + (base + frames)) < length
        a1[slot, frames + wing :] = jnp.where(after, halo_a[place, 1], outside)


        @pl.when(last)
        def _():
            for row in range(frames - plan.tail, frames, CHUNK):
                keep = wide(valid_rows(row, CHUNK, length).astype(F32), units) > 0.5
                rows = slice(row + wing, row + wing + CHUNK)
                a1[slot, rows] = jnp.where(keep, a1[slot, rows], outside)

    def phase_b(place, merged):
        slot = lax.rem(place, 4)
        pair = lax.rem(place, 2)
        length = lens[place]

        def lanes_step(lanes, carry):
            cut = pl.ds(lanes, LANES)
            slope = slope2[:, cut]
            w0, w1, w2, const = (coef[k : k + 1, cut] for k in range(4))

            def rows_step(row, masked, carry):
                rows = pl.ds(row, CHUNK)
                x = const + w0 * a1[slot, rows, cut]
                x += w1 * a1[slot, pl.ds(row + wing, CHUNK), cut]
                x += w2 * a1[slot, pl.ds(row + 2 * wing, CHUNK), cut]
                half = jnp.tanh(0.5 * x)
                act = jnp.maximum(x, slope * x) - (1.0 - slope) * jnp.log(
                    0.5 + 0.5 * jnp.abs(half))
                conv[pair, rows, cut] = x
                act2[pair, rows, cut] = act
                d2[pair, rows, cut] = (0.5 + 0.5 * slope) + (0.5 - 0.5 * slope) * half
                act_high, act_low = halves(act)
                high[rows, cut] = act_high
                low[rows, cut] = act_low
                if masked:
                    act = jnp.where(valid_rows(row, CHUNK, length), act, 0.0)
                return carry[0] + fold_rows(act), carry[1] + fold_rows(act * act)

            return by_rows(rows_step, carry)

        zero = jnp.zeros((8, LANES), F32)
        carry = by_lanes(lanes_step, (zero, zero), merged)
        act_sums[0:1] = jnp.sum(carry[0], axis=0, keepdims=True)
        act_sums[1:2] = jnp.sum(carry[1], axis=0, keepdims=True)

    def cotangents(place):
        item = order[place]
        pair = lax.rem(place, 2)
        keep = lane_mask(lens[place])[0:1]
        in_sum = None
        for side, source in enumerate((cr, cs)):
            cot = jnp.where(keep, source[item], 0.0)
            cot_high, cot_low = halves(cot)
            gcat[side * chans : (side + 1) * chans] = cot_high
            gcat[(2 + side) * chans : (3 + side) * chans] = cot_low
            partial = fold_lanes(cot)
            rows = pl.ds(side * chans, chans)
            y_acc[1 + pair, rows] = partial
            gb_acc[rows] += partial
            by_weight = cols[2 + side] * partial
            in_sum = by_weight if in_sum is None else in_sum + by_weight
        act_sums[2:3] = jnp.sum(in_sum, axis=0, keepdims=True)

    def products(place):
        cot_high, cot_low = gcat[0 : 2 * chans], gcat[2 * chans :]
        act_h, act_l = high[...], low[...]
        left = jnp.concatenate([cot_high, cot_high, cot_low], axis=1)
        found = dot(left, jnp.concatenate([act_h, act_l, act_h], axis=0), 1, 0)
        grad_a[...] = found
        cross = jnp.sum(fold_lanes(fold_rows(wg[...] * found)), axis=0, keepdims=True)
        put_stats(1, place, (act_sums[0:1], act_sums[1:2], act_sums[2:3], cross))
        left = jnp.concatenate([wg_high[...], wg_high[...], wg_low[...]], axis=1)
        raw[...] = dot(left, jnp.concatenate([act_h, act_l, act_h], axis=1), 1, 1)

    def back_product():
        left = jnp.concatenate([gcat[...], gcat[0 : 2 * chans]], axis=0)
        right = jnp.concatenate([wg_high[...], wg_high[...], wg_low[...]], axis=0)
        e2[...] = dot(left, right, 0, 0)

    def before_c(place):
        length = lens[place]
        totals = read_stats(1, place)
        mean, inverse, count = scales(totals, length)
        sum_e, sum_ea = totals[2], totals[3]
        mean_e = sum_e / count
        mean_ex = inverse * (sum_ea - mean * sum_e) / count
        by_act = -inverse * inverse * mean_ex
        by_one = -inverse * mean_e - by_act * mean
        mean_1, inverse_1, _ = scales(read_stats(0, place), length)
        scale_1 = gamma1[...] * inverse_1
        coef[4:5] = scale_1
        coef[5:6] = beta1[...] - scale_1 * mean_1
        for row, value in ((10, by_act), (11, by_one), (12, inverse), (13, inverse * mean)):
            coef[row : row + 1] = jnp.broadcast_to(value, (1, units))

    def phase_c(place, merged):
        slot = lax.rem(place, 4)
        pair = lax.rem(place, 2)
        length = lens[place]
        keep = lane_mask(length)[0:1]
        y_acc[0] += coef[13:14, 0:LANES] * y_acc[1 + pair]
        inverse, by_mean = coef[12:13, 0:1], coef[13:14, 0:1]
        out = inverse * raw[0:chans] + wide(cols[4] - by_mean * cols[2], frames)
        out_res[pair] = jnp.where(keep, mixed_s[lax.rem(place, 5)] + out, 0.0)
        out = inverse * raw[chans:] + wide(cols[5] - by_mean * cols[3], frames)
        out_skip[pair] = jnp.where(keep, out, 0.0)
        x_acc[...] += inverse * grad_a[...]
        edge_rows = min(frames, plan.tail + CHUNK)

        def lanes_step(lanes, carry):
            cut = pl.ds(lanes, LANES)
            by_a, by_1, inv_e = (coef[k : k + 1, cut] for k in (10, 11, 12))

            def rows_step(row, masked, carry):
                rows = pl.ds(row, CHUNK)
                middle = pl.ds(row + wing, CHUNK)
                behind = pl.ds(row + 2 * wing, CHUNK)
                act = act2[pair, rows, cut]
                g = inv_e * e2[rows, cut] + by_a * act + by_1
                if masked:
                    g = jnp.where(valid_rows(row, CHUNK, length), g, 0.0)
                gc = g * d2[pair, rows, cut]
                gconv[pair, middle, cut] = gc
                parts = (
                    g * (conv[pair, rows, cut] - act), gc, gc * a1[slot, rows, cut],
                    gc * a1[slot, middle, cut], gc * a1[slot, behind, cut],
                )
                return tuple(c + fold_rows(p) for c, p in zip(carry, parts))

            zero = jnp.zeros((8, LANES), F32)
            found = by_rows(rows_step, (zero,) * 5)
            slope_sum, total, n0, n1, n2 = (jnp.sum(f, axis=0, keepdims=True) for f in found)

            def edge_step(c, carry):
                row = c * CHUNK
                gc = gconv[pair, pl.ds(row + wing, CHUNK), cut]
                inside = valid_rows(row + wing, CHUNK, length)
                return carry + fold_rows(jnp.where(inside, 0.0, gc))

            late = zero
            for c in range((frames - edge_rows) // CHUNK, chunks):
                late = edge_step(c, late)
            late = jnp.sum(late, axis=0, keepdims=True)
            early = jnp.sum(gconv[pair, wing : 2 * wing, cut], axis=0, keepdims=True)
            early = jnp.where(first, early, 0.0)
            scale, shift = coef[4:5, cut], coef[5:6, cut]
            gains, bias = gamma1[:, cut], beta1[:, cut]
            reach = (total - early, total, total - late)
            by_beta = jnp.zeros((1, LANES), F32)
            by_gamma = jnp.zeros((1, LANES), F32)
            for k, (n_k, b_k) in enumerate(zip((n0, n1, n2), reach)):
                tap = tap_rows[k : k + 1, cut]
                n_k = scale * n_k + shift * total
                add_sum(TAP + k, lanes, n_k)
                by_beta += tap * b_k
                by_gamma += tap * (n_k - bias * b_k)
            add_sum(SLOPE_TWO, lanes, slope_sum)
            add_sum(B_DEPTH, lanes, total)
            add_sum(BETA_ONE, lanes, by_beta)
            add_sum(GAMMA_ONE, lanes, by_gamma)
            return carry[0] + gains * by_beta, carry[1] + by_gamma

        zero = jnp.zeros((1, LANES), F32)
        put_stats(2, place, by_lanes(lanes_step, (zero, zero), merged))

    def out_copies(item):
        pair = lax.rem(item, 2)
        return (
            pltpu.make_async_copy(out_res.at[pair], res_h.at[item], out_sem.at[0, item]),
            pltpu.make_async_copy(out_skip.at[pair], skip_h.at[item], out_sem.at[1, item]),
        )

    def gs1_copy(item):
        return pltpu.make_async_copy(
            out_gs1.at[lax.rem(item, 2)], gs1_h.at[item], out_sem.at[2, item])

    def gmoved_copy(item):
        return pltpu.make_async_copy(
            gbuf.at[pl.ds(item * frames, frames)], gmoved_h.at[item], out_sem.at[3, item])

    def before_d(place):
        pair = lax.rem(place, 2)
        length = lens[place]
        totals = read_stats(2, place)
        mean, inverse, count = scales(read_stats(0, place), length)
        mean_e, mean_ex = totals[0] / count, totals[1] / count
        by_act = -inverse * inverse * mean_ex
        by_one = -inverse * mean_e - by_act * mean
        for k in range(3):
            coef[6 + k : 7 + k] = tap_rows[k : k + 1] * gamma1[...] * inverse
        for row, value in ((14, by_act), (15, by_one)):
            coef[row : row + 1] = jnp.broadcast_to(value, (1, units))
        gconv[pair, 0:wing] = jnp.where(first, 0.0, halo_g[place, 0])
        gconv[pair, frames + wing :] = jnp.where(last, 0.0, halo_g[place, 1])

    def phase_d(place, merged):
        slot = lax.rem(place, 4)
        pair = lax.rem(place, 2)
        length = lens[place]

        def lanes_step(lanes, carry):
            cut = pl.ds(lanes, LANES)
            slope = slope1[:, cut]
            by_a, by_1 = coef[14:15, cut], coef[15:16, cut]
            u0, u1, u2 = (coef[6 + k : 7 + k, cut] for k in range(3))

            def rows_step(row, masked, carry):
                rows = pl.ds(row, CHUNK)
                middle = pl.ds(row + wing, CHUNK)
                behind = pl.ds(row + 2 * wing, CHUNK)
                act, x = a1[slot, middle, cut], pre1[slot, rows, cut]
                g = by_a * act + by_1 + u0 * gconv[pair, behind, cut]
                g += u1 * gconv[pair, middle, cut] + u2 * gconv[pair, rows, cut]
                if masked:
                    g = jnp.where(valid_rows(row, CHUNK, length), g, 0.0)
                half = jnp.tanh(0.5 * x)
                gp = g * ((0.5 + 0.5 * slope) + (0.5 - 0.5 * slope) * half)
                gp_h, gp_l = halves(gp)
                gp_high[rows, cut] = gp_h
                gp_low[rows, cut] = gp_l
                return carry[0] + fold_rows(g * (x - act)), carry[1] + fold_rows(gp)

            zero = jnp.zeros((8, LANES), F32)
            slope_sum, bias_sum = by_rows(rows_step, (zero, zero))
            add_sum(SLOPE_ONE, lanes, jnp.sum(slope_sum, axis=0, keepdims=True))
            add_sum(B_IN, lanes, jnp.sum(bias_sum, axis=0, keepdims=True))
            return carry

        by_lanes(lanes_step, 0, merged)

    def weight_product(place):
        slot = lax.rem(place, 5)
        g_h, g_l = gp_high[...], gp_low[...]
        gw_acc[...] += dot(mcat[slot], g_h, 1, 0)
        gw_acc[0:chans] += dot(mcat[slot, 0:chans], g_l, 1, 0)

    def mixture_gradient(place):
        slot = lax.rem(place, 5)
        pair = lax.rem(place, 2)
        item = order[place]
        both = dot(w_t[0 : 2 * chans], gp_high[...], 1, 1)
        g_mixed = both[0:chans] + both[chans:] + dot(w_t[0:chans], gp_low[...], 1, 1)
        g_mixed = jnp.where(lane_mask(lens[place])[0:1], cr[item] + g_mixed, 0.0)
        out_gs1[pair] = wide(cols[0], frames) * g_mixed
        gain_acc[0] += fold_lanes(g_mixed * s1[item])
        gain_acc[1] += fold_lanes(g_mixed * moved_s[slot])
        gbuf[pl.ds(pl.multiple_of(place * frames, 8), frames)] = (
            wide(cols[1], frames) * g_mixed).T

    big, small_part = plan.seg // n_it, plan.seg // n_it // n_tm

    def segment(seg):
        return seg * plan.seg, big, small_part

    def stage_copies(seg, stage):
        start, big, small = segment(seg)
        offset = start // n_it
        send, recv = ar_send.at[seg, stage], ar_recv.at[seg, stage]
        if stage == 0:
            return "items", n_it, it, lambda peer: remote(
                gall.at[pl.ds(start + peer * big, big)], rs_it.at[it, pl.ds(offset, big)],
                send, recv, "items", peer)
        if stage == 1:
            return "tm", n_tm, tm, lambda peer: remote(
                part.at[pl.ds(offset + peer * small, small)],
                rs_tm.at[tm, pl.ds(offset // n_tm, small)], send, recv, "tm", peer)
        if stage == 2:
            mine = quarter.at[pl.ds(offset + tm * small, small)]
            return "tm", n_tm, tm, lambda peer: remote(mine, mine, send, recv, "tm", peer)
        mine = done.at[pl.ds(start + it * big, big)]
        return "items", n_it, it, lambda peer: remote(mine, mine, send, recv, "items", peer)

    def stage_start(seg, stage):
        axis, count, mine, copy = stage_copies(seg, stage)
        others(axis, count, mine, lambda peer: copy(peer).start())

    def stage_wait(seg, stage, sem):
        start, big, small = segment(seg)
        count, rows = ((n_it, big), (n_tm, small), (n_tm, small), (n_it, big))[stage]
        if count > 1:
            block = gall.at[pl.ds(0, (count - 1) * rows)]
            pltpu.make_async_copy(block, block, sem.at[seg, stage]).wait()

    def added(ref, count, rows):
        total = ref[0, rows]
        for peer in range(1, count):
            total = total + ref[peer, rows]
        return total

    def stage_zero(seg):
        start, big, _ = segment(seg)
        rs_it[it, pl.ds(start // n_it, big)] = gall[pl.ds(start + it * big, big)]
        stage_start(seg, 0)

    def stage_one(seg):
        start, big, small = segment(seg)
        offset = start // n_it
        stage_wait(seg, 0, ar_recv)
        part[pl.ds(offset, big)] = added(rs_it, n_it, pl.ds(offset, big))
        rs_tm[tm, pl.ds(offset // n_tm, small)] = part[pl.ds(offset + tm * small, small)]
        stage_start(seg, 1)

    def stage_two(seg):
        start, big, small = segment(seg)
        offset = start // n_it
        stage_wait(seg, 1, ar_recv)
        quarter[pl.ds(offset + tm * small, small)] = added(
            rs_tm, n_tm, pl.ds(offset // n_tm, small))
        stage_start(seg, 2)

    def stage_three(seg):
        start, big, _ = segment(seg)
        offset = start // n_it
        stage_wait(seg, 2, ar_recv)
        done[pl.ds(start + it * big, big)] = quarter[pl.ds(offset, big)]
        stage_start(seg, 3)

    def weights_sum():
        for side, weight in enumerate((w_res, w_skip)):
            rows = slice(side * chans, (side + 1) * chans)
            ones = jnp.sum(gb_acc[rows], axis=1, keepdims=True)
            centred = x_acc[rows] - jnp.sum(y_acc[0, rows], axis=1, keepdims=True)
            grad = gamma2[...] * centred + beta2[...] * ones
            for b in range(blocks):
                gall[b * 2 * chans + side * chans : b * 2 * chans + (side + 1) * chans] = grad[
                    :, b * LANES : (b + 1) * LANES]
            sums[GAMMA_TWO : GAMMA_TWO + 1] += jnp.sum(
                weight[...] * centred, axis=0, keepdims=True)
            sums[BETA_TWO : BETA_TWO + 1] += jnp.sum(weight[...] * ones, axis=0, keepdims=True)
            sums[NARROW : NARROW + 1, (2 + side) * LANES : (3 + side) * LANES] = jnp.sum(
                gb_acc[rows].T, axis=0, keepdims=True)

    def input_weights_sum():
        start = plan.weight_segs * plan.seg
        grad = gw_acc[0:chans] + gw_acc[chans:]
        for b in range(blocks):
            gall[start + b * chans : start + (b + 1) * chans] = grad[
                :, b * LANES : (b + 1) * LANES]

    def narrow_sums():
        for side in range(2):
            sums[NARROW : NARROW + 1, side * LANES : (side + 1) * LANES] = jnp.sum(
                gain_acc[side].T, axis=0, keepdims=True)
        sums[SLOPE_ONE : SLOPE_ONE + 1] = sums[SLOPE_ONE : SLOPE_ONE + 1] / (1.0 - slope1[...])
        sums[SLOPE_TWO : SLOPE_TWO + 1] = sums[SLOPE_TWO : SLOPE_TWO + 1] / (1.0 - slope2[...])
        sums[GAMMA_ONE : GAMMA_ONE + 1] = sums[GAMMA_ONE : GAMMA_ONE + 1] / gamma1[...]
        for b in range(blocks):
            small[b * SUM_ROWS : (b + 1) * SUM_ROWS] = sums[:, b * LANES : (b + 1) * LANES]
        small_it[it] = small[...]

    narrow = plan.small // n_tm

    def small_copies(stage):
        send, recv = ar_send.at[plan.segs, stage], ar_recv.at[plan.segs, stage]
        if stage == 0:
            return "items", n_it, it, lambda peer: remote(
                small, small_it.at[it], send, recv, "items", peer)
        if stage == 1:
            return "tm", n_tm, tm, lambda peer: remote(
                small.at[pl.ds(peer * narrow, narrow)], small_tm.at[tm], send, recv, "tm", peer)
        mine = small_done.at[pl.ds(tm * narrow, narrow)]
        return "tm", n_tm, tm, lambda peer: remote(mine, mine, send, recv, "tm", peer)

    def small_start(stage):
        axis, count, mine, copy = small_copies(stage)
        others(axis, count, mine, lambda peer: copy(peer).start())

    def small_wait(stage, sem):
        count, rows = ((n_it, plan.small), (n_tm, narrow), (n_tm, narrow))[stage]
        if count > 1:
            block = gall.at[pl.ds(0, (count - 1) * rows)]
            pltpu.make_async_copy(block, block, sem.at[plan.segs, stage]).wait()

    def small_one():
        small_wait(0, ar_recv)
        small_wait(0, ar_send)
        total = small_it[0]
        for peer in range(1, n_it):
            total = total + small_it[peer]
        small[...] = total
        small_tm[tm] = small[pl.ds(tm * narrow, narrow)]
        small_start(1)

    def small_two():
        small_wait(1, ar_recv)
        total = small_tm[0]
        for peer in range(1, n_tm):
            total = total + small_tm[peer]
        small_done[pl.ds(tm * narrow, narrow)] = total
        small_start(2)

    load(0).wait()
    load(1).wait()
    arrived(0)
    mix(0)
    mix_product(0)
    load(2).wait()
    load(3).wait()
    end = items - 1

    def step(index, carry):
        def within(lag, back=0):
            return (index >= lag) & (index <= end + lag - back)

        pl.when(within(6))(lambda: gs1_copy(index - 6).wait())

        side_by_side(index, (4, end), (
            (0, end, lambda merged: phase_a(index, merged)),
            (4, end + 3, lambda merged: weight_product(index - 4)),
            (4, end + 3, lambda merged: mixture_gradient(index - 4)),
        ))

        @pl.when(within(0))
        def _():
            send_stats(0, index)
            send_halo(0, index, a1, lax.rem(index, 4), halo_a)

        @pl.when(index == end + 4)
        def _():
            weight_product(index - 4)
            input_weights_sum()
            for seg in range(plan.weight_segs, plan.segs):
                stage_zero(seg)
            mixture_gradient(index - 4)

        @pl.when(within(4))
        def _():
            gs1_copy(index - 4).start()
            gmoved_copy(index - 4).start()

        bulk(index, 0)

        @pl.when(within(1))
        def _():
            wait_halo(0, index - 1, a1, lax.rem(index + 3, 4), halo_a)
            wait_stats(0, index - 1, stat_recv)
            before_b(index - 1)

        side_by_side(index, (2, end + 1), (
            (1, end + 1, lambda merged: phase_b(index - 1, merged)),
            (2, end + 2, lambda merged: back_product()),
        ))

        @pl.when(within(2))
        def _():
            wait_stats(1, index - 2, stat_recv)
            before_c(index - 2)

        @pl.when(within(4))
        def _():
            for copy in out_copies(index - 4):
                copy.wait()

        pl.when(within(1))(lambda: cotangents(index - 1))
        side_by_side(index, (2, end + 1), (
            (2, end + 2, lambda merged: phase_c(index - 2, merged)),
            (1, end + 1, lambda merged: products(index - 1)),
        ))

        @pl.when(within(1))
        def _():
            send_stats(1, index - 1)

        @pl.when(within(2))
        def _():
            send_stats(2, index - 2)
            send_halo(1, index - 2, gconv, lax.rem(index, 2), halo_g)
            for copy in out_copies(index - 2):
                copy.start()

        @pl.when(index == end + 2)
        def _():
            weights_sum()
            for seg in range(plan.weight_segs):
                stage_zero(seg)

        bulk(index, 1)

        @pl.when(within(3))
        def _():
            wait_halo(1, index - 3, gconv, lax.rem(index + 1, 2), halo_g)
            wait_stats(2, index - 3, stat_recv)
            before_d(index - 3)

        @pl.when(index < end)
        def _():
            arrived(index + 1)
            mix(index + 1)

        side_by_side(index, (3, end - 1), (
            (3, end + 3, lambda merged: phase_d(index - 3, merged)),
            (0, end - 1, lambda merged: mix_product(index + 1)),
        ))
        return carry

    lax.fori_loop(0, items + 4, step, 0)
    narrow_sums()
    small_start(0)
    ahead = 2
    for seg in range(plan.segs + ahead):
        if seg < plan.segs:
            stage_one(seg)
        if seg >= ahead:
            stage_two(seg - ahead)
    small_one()
    for seg in range(plan.segs):
        stage_three(seg)
    small_two()
    for seg in range(plan.segs):
        stage_wait(seg, 3, ar_recv)
    small_wait(2, ar_recv)
    total_copy = pltpu.make_async_copy(done, total_h, out_sem.at[0, 0])
    total_copy.start()
    small_copy = pltpu.make_async_copy(small_done, small_h, out_sem.at[1, 0])
    small_copy.start()

    def finish(item, carry):
        for phase in range(3):
            wait_stats(phase, item, stat_send)
        gmoved_copy(item).wait()
        return carry

    def finish_chunk(chunk, carry):
        @pl.when(jnp.logical_not(first))
        def _():
            to_previous(chunk).wait_send()

        @pl.when(jnp.logical_not(last))
        def _():
            to_next(chunk).wait_send()
            to_previous(chunk).wait_recv()

        return carry

    lax.fori_loop(0, items, finish, 0)
    lax.fori_loop(0, plan.parts, finish_chunk, 0)
    for item in range(max(0, items - 2), items):
        gs1_copy(item).wait()
    for seg in range(plan.segs):
        for stage in range(4):
            stage_wait(seg, stage, ar_send)
    small_wait(1, ar_send)
    small_wait(2, ar_send)
    total_copy.wait()
    small_copy.wait()


def prelude(plan):
    items, frames, chans = plan.items, plan.frames, plan.chans
    rows = items * frames
    groups = rows // GROUP
    table = (rounded(groups, LANES) // LANES, LANES)
    per_item = frames // GROUP

    def body(
        offs_in, lens_in, s2_h, s2t_h, packed_h, pack, order, offs, lens, window, window_back,
        which, s2, s2t, packed, lookup_v, lookup, held, in_sem, out_sem, table_sem, send, recv,
    ):
        n_it = plan.n_it
        it = lax.axis_index("items")
        load = pltpu.make_async_copy(s2_h, s2, in_sem)
        load.start()
        barrier = pltpu.get_barrier_semaphore()

        def peers(act):
            def turn(step, carry):
                act(lax.rem(it + step, n_it))
                return carry

            lax.fori_loop(1, n_it, turn, 0)

        def copy(peer):
            return pltpu.make_async_remote_copy(
                src_ref=held.at[it], dst_ref=held.at[it], send_sem=send, recv_sem=recv,
                device_id={"items": peer}, device_id_type=MESH)

        peers(lambda peer: pl.semaphore_signal(
            barrier, inc=1, device_id={"items": peer}, device_id_type=MESH))
        given = [offs_in[i] for i in range(items)]
        places = []
        for i in range(items):
            rank = jnp.int32(0)
            for j in range(items):
                if j != i:
                    before = given[j] <= given[i] if j < i else given[j] < given[i]
                    rank += jnp.where(before, 1, 0)
            places.append(jnp.where(rank % 2 == 0, rank // 2, items - 1 - rank // 2))
        starts, needs, end = [], [], jnp.int32(0)
        taken = []
        for k in range(items):
            here = [jnp.where(place == k, 1, 0) for place in places]
            item = sum(i * h for i, h in enumerate(here))
            offset = sum(given[i] * h for i, h in enumerate(here))
            taken.append(item)
            order[k] = item
            offs[k] = offset
            lens[k] = sum(lens_in[i] * h for i, h in enumerate(here))
            needs.append((offset + GROUP - 1) // GROUP)
            starts.append(end)
            end = end + needs[k]
            window[k] = end
        held[it] = jnp.full((1, LANES), end, jnp.int32)
        pl.semaphore_wait(barrier, n_it - 1)
        peers(lambda peer: copy(peer).start())

        index = (
            lax.broadcasted_iota(jnp.int32, table, 0) * LANES
            + lax.broadcasted_iota(jnp.int32, table, 1))

        def looked_up(index, firsts):
            total, previous = index, jnp.int32(0)
            for k in range(items):
                shift = firsts[k] - starts[k]
                total = total + jnp.where(index >= starts[k], shift - previous, 0)
                previous = shift
            return jnp.minimum(total, groups - 1)

        lookup_v[...] = looked_up(
            index, [(k + 1) * per_item - needs[k] for k in range(items)])
        to_smem = pltpu.make_async_copy(lookup_v, lookup, table_sem)
        to_smem.start()
        load.wait()
        for k in range(items):
            s2t[k * frames : (k + 1) * frames] = s2[taken[k]].T
        to_smem.wait()
        own_out = pltpu.make_async_copy(s2t, s2t_h, out_sem.at[0])
        own_out.start()

        def turn(group, carry):
            source = lookup[group // LANES, group % LANES] * GROUP
            packed[pl.ds(pl.multiple_of(group * GROUP, GROUP), GROUP)] = s2t[
                pl.ds(source, GROUP)]
            return carry

        lax.fori_loop(0, groups, turn, 0, unroll=16)
        packed_out = pltpu.make_async_copy(packed, packed_h, out_sem.at[1])
        packed_out.start()

        if n_it > 1:
            block = held.at[pl.ds(0, n_it - 1)]
            pltpu.make_async_copy(block, block, recv).wait()
        most = held[0]
        for peer in range(1, n_it):
            most = jnp.maximum(most, held[peer])
        choice = jnp.zeros((1, LANES), jnp.int32)
        sent = jnp.full((1, LANES), plan.caps[0] // GROUP, jnp.int32)
        for low_cap, cap in zip(plan.caps[:-1], plan.caps[1:]):
            more = most * GROUP > low_cap
            choice += more.astype(jnp.int32)
            sent += jnp.where(more, (cap - low_cap) // GROUP, 0)
        which[0] = jnp.max(choice)
        base = jnp.max(sent) - end
        for k in range(items):
            window_back[k] = base + starts[k]
        back = looked_up(index - base, [jnp.int32(k * per_item) for k in range(items)])
        pack[...] = jnp.where(index < base, 0, back)
        own_out.wait()
        packed_out.wait()
        if n_it > 1:
            pltpu.make_async_copy(block, block, send).wait()

    smem = pl.BlockSpec(memory_space=pltpu.SMEM)
    hbm = pl.BlockSpec(memory_space=pl.ANY)
    short = jax.ShapeDtypeStruct((items,), jnp.int32)
    flat = jax.ShapeDtypeStruct((rows, chans), F32)
    sem = pltpu.SemaphoreType.DMA
    return pl.pallas_call(
        body,
        out_shape=(
            flat, flat, jax.ShapeDtypeStruct(table, jnp.int32), short, short, short, short, short,
            jax.ShapeDtypeStruct((1,), jnp.int32),
        ),
        in_specs=[smem, smem, hbm],
        out_specs=(hbm, hbm, pl.BlockSpec(memory_space=pltpu.VMEM)) + (smem,) * 6,
        scratch_shapes=[
            pltpu.VMEM((items, chans, frames), F32), pltpu.VMEM((rows, chans), F32),
            pltpu.VMEM((rows, chans), F32), pltpu.VMEM(table, jnp.int32),
            pltpu.SMEM(table, jnp.int32), pltpu.VMEM((plan.n_it, 1, LANES), jnp.int32),
            sem, sem((2,)), sem, sem, sem,
        ],
        compiler_params=pltpu.CompilerParams(
            collective_id=0, has_side_effects=True, vmem_limit_bytes=62 * 2**20),
        name="prelude",
    )


def finisher(plan, rows):
    items, frames, chans, units = plan.items, plan.frames, plan.chans, plan.units
    blocks = units // LANES

    def body(
        order, offs, window, gmoved_h, from_right_h, total_h, small_h, res_h, skip_h, gs1_h, *rest
    ):
        outs, scratch = rest[:20], rest[20:]
        cat, gs2, total, small, passed, in_sem, out_sem, pass_sem, total_sem = scratch
        out_res, out_skip, out_gs1, out_gs2 = outs[:4]
        last = lax.axis_index("tm") == plan.n_tm - 1
        def through(kind, item):
            src, dst = ((res_h, out_res), (skip_h, out_skip), (gs1_h, out_gs1))[kind]
            held = passed.at[kind, item]
            return (
                pltpu.make_async_copy(src.at[item], held, pass_sem.at[0, kind, item]),
                pltpu.make_async_copy(held, dst.at[order[item]], pass_sem.at[1, kind, item]),
            )

        def loads(item):
            start = pl.multiple_of(window[item] * GROUP, GROUP)
            return (
                pltpu.make_async_copy(
                    gmoved_h.at[item], cat.at[item, pl.ds(0, frames)], in_sem.at[0, item]),
                pltpu.make_async_copy(
                    from_right_h.at[pl.ds(start, frames)], cat.at[item, pl.ds(frames, frames)],
                    in_sem.at[1, item]),
            )

        def store(item):
            return pltpu.make_async_copy(gs2.at[item], out_gs2.at[order[item]], out_sem.at[item])

        def start(item, carry):
            for copy in loads(item):
                copy.start()
            for kind in range(3):
                through(kind, item)[0].start()
            return carry

        total_copy = pltpu.make_async_copy(total_h, total, total_sem.at[0])
        total_copy.start()
        small_copy = pltpu.make_async_copy(small_h, small, total_sem.at[1])
        small_copy.start()
        lax.fori_loop(0, items, start, 0)

        def turn(item, carry):
            for copy in loads(item):
                copy.wait()
            for kind in range(3):
                arriving, leaving = through(kind, item)
                arriving.wait()
                leaving.start()

            @pl.when(last)
            def _():
                cat[item, frames:] = jnp.zeros((frames, chans), F32)

            gs2[item] = cat[item, pl.ds(offs[item], frames), :].T
            store(item).start()
            return carry

        lax.fori_loop(0, items, turn, 0)
        total_copy.wait()
        small_copy.wait()
        (
            gain_1, gain_2, g_in, gb_in, g_slope1, g_gamma1, g_beta1, g_taps, gb_depth, g_slope2,
            g_gamma2, g_beta2, g_res, gb_res, g_skip, gb_skip,
        ) = outs[4:]
        start_in = plan.weight_segs * plan.seg
        for b in range(blocks):
            cut = slice(b * LANES, (b + 1) * LANES)
            g_res[:, cut] = total[2 * b * chans : (2 * b + 1) * chans]
            g_skip[:, cut] = total[(2 * b + 1) * chans : (2 * b + 2) * chans]
            g_in[cut] = total[start_in + b * chans : start_in + (b + 1) * chans].T
            sums = small[b * SUM_ROWS : (b + 1) * SUM_ROWS]
            for out, row in (
                (gb_in, B_IN), (g_slope1, SLOPE_ONE), (g_gamma1, GAMMA_ONE), (g_beta1, BETA_ONE),
                (gb_depth, B_DEPTH), (g_slope2, SLOPE_TWO), (g_gamma2, GAMMA_TWO),
                (g_beta2, BETA_TWO),
            ):
                out[:, cut] = sums[row : row + 1]
            g_taps[:, cut] = sums[TAP : TAP + 3]
            (gain_1, gain_2, gb_res, gb_skip)[b][...] = sums[NARROW : NARROW + 1]

        def end(item, carry):
            store(item).wait()
            for kind in range(3):
                through(kind, item)[1].wait()
            return carry

        lax.fori_loop(0, items, end, 0)

    smem = pl.BlockSpec(memory_space=pltpu.SMEM)
    hbm = pl.BlockSpec(memory_space=pl.ANY)
    vmem = pl.BlockSpec(memory_space=pltpu.VMEM)
    big = jax.ShapeDtypeStruct((items, chans, frames), F32)

    def array(*shape):
        return jax.ShapeDtypeStruct(shape, F32)

    narrow, per_unit = array(1, chans), array(1, units)
    sem = pltpu.SemaphoreType.DMA
    return pl.pallas_call(
        body,
        out_shape=(big,) * 4 + (
            narrow, narrow, array(units, chans), per_unit, per_unit, per_unit, per_unit,
            array(3, units), per_unit, per_unit, per_unit, per_unit, array(chans, units), narrow,
            array(chans, units), narrow,
        ),
        in_specs=[smem] * 3 + [hbm] * 7,
        out_specs=(hbm,) * 4 + (vmem,) * 16,
        scratch_shapes=[
            pltpu.VMEM((items, 2 * frames, chans), F32), pltpu.VMEM((items, chans, frames), F32),
            pltpu.VMEM((rows, LANES), F32), pltpu.VMEM((plan.small, LANES), F32),
            pltpu.VMEM((3, items, chans, frames), F32),
            sem((2, items)), sem((items,)), sem((2, 3, items)), sem((2,)),
        ],
        compiler_params=pltpu.CompilerParams(vmem_limit_bytes=62 * 2**20),
        name="finisher",
    )


def per_device(
    mesh, source_one, source_two, offsets, lengths, gain_one, gain_two, w_in, b_in, slope_one,
    first_norm_gain, first_norm_bias, depthwise_weight, depthwise_bias, slope_two,
    second_norm_gain, second_norm_bias, w_res, b_res, w_skip, b_skip, cot_res, cot_skip,
):
    items, chans, frames = source_one.shape
    units = w_in.shape[0]
    plan = Plan(mesh, items, chans, frames, units)
    n_tm, n_it, wing = plan.n_tm, plan.n_it, DILATION_RATE
    full = items * frames
    s2t, packed, pack, order, offs, lens, window, window_back, which = prelude(plan)(
        offsets, lengths, source_two)

    def row(value):
        return value.reshape(1, -1)

    smem = pl.BlockSpec(memory_space=pltpu.SMEM)
    hbm = pl.BlockSpec(memory_space=pl.ANY)
    vmem = pl.BlockSpec(memory_space=pltpu.VMEM)
    rows = plan.segs * plan.seg

    def floats(*shape):
        return pltpu.VMEM(shape, F32)

    def shorts(*shape):
        return pltpu.VMEM(shape, BF16)

    big = jax.ShapeDtypeStruct((items, chans, frames), F32)
    sem = pltpu.SemaphoreType.DMA
    def block(sent, index):
        return pl.pallas_call(
            functools.partial(kernel, plan, sent),
            out_shape=(
                big, big, big, jax.ShapeDtypeStruct((items, frames, chans), F32),
                jax.ShapeDtypeStruct((full + frames, chans), F32),
                jax.ShapeDtypeStruct((rows, LANES), F32),
                jax.ShapeDtypeStruct((plan.small, LANES), F32),
            ),
            in_specs=[smem] * 5 + [hbm] * 5 + [vmem] * 16,
            out_specs=[hbm] * 7,
            scratch_shapes=[
                floats(items, chans, frames), floats(items, frames, chans),
                floats(items, chans, frames), floats(items, chans, frames),
                floats(sent, chans), floats(frames + sent, chans), floats(full, chans),
                floats(sent, chans),
                floats(2, chans, frames), floats(2, chans, frames), floats(2, chans, frames),
                floats(2 * frames, chans),
                floats(5, chans, frames), floats(5, chans, frames), shorts(5, 2 * chans, frames),
                floats(frames, units), floats(4, frames + 2 * wing, units),
                floats(4, frames, units),
                floats(2, frames, units), floats(2, frames, units), floats(2, frames, units),
                floats(frames, units), shorts(frames, units), shorts(frames, units),
                floats(2 * chans, frames), floats(2 * chans, units),
                floats(2, frames + 2 * wing, units), shorts(frames, units),
                shorts(frames, units), shorts(4 * chans, frames),
                floats(items, 2, wing, units), floats(items, 2, wing, units),
                floats(3, items, n_tm, 4, LANES), floats(8, LANES), floats(16, units),
                shorts(3 * chans, units), shorts(2 * chans, units), shorts(2 * chans, units),
                floats(2 * chans, units), floats(6, chans, LANES),
                floats(2 * chans, units), floats(2 * chans, units),
                floats(2 * chans, LANES), floats(3, 2 * chans, LANES), floats(2, chans, LANES),
                floats(SUM_ROWS, units),
                floats(rows, LANES), floats(n_it, rows // n_it, LANES),
                floats(rows // n_it, LANES),
                floats(n_tm, rows // n_it // n_tm, LANES), floats(rows // n_it, LANES),
                floats(rows, LANES),
                floats(plan.small, LANES), floats(n_it, plan.small, LANES),
                floats(n_tm, plan.small // n_tm, LANES), floats(plan.small, LANES),
                sem((4,)), sem((4, items)), sem((plan.parts,)), sem((plan.parts,)),
                sem((plan.parts,)), sem((plan.parts,)), sem((2, items, 2)), sem((2, items, 2)),
                sem((3, items)), sem((3, items)), sem((plan.segs + 1, 4)),
                sem((plan.segs + 1, 4)),
            ],
            compiler_params=pltpu.CompilerParams(
                collective_id=1 + index, has_side_effects=True,
                vmem_limit_bytes=62 * 2**20),
            name="tcn_block",
        )

    branches = [block(sent, index) for index, sent in enumerate(plan.caps)]
    res, skip, gs1, gmoved, from_right, total, narrow = lax.switch(
        which[0], branches,
        order, offs, lens, window, pack, source_one, s2t.reshape(items, frames, chans), packed,
        cot_res, cot_skip,
        row(gain_one), row(gain_two), w_in, row(b_in), row(slope_one), row(first_norm_gain),
        row(first_norm_bias), depthwise_weight.T, row(depthwise_bias), row(slope_two),
        row(second_norm_gain), row(second_norm_bias), w_res, row(b_res), w_skip, row(b_skip),
    )
    outs = list(finisher(plan, rows)(
        order, offs, window_back, gmoved, from_right, total, narrow, res, skip, gs1))
    outs[11] = outs[11].T
    return tuple(out.reshape(-1) if out.shape[0] == 1 else out for out in outs)


def solution(mesh):
    split = P("items", None, "tm")
    in_specs = (split, split, P("items"), P("items")) + (P(),) * 16 + (split, split)
    out_specs = (split,) * 4 + (P(),) * 16
    return jax.shard_map(
        functools.partial(per_device, mesh), mesh=mesh, in_specs=in_specs, out_specs=out_specs,
        check_vma=False,
    )
```

```python
import functools

import jax
import jax.numpy as jnp
from jax import lax
from jax.experimental import pallas as pl
from jax.experimental.pallas import tpu as pltpu
from jax.sharding import PartitionSpec as P

DILATION_RATE = 16
EPS = 1e-05
LANES = 128
F32 = jnp.float32
BF16 = jnp.bfloat16
MESH = pl.DeviceIdType.MESH
CHUNK = 64
GROUP = 16

B_IN, SLOPE_ONE, GAMMA_ONE, BETA_ONE, TAP, B_DEPTH, SLOPE_TWO, GAMMA_TWO, BETA_TWO, NARROW = (
    0, 1, 2, 3, 4, 7, 8, 9, 10, 11,
)
SUM_ROWS = 16


def halves(value):
    high = value.astype(BF16)
    return high, (value - high.astype(F32)).astype(BF16)


def dot(left, right, over_left, over_right):
    return lax.dot_general(
        left, right, (((over_left,), (over_right,)), ((), ())), preferred_element_type=F32
    )


def fold_rows(value):
    return jnp.sum(value.reshape(value.shape[0] // 8, 8, value.shape[1]), axis=0)


def fold_lanes(value):
    total = value[:, :LANES]
    for start in range(LANES, value.shape[1], LANES):
        total = total + value[:, start : start + LANES]
    return total


def column(row):
    return jnp.broadcast_to(row, (LANES, LANES)).T


def wide(tile, width):
    return jnp.concatenate([tile] * (width // LANES), axis=1)


def rounded(size, step):
    return -(-size // step) * step


class Plan:
    def __init__(self, mesh, items, chans, frames, units):
        self.n_tm = mesh.shape["tm"]
        self.n_it = mesh.shape["items"]
        self.items, self.chans, self.frames, self.units = items, chans, frames, units
        whole = frames * self.n_tm
        self.tail = min(frames, rounded(whole // 32, CHUNK))
        step = 8 * self.n_tm * self.n_it
        self.seg = step
        weight_rows, rows = 2 * chans * units // LANES, chans * units // LANES
        if step >= weight_rows + rows:
            self.weight_segs, self.segs, self.in_start = 0, 1, weight_rows
        else:
            self.weight_segs = -(-weight_rows // step)
            self.segs = self.weight_segs + -(-rows // step)
            self.in_start = self.weight_segs * step
        self.small = rounded(SUM_ROWS * units // LANES, 8 * self.n_tm)
        full = items * frames
        self.parts = 32
        self.caps = tuple(sorted({
            rounded(full * part // 16, GROUP * self.parts) for part in (9, 10, 11, 12, 16)}))
        if items == 8 and self.caps[0] >= 4 * frames:
            self.arrive = (4, 8, 12, 16, 24, 32, 32, 32)
            self.out = (8, ((2, 2), (3, 2), (3, 3), (3, 2), (4, 0)))
            self.back = {6: (2, 2), 7: (3, 3), 8: (3, 3), 9: (3, 3), 10: (2, 0)}
        else:
            self.arrive = (self.parts,) * items
            self.out = (self.parts, ())
            self.back = {items + 3: (self.parts, 0)}


def kernel(plan, rows_sent, *refs):
    n_tm, n_it = plan.n_tm, plan.n_it
    items, chans, frames, units = plan.items, plan.chans, plan.frames, plan.units
    wing = DILATION_RATE
    blocks = units // LANES
    (
        order, offs, lens, window, pack, s1_h, s2t_h, packed_h, cr_h, cs_h,
        gain1, gain2, w_in, b_in, slope1, gamma1, beta1, tap_rows, b_depth, slope2, gamma2, beta2,
        w_res, b_res, w_skip, b_skip,
        res_h, skip_h, gs1_h, gmoved_h, from_right_h, total_h, small_h,
        s1, s2t, cr, cs, from_left, staged, gbuf, gpack, out_skip, out_gs1, cat,
        moved_s, mixed_s, mcat, pre_raw, a1, pre1, conv, act2, d2, e2, high, low, grad_a,
        gconv, gp_high, gp_low, gcat, edges, halo_m, edge_act, halo_g, stats, act_sums, coef, out_coef,
        w_t, wg_high, wg_low, wg, cols, x_acc, gw_acc, gb_acc, y_acc, gain_acc, sums,
        gall, rs_it, part, rs_tm, quarter, done, small, small_it, small_tm, small_done,
        in_sem, out_sem, left_send, left_recv, right_send, right_recv,
        halo_send, halo_recv, stat_send, stat_recv, ar_send, ar_recv,
    ) = refs
    size = rows_sent // plan.parts
    out_res = out_gs1
    tm = lax.axis_index("tm")
    it = lax.axis_index("items")
    first, last = tm == 0, tm == n_tm - 1
    base = tm * frames
    whole = frames * n_tm

    def remote(src, dst, send, recv, axis, peer):
        return pltpu.make_async_remote_copy(
            src_ref=src, dst_ref=dst, send_sem=send, recv_sem=recv,
            device_id={axis: peer}, device_id_type=MESH,
        )

    def others(axis, count, mine, act):
        def turn(step, carry):
            act(lax.rem(mine + step, count))
            return carry

        lax.fori_loop(1, count, turn, 0)

    def load(kind):
        src, dst = ((s2t_h, s2t), (s1_h, s1), (cr_h, cr), (cs_h, cs))[kind]
        return pltpu.make_async_copy(src, dst, in_sem.at[kind])

    for kind in range(4):
        load(kind).start()

    barrier = pltpu.get_barrier_semaphore()

    def greet(axis):
        def act(peer):
            pl.semaphore_signal(barrier, inc=1, device_id={axis: peer}, device_id_type=MESH)

        return act

    others("tm", n_tm, tm, greet("tm"))
    others("items", n_it, it, greet("items"))
    pl.semaphore_wait(barrier, n_tm + n_it - 2)

    def to_next(chunk):
        cut = pl.ds(chunk * size, size)
        return remote(
            packed_h.at[cut], from_left.at[cut], left_send.at[chunk], left_recv.at[chunk],
            "tm", jnp.minimum(tm + 1, n_tm - 1),
        )

    def to_previous(chunk):
        cut = pl.ds(chunk * size, size)
        return remote(
            gpack.at[cut], from_right_h.at[cut], right_send.at[chunk], right_recv.at[chunk],
            "tm", jnp.maximum(tm - 1, 0),
        )

    def start_to_next(chunk):
        @pl.when((chunk < plan.parts) & jnp.logical_not(last))
        def _():
            to_next(chunk).start()

    for chunk in range(plan.out[0]):
        start_to_next(chunk)

    def arrived(place):
        def take(chunk, carry):
            @pl.when(jnp.logical_not(first))
            def _():
                to_next(chunk).wait_recv()
                staged[pl.ds(pl.multiple_of(frames + chunk * size, 8), size)] = from_left[
                    pl.ds(pl.multiple_of(chunk * size, 8), size)]

            return carry

        for k in range(items):
            low_end, high_end = (plan.arrive[k - 1] if k else 0), plan.arrive[k]
            if high_end > low_end:
                @pl.when(place == k)
                def _():
                    lax.fori_loop(low_end, high_end, take, 0)

    def send_back(low_end, high_end):
        def put(chunk, carry):
            def turn(block, carry):
                block = chunk * (size // GROUP) + block
                source = pack[block // LANES, block % LANES] * GROUP
                gpack[pl.ds(pl.multiple_of(block * GROUP, GROUP), GROUP)] = gbuf[
                    pl.ds(source, GROUP)]
                return carry

            lax.fori_loop(0, size // GROUP, turn, 0, unroll=True)
            pl.when(jnp.logical_not(first))(to_previous(chunk).start)
            return carry

        lax.fori_loop(low_end, high_end, put, 0)

    def bulk(index, point):
        sent = plan.out[0]
        for k, counts in enumerate(plan.out[1]):
            start, end = sent + point * counts[0], sent + counts[0] + point * counts[1]
            sent += sum(counts)
            if end > start:
                @pl.when(index == k)
                def _():
                    for chunk in range(start, end):
                        start_to_next(chunk)

        returned = 0
        for k, counts in plan.back.items():
            start = returned + point * counts[0]
            end = returned + counts[0] + point * counts[1]
            returned += sum(counts)
            if end > start:
                pl.when(index == k)(functools.partial(send_back, start, end))

    w_high, w_low = halves(w_in[...].T)
    w_t[0:chans] = w_high
    w_t[chans : 2 * chans] = w_low
    w_t[2 * chans :] = w_high
    wg[0:chans] = w_res[...] * gamma2[...]
    wg[chans:] = w_skip[...] * gamma2[...]
    high_part, low_part = halves(wg[...])
    wg_high[...] = high_part
    wg_low[...] = low_part
    cols[0] = column(gain1[...])
    cols[1] = column(gain2[...])
    for side, (weight, bias) in enumerate(((w_res, b_res), (w_skip, b_skip))):
        weight_sum = jnp.sum(wg[side * chans : (side + 1) * chans], axis=1, keepdims=True)
        shift = jnp.sum(weight[...] * beta2[...], axis=1, keepdims=True)
        cols[2 + side] = jnp.broadcast_to(weight_sum, (chans, LANES))
        cols[4 + side] = jnp.broadcast_to(shift, (chans, LANES)) + column(bias[...])
    x_acc[...] = jnp.zeros_like(x_acc)
    gw_acc[...] = jnp.zeros_like(gw_acc)
    gb_acc[...] = jnp.zeros_like(gb_acc)
    y_acc[...] = jnp.zeros_like(y_acc)
    gain_acc[...] = jnp.zeros_like(gain_acc)
    sums[...] = jnp.zeros_like(sums)

    main = (frames - plan.tail) // CHUNK
    chunks = frames // CHUNK

    def by_lanes(act, init, merged):
        if merged:
            for b in range(blocks):
                init = act(b * LANES, init)
            return init
        return lax.fori_loop(0, blocks, lambda b, c: act(pl.multiple_of(b * LANES, LANES), c), init)

    def side_by_side(index, together, parts):
        low_end, high_end = together
        all_due = (index >= low_end) & (index <= high_end)

        @pl.when(all_due)
        def _():
            for _, _, act in parts:
                act(True)

        for first_turn, last_turn, act in parts:
            due = (index >= first_turn) & (index <= last_turn) & jnp.logical_not(all_due)
            pl.when(due)(functools.partial(act, False))

    def by_rows(act, init):
        def at(masked):
            return lambda c, carry: act(pl.multiple_of(c * CHUNK, CHUNK), masked, carry)

        carry = init
        for c in range(chunks):
            carry = act(c * CHUNK, c >= main, carry)
        return carry

    def valid_rows(row, count, length):
        index = lax.broadcasted_iota(jnp.int32, (count, LANES), 0)
        return (index + (base + row)) < length

    def lane_mask(length):
        return (lax.broadcasted_iota(jnp.int32, (8, frames), 1) + base) < length

    def add_sum(row, lanes, value):
        sums[pl.ds(row, 1), pl.ds(lanes, LANES)] += value

    def send_stats(phase, item):
        mine = stats.at[phase, item, tm]
        others("tm", n_tm, tm, lambda peer: remote(
            mine, mine, stat_send.at[phase, item], stat_recv.at[phase, item], "tm", peer).start())

    def wait_stats(phase, item, sem):
        if n_tm > 1:
            block = stats.at[phase, item, pl.ds(0, n_tm - 1)]
            pltpu.make_async_copy(block, block, sem.at[phase, item]).wait()

    def read_stats(phase, item):
        total = stats[phase, item, 0]
        for peer in range(1, n_tm):
            total = total + stats[phase, item, peer]
        total = jnp.sum(total, axis=1, keepdims=True)
        return [total[k : k + 1] for k in range(4)]

    def put_stats(phase, item, rows):
        for k, row in enumerate(rows):
            stats[phase, item, tm, k : k + 1] = row
        for k in range(len(rows), 4):
            stats[phase, item, tm, k : k + 1] = jnp.zeros((1, LANES), F32)

    def halo_copies(kind, place, slot):
        if kind == 0:
            ends, halo = (edges.at[place, 0], edges.at[place, 1]), halo_m
        else:
            ends = (gconv.at[slot, pl.ds(wing, wing)], gconv.at[slot, pl.ds(frames, wing)])
            halo = halo_g
        down = remote(
            ends[0], halo.at[place, 1], halo_send.at[kind, place, 0],
            halo_recv.at[kind, place, 1], "tm", jnp.maximum(tm - 1, 0))
        up = remote(
            ends[1], halo.at[place, 0], halo_send.at[kind, place, 1],
            halo_recv.at[kind, place, 0], "tm", jnp.minimum(tm + 1, n_tm - 1))
        return down, up

    def send_halo(kind, place, slot=None):
        down, up = halo_copies(kind, place, slot)
        pl.when(jnp.logical_not(first))(down.start)
        pl.when(jnp.logical_not(last))(up.start)

    def wait_halo(kind, place, slot=None):
        down, up = halo_copies(kind, place, slot)

        @pl.when(jnp.logical_not(first))
        def _():
            down.wait_send()
            up.wait_recv()

        @pl.when(jnp.logical_not(last))
        def _():
            up.wait_send()
            down.wait_recv()

    def mix(place):
        slot = lax.rem(place, 5)
        item = order[place]
        before = staged[pl.ds(window[place] * GROUP, frames)]
        cat[0:frames] = jnp.where(first, 0.0, before)
        cat[frames:] = s2t[place]
        moved = cat[pl.ds(frames - offs[place], frames), :].T
        moved_s[slot] = moved
        mixed = wide(cols[0], frames) * s1[item] + wide(cols[1], frames) * moved
        mixed = jnp.where(lane_mask(lens[place])[0:1], mixed, 0.0)
        mixed_s[place] = mixed
        for side, row in enumerate((0, frames - wing)):
            near = cat[pl.ds(frames + row - offs[place], wing), :]
            block = 0 if side == 0 else frames - LANES
            turned = s1[item, :, block : block + LANES].T[row - block : row - block + wing]
            ends = gain1[...] * turned + gain2[...] * near
            edges[place, side] = jnp.where(valid_rows(row, wing, lens[place]), ends, 0.0)
        mix_high, mix_low = halves(mixed)
        mcat[slot, 0:chans] = mix_high
        mcat[slot, chans:] = mix_low

    def mix_product(place):
        slot = lax.rem(place, 5)
        left = jnp.concatenate([mcat[slot, 0:chans], mcat[slot]], axis=0)
        pre_raw[...] = dot(left, w_t[...], 0, 0)

    def edge_product(place):
        end_high, end_low = halves(halo_m[place].reshape(2 * wing, chans))
        left = jnp.concatenate([end_high, end_high, end_low], axis=1)
        x = dot(left, w_t[...], 1, 0) + b_in[...]
        half = jnp.tanh(0.5 * x)
        edge_act[...] = jnp.maximum(x, slope1[...] * x) - (1.0 - slope1[...]) * jnp.log(
            0.5 + 0.5 * jnp.abs(half))

    def phase_a(place, merged):
        slot = lax.rem(place, 4)
        length = lens[place]

        def lanes_step(lanes, carry):
            cut = pl.ds(lanes, LANES)
            bias, slope = b_in[:, cut], slope1[:, cut]

            def rows_step(row, masked, carry):
                rows = pl.ds(row, CHUNK)
                x = pre_raw[rows, cut] + bias
                half = jnp.tanh(0.5 * x)
                act = jnp.maximum(x, slope * x) - (1.0 - slope) * jnp.log(
                    0.5 + 0.5 * jnp.abs(half))
                pre1[slot, rows, cut] = x
                a1[slot, pl.ds(row + wing, CHUNK), cut] = act
                if masked:
                    act = jnp.where(valid_rows(row, CHUNK, length), act, 0.0)
                return carry[0] + fold_rows(act), carry[1] + fold_rows(act * act)

            return by_rows(rows_step, carry)

        zero = jnp.zeros((8, LANES), F32)
        carry = by_lanes(lanes_step, (zero, zero), merged)
        put_stats(0, place, [jnp.sum(c, axis=0, keepdims=True) for c in carry])

    def scales(totals, length):
        count = jnp.float32(units) * length.astype(F32)
        mean = totals[0] / count
        inverse = lax.rsqrt(totals[1] / count - mean * mean + EPS)
        return mean, inverse, count

    def before_b(place):
        slot = lax.rem(place, 4)
        length = lens[place]
        mean, inverse, _ = scales(read_stats(0, place), length)
        scale = gamma1[...] * inverse
        shift = beta1[...] - scale * mean
        outside = mean - beta1[...] / scale
        taps = [tap_rows[k : k + 1] for k in range(3)]
        coef[0:1] = taps[0] * scale
        coef[1:2] = taps[1] * scale
        coef[2:3] = taps[2] * scale
        coef[3:4] = b_depth[...] + shift * (taps[0] + taps[1] + taps[2])
        a1[slot, 0:wing] = jnp.where(first, outside, edge_act[0:wing])
        after = (lax.broadcasted_iota(jnp.int32, (wing, units), 0) + (base + frames)) < length
        a1[slot, frames + wing :] = jnp.where(after, edge_act[wing:], outside)


        @pl.when(last)
        def _():
            for row in range(frames - plan.tail, frames, CHUNK):
                keep = wide(valid_rows(row, CHUNK, length).astype(F32), units) > 0.5
                rows = slice(row + wing, row + wing + CHUNK)
                a1[slot, rows] = jnp.where(keep, a1[slot, rows], outside)

    def phase_b(place, merged):
        slot = lax.rem(place, 4)
        pair = lax.rem(place, 2)
        length = lens[place]

        def lanes_step(lanes, carry):
            cut = pl.ds(lanes, LANES)
            slope = slope2[:, cut]
            w0, w1, w2, const = (coef[k : k + 1, cut] for k in range(4))

            def rows_step(row, masked, carry):
                rows = pl.ds(row, CHUNK)
                x = const + w0 * a1[slot, rows, cut]
                x += w1 * a1[slot, pl.ds(row + wing, CHUNK), cut]
                x += w2 * a1[slot, pl.ds(row + 2 * wing, CHUNK), cut]
                half = jnp.tanh(0.5 * x)
                act = jnp.maximum(x, slope * x) - (1.0 - slope) * jnp.log(
                    0.5 + 0.5 * jnp.abs(half))
                conv[pair, rows, cut] = x
                act2[pair, rows, cut] = act
                d2[pair, rows, cut] = (0.5 + 0.5 * slope) + (0.5 - 0.5 * slope) * half
                act_high, act_low = halves(act)
                high[place, rows, cut] = act_high
                low[place, rows, cut] = act_low
                if masked:
                    act = jnp.where(valid_rows(row, CHUNK, length), act, 0.0)
                return carry[0] + fold_rows(act), carry[1] + fold_rows(act * act)

            return by_rows(rows_step, carry)

        zero = jnp.zeros((8, LANES), F32)
        carry = by_lanes(lanes_step, (zero, zero), merged)
        act_sums[0:1] = jnp.sum(carry[0], axis=0, keepdims=True)
        act_sums[1:2] = jnp.sum(carry[1], axis=0, keepdims=True)

    def cotangents(place):
        item = order[place]
        pair = lax.rem(place, 2)
        keep = lane_mask(lens[place])[0:1]
        in_sum = None
        for side, source in enumerate((cr, cs)):
            cot = jnp.where(keep, source[item], 0.0)
            cot_high, cot_low = halves(cot)
            gcat[side * chans : (side + 1) * chans] = cot_high
            gcat[(2 + side) * chans : (3 + side) * chans] = cot_low
            partial = fold_lanes(cot)
            rows = pl.ds(side * chans, chans)
            y_acc[1 + pair, rows] = partial
            gb_acc[rows] += partial
            by_weight = cols[2 + side] * partial
            in_sum = by_weight if in_sum is None else in_sum + by_weight
        act_sums[2:3] = jnp.sum(in_sum, axis=0, keepdims=True)

    def products(place):
        cot_high, cot_low = gcat[0 : 2 * chans], gcat[2 * chans :]
        act_h, act_l = high[place], low[place]
        left = jnp.concatenate([cot_high, cot_high, cot_low], axis=1)
        found = dot(left, jnp.concatenate([act_h, act_l, act_h], axis=0), 1, 0)
        grad_a[...] = found
        cross = jnp.sum(fold_lanes(fold_rows(wg[...] * found)), axis=0, keepdims=True)
        put_stats(1, place, (act_sums[0:1], act_sums[1:2], act_sums[2:3], cross))

    def outputs(place):
        pair = lax.rem(place, 2)
        act_h, act_l = high[place], low[place]
        left = jnp.concatenate([wg_high[...], wg_high[...], wg_low[...]], axis=1)
        raw = dot(left, jnp.concatenate([act_h, act_l, act_h], axis=1), 1, 1)
        keep = lane_mask(lens[place])[0:1]
        inverse, by_mean = out_coef[place, 0:1, 0:1], out_coef[place, 1:2, 0:1]
        out = inverse * raw[0:chans] + wide(cols[4] - by_mean * cols[2], frames)
        out_res[pair] = jnp.where(keep, mixed_s[place] + out, 0.0)
        out = inverse * raw[chans:] + wide(cols[5] - by_mean * cols[3], frames)
        out_skip[pair] = jnp.where(keep, out, 0.0)

    def back_product():
        left = jnp.concatenate([gcat[...], gcat[0 : 2 * chans]], axis=0)
        right = jnp.concatenate([wg_high[...], wg_high[...], wg_low[...]], axis=0)
        e2[...] = dot(left, right, 0, 0)

    def before_c(place):
        length = lens[place]
        totals = read_stats(1, place)
        mean, inverse, count = scales(totals, length)
        sum_e, sum_ea = totals[2], totals[3]
        mean_e = sum_e / count
        mean_ex = inverse * (sum_ea - mean * sum_e) / count
        by_act = -inverse * inverse * mean_ex
        by_one = -inverse * mean_e - by_act * mean
        mean_1, inverse_1, _ = scales(read_stats(0, place), length)
        scale_1 = gamma1[...] * inverse_1
        coef[4:5] = scale_1
        coef[5:6] = beta1[...] - scale_1 * mean_1
        for row, value in ((10, by_act), (11, by_one), (12, inverse), (13, inverse * mean)):
            coef[row : row + 1] = jnp.broadcast_to(value, (1, units))
        out_coef[place, 0:1] = jnp.broadcast_to(inverse, (1, LANES))
        out_coef[place, 1:2] = jnp.broadcast_to(inverse * mean, (1, LANES))

    def phase_c(place, merged):
        slot = lax.rem(place, 4)
        pair = lax.rem(place, 2)
        length = lens[place]
        y_acc[0] += coef[13:14, 0:LANES] * y_acc[1 + pair]
        inverse = coef[12:13, 0:1]
        x_acc[...] += inverse * grad_a[...]
        edge_rows = min(frames, plan.tail + CHUNK)

        def lanes_step(lanes, carry):
            cut = pl.ds(lanes, LANES)
            by_a, by_1, inv_e = (coef[k : k + 1, cut] for k in (10, 11, 12))

            def rows_step(row, masked, carry):
                rows = pl.ds(row, CHUNK)
                middle = pl.ds(row + wing, CHUNK)
                behind = pl.ds(row + 2 * wing, CHUNK)
                act = act2[pair, rows, cut]
                g = inv_e * e2[rows, cut] + by_a * act + by_1
                if masked:
                    g = jnp.where(valid_rows(row, CHUNK, length), g, 0.0)
                gc = g * d2[pair, rows, cut]
                gconv[pair, middle, cut] = gc
                parts = (
                    g * (conv[pair, rows, cut] - act), gc, gc * a1[slot, rows, cut],
                    gc * a1[slot, middle, cut], gc * a1[slot, behind, cut],
                )
                return tuple(c + fold_rows(p) for c, p in zip(carry, parts))

            zero = jnp.zeros((8, LANES), F32)
            found = by_rows(rows_step, (zero,) * 5)
            slope_sum, total, n0, n1, n2 = (jnp.sum(f, axis=0, keepdims=True) for f in found)

            def edge_step(c, carry):
                row = c * CHUNK
                gc = gconv[pair, pl.ds(row + wing, CHUNK), cut]
                inside = valid_rows(row + wing, CHUNK, length)
                return carry + fold_rows(jnp.where(inside, 0.0, gc))

            late = zero
            for c in range((frames - edge_rows) // CHUNK, chunks):
                late = edge_step(c, late)
            late = jnp.sum(late, axis=0, keepdims=True)
            early = jnp.sum(gconv[pair, wing : 2 * wing, cut], axis=0, keepdims=True)
            early = jnp.where(first, early, 0.0)
            scale, shift = coef[4:5, cut], coef[5:6, cut]
            gains, bias = gamma1[:, cut], beta1[:, cut]
            reach = (total - early, total, total - late)
            by_beta = jnp.zeros((1, LANES), F32)
            by_gamma = jnp.zeros((1, LANES), F32)
            for k, (n_k, b_k) in enumerate(zip((n0, n1, n2), reach)):
                tap = tap_rows[k : k + 1, cut]
                n_k = scale * n_k + shift * total
                add_sum(TAP + k, lanes, n_k)
                by_beta += tap * b_k
                by_gamma += tap * (n_k - bias * b_k)
            add_sum(SLOPE_TWO, lanes, slope_sum)
            add_sum(B_DEPTH, lanes, total)
            add_sum(BETA_ONE, lanes, by_beta)
            add_sum(GAMMA_ONE, lanes, by_gamma)
            return carry[0] + gains * by_beta, carry[1] + by_gamma

        zero = jnp.zeros((1, LANES), F32)
        put_stats(2, place, by_lanes(lanes_step, (zero, zero), merged))

    def out_copies(item):
        pair = lax.rem(item, 2)
        return (
            pltpu.make_async_copy(out_res.at[pair], res_h.at[item], out_sem.at[0, item]),
            pltpu.make_async_copy(out_skip.at[pair], skip_h.at[item], out_sem.at[1, item]),
        )

    def gs1_copy(item):
        return pltpu.make_async_copy(
            out_gs1.at[lax.rem(item, 2)], gs1_h.at[item], out_sem.at[2, item])

    def gmoved_copy(item):
        return pltpu.make_async_copy(
            gbuf.at[pl.ds(item * frames, frames)], gmoved_h.at[item], out_sem.at[3, item])

    def before_d(place):
        pair = lax.rem(place, 2)
        length = lens[place]
        totals = read_stats(2, place)
        mean, inverse, count = scales(read_stats(0, place), length)
        mean_e, mean_ex = totals[0] / count, totals[1] / count
        by_act = -inverse * inverse * mean_ex
        by_one = -inverse * mean_e - by_act * mean
        for k in range(3):
            coef[6 + k : 7 + k] = tap_rows[k : k + 1] * gamma1[...] * inverse
        for row, value in ((14, by_act), (15, by_one)):
            coef[row : row + 1] = jnp.broadcast_to(value, (1, units))
        gconv[pair, 0:wing] = jnp.where(first, 0.0, halo_g[place, 0])
        gconv[pair, frames + wing :] = jnp.where(last, 0.0, halo_g[place, 1])

    def phase_d(place, merged):
        slot = lax.rem(place, 4)
        pair = lax.rem(place, 2)
        length = lens[place]

        def lanes_step(lanes, carry):
            cut = pl.ds(lanes, LANES)
            slope = slope1[:, cut]
            by_a, by_1 = coef[14:15, cut], coef[15:16, cut]
            u0, u1, u2 = (coef[6 + k : 7 + k, cut] for k in range(3))

            def rows_step(row, masked, carry):
                rows = pl.ds(row, CHUNK)
                middle = pl.ds(row + wing, CHUNK)
                behind = pl.ds(row + 2 * wing, CHUNK)
                act, x = a1[slot, middle, cut], pre1[slot, rows, cut]
                g = by_a * act + by_1 + u0 * gconv[pair, behind, cut]
                g += u1 * gconv[pair, middle, cut] + u2 * gconv[pair, rows, cut]
                if masked:
                    g = jnp.where(valid_rows(row, CHUNK, length), g, 0.0)
                half = jnp.tanh(0.5 * x)
                gp = g * ((0.5 + 0.5 * slope) + (0.5 - 0.5 * slope) * half)
                gp_h, gp_l = halves(gp)
                gp_high[rows, cut] = gp_h
                gp_low[rows, cut] = gp_l
                return carry[0] + fold_rows(g * (x - act)), carry[1] + fold_rows(gp)

            zero = jnp.zeros((8, LANES), F32)
            slope_sum, bias_sum = by_rows(rows_step, (zero, zero))
            add_sum(SLOPE_ONE, lanes, jnp.sum(slope_sum, axis=0, keepdims=True))
            add_sum(B_IN, lanes, jnp.sum(bias_sum, axis=0, keepdims=True))
            return carry

        by_lanes(lanes_step, 0, merged)

    def weight_product(place):
        slot = lax.rem(place, 5)
        g_h, g_l = gp_high[...], gp_low[...]
        gw_acc[...] += dot(mcat[slot], g_h, 1, 0)
        gw_acc[0:chans] += dot(mcat[slot, 0:chans], g_l, 1, 0)

    def mixture_gradient(place):
        slot = lax.rem(place, 5)
        pair = lax.rem(place, 2)
        item = order[place]
        both = dot(w_t[0 : 2 * chans], gp_high[...], 1, 1)
        g_mixed = both[0:chans] + both[chans:] + dot(w_t[0:chans], gp_low[...], 1, 1)
        g_mixed = jnp.where(lane_mask(lens[place])[0:1], cr[item] + g_mixed, 0.0)
        out_gs1[pair] = wide(cols[0], frames) * g_mixed
        gain_acc[0] += fold_lanes(g_mixed * s1[item])
        gain_acc[1] += fold_lanes(g_mixed * moved_s[slot])
        gbuf[pl.ds(pl.multiple_of(place * frames, 8), frames)] = (
            wide(cols[1], frames) * g_mixed).T

    big, small_part = plan.seg // n_it, plan.seg // n_it // n_tm

    def segment(seg):
        return seg * plan.seg, big, small_part

    def stage_copies(seg, stage):
        start, big, small = segment(seg)
        offset = start // n_it
        send, recv = ar_send.at[seg, stage], ar_recv.at[seg, stage]
        if stage == 0:
            return "items", n_it, it, lambda peer: remote(
                gall.at[pl.ds(start + peer * big, big)], rs_it.at[it, pl.ds(offset, big)],
                send, recv, "items", peer)
        if stage == 1:
            return "tm", n_tm, tm, lambda peer: remote(
                part.at[pl.ds(offset + peer * small, small)],
                rs_tm.at[tm, pl.ds(offset // n_tm, small)], send, recv, "tm", peer)
        if stage == 2:
            mine = quarter.at[pl.ds(offset + tm * small, small)]
            return "tm", n_tm, tm, lambda peer: remote(mine, mine, send, recv, "tm", peer)
        mine = done.at[pl.ds(start + it * big, big)]
        return "items", n_it, it, lambda peer: remote(mine, mine, send, recv, "items", peer)

    def stage_start(seg, stage):
        axis, count, mine, copy = stage_copies(seg, stage)
        others(axis, count, mine, lambda peer: copy(peer).start())

    def stage_wait(seg, stage, sem):
        start, big, small = segment(seg)
        count, rows = ((n_it, big), (n_tm, small), (n_tm, small), (n_it, big))[stage]
        if count > 1:
            block = gall.at[pl.ds(0, (count - 1) * rows)]
            pltpu.make_async_copy(block, block, sem.at[seg, stage]).wait()

    def added(ref, count, rows):
        total = ref[0, rows]
        for peer in range(1, count):
            total = total + ref[peer, rows]
        return total

    def stage_zero(seg):
        start, big, _ = segment(seg)
        rs_it[it, pl.ds(start // n_it, big)] = gall[pl.ds(start + it * big, big)]
        stage_start(seg, 0)

    def stage_one(seg):
        start, big, small = segment(seg)
        offset = start // n_it
        stage_wait(seg, 0, ar_recv)
        part[pl.ds(offset, big)] = added(rs_it, n_it, pl.ds(offset, big))
        rs_tm[tm, pl.ds(offset // n_tm, small)] = part[pl.ds(offset + tm * small, small)]
        stage_start(seg, 1)

    def stage_two(seg):
        start, big, small = segment(seg)
        offset = start // n_it
        stage_wait(seg, 1, ar_recv)
        quarter[pl.ds(offset + tm * small, small)] = added(
            rs_tm, n_tm, pl.ds(offset // n_tm, small))
        stage_start(seg, 2)

    def stage_three(seg):
        start, big, _ = segment(seg)
        offset = start // n_it
        stage_wait(seg, 2, ar_recv)
        done[pl.ds(start + it * big, big)] = quarter[pl.ds(offset, big)]
        stage_start(seg, 3)

    def weights_sum():
        for side, weight in enumerate((w_res, w_skip)):
            rows = slice(side * chans, (side + 1) * chans)
            ones = jnp.sum(gb_acc[rows], axis=1, keepdims=True)
            centred = x_acc[rows] - jnp.sum(y_acc[0, rows], axis=1, keepdims=True)
            grad = gamma2[...] * centred + beta2[...] * ones
            for b in range(blocks):
                gall[b * 2 * chans + side * chans : b * 2 * chans + (side + 1) * chans] = grad[
                    :, b * LANES : (b + 1) * LANES]
            sums[GAMMA_TWO : GAMMA_TWO + 1] += jnp.sum(
                weight[...] * centred, axis=0, keepdims=True)
            sums[BETA_TWO : BETA_TWO + 1] += jnp.sum(weight[...] * ones, axis=0, keepdims=True)
            sums[NARROW : NARROW + 1, (2 + side) * LANES : (3 + side) * LANES] = jnp.sum(
                gb_acc[rows].T, axis=0, keepdims=True)

    def input_weights_sum():
        start = plan.in_start
        grad = gw_acc[0:chans] + gw_acc[chans:]
        for b in range(blocks):
            gall[start + b * chans : start + (b + 1) * chans] = grad[
                :, b * LANES : (b + 1) * LANES]

    def narrow_sums():
        for side in range(2):
            sums[NARROW : NARROW + 1, side * LANES : (side + 1) * LANES] = jnp.sum(
                gain_acc[side].T, axis=0, keepdims=True)
        sums[SLOPE_ONE : SLOPE_ONE + 1] = sums[SLOPE_ONE : SLOPE_ONE + 1] / (1.0 - slope1[...])
        sums[SLOPE_TWO : SLOPE_TWO + 1] = sums[SLOPE_TWO : SLOPE_TWO + 1] / (1.0 - slope2[...])
        sums[GAMMA_ONE : GAMMA_ONE + 1] = sums[GAMMA_ONE : GAMMA_ONE + 1] / gamma1[...]
        for b in range(blocks):
            small[b * SUM_ROWS : (b + 1) * SUM_ROWS] = sums[:, b * LANES : (b + 1) * LANES]
        small_it[it] = small[...]

    narrow = plan.small // n_tm

    def small_copies(stage):
        send, recv = ar_send.at[plan.segs, stage], ar_recv.at[plan.segs, stage]
        if stage == 0:
            return "items", n_it, it, lambda peer: remote(
                small, small_it.at[it], send, recv, "items", peer)
        if stage == 1:
            return "tm", n_tm, tm, lambda peer: remote(
                small.at[pl.ds(peer * narrow, narrow)], small_tm.at[tm], send, recv, "tm", peer)
        mine = small_done.at[pl.ds(tm * narrow, narrow)]
        return "tm", n_tm, tm, lambda peer: remote(mine, mine, send, recv, "tm", peer)

    def small_start(stage):
        axis, count, mine, copy = small_copies(stage)
        others(axis, count, mine, lambda peer: copy(peer).start())

    def small_wait(stage, sem):
        count, rows = ((n_it, plan.small), (n_tm, narrow), (n_tm, narrow))[stage]
        if count > 1:
            block = gall.at[pl.ds(0, (count - 1) * rows)]
            pltpu.make_async_copy(block, block, sem.at[plan.segs, stage]).wait()

    def small_one():
        small_wait(0, ar_recv)
        small_wait(0, ar_send)
        total = small_it[0]
        for peer in range(1, n_it):
            total = total + small_it[peer]
        small[...] = total
        small_tm[tm] = small[pl.ds(tm * narrow, narrow)]
        small_start(1)

    def small_two():
        small_wait(1, ar_recv)
        total = small_tm[0]
        for peer in range(1, n_tm):
            total = total + small_tm[peer]
        small_done[pl.ds(tm * narrow, narrow)] = total
        small_start(2)

    load(0).wait()
    load(1).wait()
    arrived(0)
    mix(0)
    send_halo(0, 0)
    mix_product(0)
    load(2).wait()
    load(3).wait()
    end = items - 1

    def step(index, carry):
        def within(lag, back=0):
            return (index >= lag) & (index <= end + lag - back)

        pl.when(within(6))(lambda: gs1_copy(index - 6).wait())
        pl.when(within(1))(lambda: wait_halo(0, index - 1))
        side_by_side(index, (4, end), (
            (1, end + 1, lambda merged: edge_product(index - 1)),
            (0, end, lambda merged: phase_a(index, merged)),
            (4, end + 3, lambda merged: weight_product(index - 4)),
            (4, end + 3, lambda merged: mixture_gradient(index - 4)),
        ))

        @pl.when(within(0))
        def _():
            send_stats(0, index)

        @pl.when(index == end + 4)
        def _():
            weight_product(index - 4)
            input_weights_sum()
            for seg in range(plan.weight_segs, plan.segs):
                stage_zero(seg)
            mixture_gradient(index - 4)
            stage_one(0)

        @pl.when(within(4))
        def _():
            gs1_copy(index - 4).start()
            gmoved_copy(index - 4).start()

        bulk(index, 0)

        @pl.when(within(1))
        def _():
            wait_stats(0, index - 1, stat_recv)
            before_b(index - 1)

        side_by_side(index, (2, end + 1), (
            (1, end + 1, lambda merged: phase_b(index - 1, merged)),
            (2, end + 2, lambda merged: back_product()),
        ))

        @pl.when(within(2))
        def _():
            wait_stats(1, index - 2, stat_recv)
            before_c(index - 2)

        pl.when(within(1))(lambda: cotangents(index - 1))
        side_by_side(index, (2, end + 1), (
            (2, end + 2, lambda merged: phase_c(index - 2, merged)),
            (1, end + 1, lambda merged: products(index - 1)),
        ))

        @pl.when(within(1))
        def _():
            send_stats(1, index - 1)

        @pl.when(within(2))
        def _():
            send_stats(2, index - 2)
            send_halo(1, index - 2, lax.rem(index, 2))

        @pl.when(index == end + 2)
        def _():
            weights_sum()
            for seg in range(plan.weight_segs):
                stage_zero(seg)

        bulk(index, 1)

        @pl.when(within(3))
        def _():
            wait_halo(1, index - 3, lax.rem(index + 1, 2))
            wait_stats(2, index - 3, stat_recv)
            before_d(index - 3)

        @pl.when(index < end)
        def _():
            arrived(index + 1)
            mix(index + 1)
            send_halo(0, index + 1)

        side_by_side(index, (3, end - 1), (
            (3, end + 3, lambda merged: phase_d(index - 3, merged)),
            (0, end - 1, lambda merged: mix_product(index + 1)),
        ))
        return carry

    lax.fori_loop(0, items + 4, step, 0)
    narrow_sums()
    small_start(0)

    def stages(acts):
        for act, *given in acts:
            act(*given)

    one, two, three = stage_one, stage_two, stage_three
    if items == 8 and plan.segs == 6:
        due = (
            ((one, 1),), ((one, 2),), ((one, 3),), ((two, 0),), ((one, 4), (two, 1)),
            ((one, 5),), ((two, 2), (small_one,)), ((two, 3),),
        )
        late = (
            (three, 0), (three, 1), (two, 4), (three, 2), (two, 5), (three, 3), (small_two,),
            (three, 4), (three, 5),
        )
    else:
        due = ((),) * items
        late = [(one, seg) for seg in range(1, plan.segs)] + [(small_one,)]
        late += [(two, seg) for seg in range(plan.segs)] + [(small_two,)]
        late += [(three, seg) for seg in range(plan.segs)]

    def turn(place, carry):
        @pl.when(place >= 2)
        def _():
            for copy in out_copies(place - 2):
                copy.wait()

        outputs(place)
        for copy in out_copies(place):
            copy.start()
        for k, acts in enumerate(due):
            if acts:
                pl.when(place == k)(functools.partial(stages, acts))
        start = sum(map(sum, plan.back.values()))
        each = (plan.parts - start) // items
        if each:
            send_back(start + place * each, start + place * each + each)
        return carry

    for place in range(max(0, items - 2), items):
        gs1_copy(place).wait()
    lax.fori_loop(0, items, turn, 0)
    stages(late)
    for seg in range(plan.segs):
        stage_wait(seg, 3, ar_recv)
    small_wait(2, ar_recv)
    total_copy = pltpu.make_async_copy(done, total_h, in_sem.at[0])
    total_copy.start()
    small_copy = pltpu.make_async_copy(small_done, small_h, in_sem.at[1])
    small_copy.start()

    def finish(item, carry):
        for phase in range(3):
            wait_stats(phase, item, stat_send)
        gmoved_copy(item).wait()
        return carry

    def finish_chunk(chunk, carry):
        @pl.when(jnp.logical_not(first))
        def _():
            to_previous(chunk).wait_send()

        @pl.when(jnp.logical_not(last))
        def _():
            to_next(chunk).wait_send()
            to_previous(chunk).wait_recv()

        return carry

    lax.fori_loop(0, items, finish, 0)
    lax.fori_loop(0, plan.parts, finish_chunk, 0)
    for item in range(max(0, items - 2), items):
        for copy in out_copies(item):
            copy.wait()
    for seg in range(plan.segs):
        for stage in range(4):
            stage_wait(seg, stage, ar_send)
    small_wait(1, ar_send)
    small_wait(2, ar_send)
    total_copy.wait()
    small_copy.wait()


def prelude(plan):
    items, frames, chans = plan.items, plan.frames, plan.chans
    rows = items * frames
    groups = rows // GROUP
    table = (rounded(groups, LANES) // LANES, LANES)
    per_item = frames // GROUP

    def body(
        offs_in, lens_in, s2_h, s2t_h, packed_h, pack, order, offs, lens, window, window_back,
        which, s2, s2t, packed, lookup_v, lookup, held, in_sem, out_sem, table_sem, send, recv,
    ):
        n_it = plan.n_it
        it = lax.axis_index("items")
        load = pltpu.make_async_copy(s2_h, s2, in_sem)
        load.start()
        barrier = pltpu.get_barrier_semaphore()

        def peers(act):
            def turn(step, carry):
                act(lax.rem(it + step, n_it))
                return carry

            lax.fori_loop(1, n_it, turn, 0)

        def copy(peer):
            return pltpu.make_async_remote_copy(
                src_ref=held.at[it], dst_ref=held.at[it], send_sem=send, recv_sem=recv,
                device_id={"items": peer}, device_id_type=MESH)

        peers(lambda peer: pl.semaphore_signal(
            barrier, inc=1, device_id={"items": peer}, device_id_type=MESH))
        given = [offs_in[i] for i in range(items)]
        places = []
        for i in range(items):
            rank = jnp.int32(0)
            for j in range(items):
                if j != i:
                    before = given[j] <= given[i] if j < i else given[j] < given[i]
                    rank += jnp.where(before, 1, 0)
            places.append(jnp.where(rank % 2 == 0, rank // 2, items - 1 - rank // 2))
        starts, needs, end = [], [], jnp.int32(0)
        taken = []
        for k in range(items):
            here = [jnp.where(place == k, 1, 0) for place in places]
            item = sum(i * h for i, h in enumerate(here))
            offset = sum(given[i] * h for i, h in enumerate(here))
            taken.append(item)
            order[k] = item
            offs[k] = offset
            lens[k] = sum(lens_in[i] * h for i, h in enumerate(here))
            needs.append((offset + GROUP - 1) // GROUP)
            starts.append(end)
            end = end + needs[k]
            window[k] = end
        held[it] = jnp.full((1, LANES), end, jnp.int32)
        pl.semaphore_wait(barrier, n_it - 1)
        peers(lambda peer: copy(peer).start())

        index = (
            lax.broadcasted_iota(jnp.int32, table, 0) * LANES
            + lax.broadcasted_iota(jnp.int32, table, 1))

        def looked_up(index, firsts):
            total, previous = index, jnp.int32(0)
            for k in range(items):
                shift = firsts[k] - starts[k]
                total = total + jnp.where(index >= starts[k], shift - previous, 0)
                previous = shift
            return jnp.minimum(total, groups - 1)

        lookup_v[...] = looked_up(
            index, [(k + 1) * per_item - needs[k] for k in range(items)])
        to_smem = pltpu.make_async_copy(lookup_v, lookup, table_sem)
        to_smem.start()
        load.wait()
        for k in range(items):
            s2t[k * frames : (k + 1) * frames] = s2[taken[k]].T
        to_smem.wait()
        own_out = pltpu.make_async_copy(s2t, s2t_h, out_sem.at[0])
        own_out.start()

        def turn(group, carry):
            source = lookup[group // LANES, group % LANES] * GROUP
            packed[pl.ds(pl.multiple_of(group * GROUP, GROUP), GROUP)] = s2t[
                pl.ds(source, GROUP)]
            return carry

        lax.fori_loop(0, groups, turn, 0, unroll=16)
        packed_out = pltpu.make_async_copy(packed, packed_h, out_sem.at[1])
        packed_out.start()

        if n_it > 1:
            block = held.at[pl.ds(0, n_it - 1)]
            pltpu.make_async_copy(block, block, recv).wait()
        most = held[0]
        for peer in range(1, n_it):
            most = jnp.maximum(most, held[peer])
        choice = jnp.zeros((1, LANES), jnp.int32)
        sent = jnp.full((1, LANES), plan.caps[0] // GROUP, jnp.int32)
        for low_cap, cap in zip(plan.caps[:-1], plan.caps[1:]):
            more = most * GROUP > low_cap
            choice += more.astype(jnp.int32)
            sent += jnp.where(more, (cap - low_cap) // GROUP, 0)
        which[0] = jnp.max(choice)
        base = jnp.max(sent) - end
        for k in range(items):
            window_back[k] = base + starts[k]
        back = looked_up(index - base, [jnp.int32(k * per_item) for k in range(items)])
        pack[...] = jnp.where(index < base, 0, back)
        own_out.wait()
        packed_out.wait()
        if n_it > 1:
            pltpu.make_async_copy(block, block, send).wait()

    smem = pl.BlockSpec(memory_space=pltpu.SMEM)
    hbm = pl.BlockSpec(memory_space=pl.ANY)
    short = jax.ShapeDtypeStruct((items,), jnp.int32)
    flat = jax.ShapeDtypeStruct((rows, chans), F32)
    sem = pltpu.SemaphoreType.DMA
    return pl.pallas_call(
        body,
        out_shape=(
            flat, flat, jax.ShapeDtypeStruct(table, jnp.int32), short, short, short, short, short,
            jax.ShapeDtypeStruct((1,), jnp.int32),
        ),
        in_specs=[smem, smem, hbm],
        out_specs=(hbm, hbm, pl.BlockSpec(memory_space=pltpu.VMEM)) + (smem,) * 6,
        scratch_shapes=[
            pltpu.VMEM((items, chans, frames), F32), pltpu.VMEM((rows, chans), F32),
            pltpu.VMEM((rows, chans), F32), pltpu.VMEM(table, jnp.int32),
            pltpu.SMEM(table, jnp.int32), pltpu.VMEM((plan.n_it, 1, LANES), jnp.int32),
            sem, sem((2,)), sem, sem, sem,
        ],
        compiler_params=pltpu.CompilerParams(
            collective_id=0, has_side_effects=True, vmem_limit_bytes=62 * 2**20),
        name="prelude",
    )


def finisher(plan, rows):
    items, frames, chans, units = plan.items, plan.frames, plan.chans, plan.units
    blocks = units // LANES

    def body(
        order, offs, window, gmoved_h, from_right_h, total_h, small_h, res_h, skip_h, gs1_h, *rest
    ):
        outs, scratch = rest[:20], rest[20:]
        cat, gs2, total, small, passed, in_sem, out_sem, pass_sem, total_sem = scratch
        out_res, out_skip, out_gs1, out_gs2 = outs[:4]
        last = lax.axis_index("tm") == plan.n_tm - 1
        def through(kind, item):
            src, dst = ((res_h, out_res), (skip_h, out_skip), (gs1_h, out_gs1))[kind]
            held = passed.at[kind, item]
            return (
                pltpu.make_async_copy(src.at[item], held, pass_sem.at[0, kind, item]),
                pltpu.make_async_copy(held, dst.at[order[item]], pass_sem.at[1, kind, item]),
            )

        def loads(item):
            start = pl.multiple_of(window[item] * GROUP, GROUP)
            return (
                pltpu.make_async_copy(
                    gmoved_h.at[item], cat.at[item, pl.ds(0, frames)], in_sem.at[0, item]),
                pltpu.make_async_copy(
                    from_right_h.at[pl.ds(start, frames)], cat.at[item, pl.ds(frames, frames)],
                    in_sem.at[1, item]),
            )

        def store(item):
            return pltpu.make_async_copy(gs2.at[item], out_gs2.at[order[item]], out_sem.at[item])

        def start(item, carry):
            for copy in loads(item):
                copy.start()
            for kind in range(3):
                through(kind, item)[0].start()
            return carry

        total_copy = pltpu.make_async_copy(total_h, total, total_sem.at[0])
        total_copy.start()
        small_copy = pltpu.make_async_copy(small_h, small, total_sem.at[1])
        small_copy.start()
        lax.fori_loop(0, items, start, 0)

        def turn(item, carry):
            for copy in loads(item):
                copy.wait()
            for kind in range(3):
                arriving, leaving = through(kind, item)
                arriving.wait()
                leaving.start()

            @pl.when(last)
            def _():
                cat[item, frames:] = jnp.zeros((frames, chans), F32)

            gs2[item] = cat[item, pl.ds(offs[item], frames), :].T
            store(item).start()
            return carry

        lax.fori_loop(0, items, turn, 0)
        total_copy.wait()
        small_copy.wait()
        (
            gain_1, gain_2, g_in, gb_in, g_slope1, g_gamma1, g_beta1, g_taps, gb_depth, g_slope2,
            g_gamma2, g_beta2, g_res, gb_res, g_skip, gb_skip,
        ) = outs[4:]
        start_in = plan.in_start
        for b in range(blocks):
            cut = slice(b * LANES, (b + 1) * LANES)
            g_res[:, cut] = total[2 * b * chans : (2 * b + 1) * chans]
            g_skip[:, cut] = total[(2 * b + 1) * chans : (2 * b + 2) * chans]
            g_in[cut] = total[start_in + b * chans : start_in + (b + 1) * chans].T
            sums = small[b * SUM_ROWS : (b + 1) * SUM_ROWS]
            for out, row in (
                (gb_in, B_IN), (g_slope1, SLOPE_ONE), (g_gamma1, GAMMA_ONE), (g_beta1, BETA_ONE),
                (gb_depth, B_DEPTH), (g_slope2, SLOPE_TWO), (g_gamma2, GAMMA_TWO),
                (g_beta2, BETA_TWO),
            ):
                out[:, cut] = sums[row : row + 1]
            g_taps[:, cut] = sums[TAP : TAP + 3]
            (gain_1, gain_2, gb_res, gb_skip)[b][...] = sums[NARROW : NARROW + 1]

        def end(item, carry):
            store(item).wait()
            for kind in range(3):
                through(kind, item)[1].wait()
            return carry

        lax.fori_loop(0, items, end, 0)

    smem = pl.BlockSpec(memory_space=pltpu.SMEM)
    hbm = pl.BlockSpec(memory_space=pl.ANY)
    vmem = pl.BlockSpec(memory_space=pltpu.VMEM)
    big = jax.ShapeDtypeStruct((items, chans, frames), F32)

    def array(*shape):
        return jax.ShapeDtypeStruct(shape, F32)

    narrow, per_unit = array(1, chans), array(1, units)
    sem = pltpu.SemaphoreType.DMA
    return pl.pallas_call(
        body,
        out_shape=(big,) * 4 + (
            narrow, narrow, array(units, chans), per_unit, per_unit, per_unit, per_unit,
            array(3, units), per_unit, per_unit, per_unit, per_unit, array(chans, units), narrow,
            array(chans, units), narrow,
        ),
        in_specs=[smem] * 3 + [hbm] * 7,
        out_specs=(hbm,) * 4 + (vmem,) * 16,
        scratch_shapes=[
            pltpu.VMEM((items, 2 * frames, chans), F32), pltpu.VMEM((items, chans, frames), F32),
            pltpu.VMEM((rows, LANES), F32), pltpu.VMEM((plan.small, LANES), F32),
            pltpu.VMEM((3, items, chans, frames), F32),
            sem((2, items)), sem((items,)), sem((2, 3, items)), sem((2,)),
        ],
        compiler_params=pltpu.CompilerParams(vmem_limit_bytes=62 * 2**20),
        name="finisher",
    )


def per_device(
    mesh, source_one, source_two, offsets, lengths, gain_one, gain_two, w_in, b_in, slope_one,
    first_norm_gain, first_norm_bias, depthwise_weight, depthwise_bias, slope_two,
    second_norm_gain, second_norm_bias, w_res, b_res, w_skip, b_skip, cot_res, cot_skip,
):
    items, chans, frames = source_one.shape
    units = w_in.shape[0]
    plan = Plan(mesh, items, chans, frames, units)
    n_tm, n_it, wing = plan.n_tm, plan.n_it, DILATION_RATE
    full = items * frames
    s2t, packed, pack, order, offs, lens, window, window_back, which = prelude(plan)(
        offsets, lengths, source_two)

    def row(value):
        return value.reshape(1, -1)

    smem = pl.BlockSpec(memory_space=pltpu.SMEM)
    hbm = pl.BlockSpec(memory_space=pl.ANY)
    vmem = pl.BlockSpec(memory_space=pltpu.VMEM)
    rows = plan.segs * plan.seg

    def floats(*shape):
        return pltpu.VMEM(shape, F32)

    def shorts(*shape):
        return pltpu.VMEM(shape, BF16)

    big = jax.ShapeDtypeStruct((items, chans, frames), F32)
    sem = pltpu.SemaphoreType.DMA
    def block(sent, index):
        return pl.pallas_call(
            functools.partial(kernel, plan, sent),
            out_shape=(
                big, big, big, jax.ShapeDtypeStruct((items, frames, chans), F32),
                jax.ShapeDtypeStruct((full + frames, chans), F32),
                jax.ShapeDtypeStruct((rows, LANES), F32),
                jax.ShapeDtypeStruct((plan.small, LANES), F32),
            ),
            in_specs=[smem] * 5 + [hbm] * 5 + [vmem] * 16,
            out_specs=[hbm] * 7,
            scratch_shapes=[
                floats(items, chans, frames), floats(items, frames, chans),
                floats(items, chans, frames), floats(items, chans, frames),
                floats(sent, chans), floats(frames + sent, chans), floats(full, chans),
                floats(sent, chans),
                floats(2, chans, frames), floats(2, chans, frames), floats(2 * frames, chans),
                floats(5, chans, frames), floats(items, chans, frames),
                shorts(5, 2 * chans, frames),
                floats(frames, units), floats(4, frames + 2 * wing, units),
                floats(4, frames, units),
                floats(2, frames, units), floats(2, frames, units), floats(2, frames, units),
                floats(frames, units), shorts(items, frames, units),
                shorts(items, frames, units), floats(2 * chans, units),
                floats(2, frames + 2 * wing, units), shorts(frames, units),
                shorts(frames, units), shorts(4 * chans, frames),
                floats(items, 2, wing, chans), floats(items, 2, wing, chans),
                floats(2 * wing, units), floats(items, 2, wing, units),
                floats(3, items, n_tm, 4, LANES), floats(8, LANES), floats(16, units),
                floats(items, 2, LANES),
                shorts(3 * chans, units), shorts(2 * chans, units), shorts(2 * chans, units),
                floats(2 * chans, units), floats(6, chans, LANES),
                floats(2 * chans, units), floats(2 * chans, units),
                floats(2 * chans, LANES), floats(3, 2 * chans, LANES), floats(2, chans, LANES),
                floats(SUM_ROWS, units),
                floats(rows, LANES), floats(n_it, rows // n_it, LANES),
                floats(rows // n_it, LANES),
                floats(n_tm, rows // n_it // n_tm, LANES), floats(rows // n_it, LANES),
                floats(rows, LANES),
                floats(plan.small, LANES), floats(n_it, plan.small, LANES),
                floats(n_tm, plan.small // n_tm, LANES), floats(plan.small, LANES),
                sem((4,)), sem((4, items)), sem((plan.parts,)), sem((plan.parts,)),
                sem((plan.parts,)), sem((plan.parts,)), sem((2, items, 2)), sem((2, items, 2)),
                sem((3, items)), sem((3, items)), sem((plan.segs + 1, 4)),
                sem((plan.segs + 1, 4)),
            ],
            compiler_params=pltpu.CompilerParams(
                collective_id=1 + index, has_side_effects=True,
                vmem_limit_bytes=63 * 2**20),
            name="tcn_block",
        )

    branches = [block(sent, index) for index, sent in enumerate(plan.caps)]
    res, skip, gs1, gmoved, from_right, total, narrow = lax.switch(
        which[0], branches,
        order, offs, lens, window, pack, source_one, s2t.reshape(items, frames, chans), packed,
        cot_res, cot_skip,
        row(gain_one), row(gain_two), w_in, row(b_in), row(slope_one), row(first_norm_gain),
        row(first_norm_bias), depthwise_weight.T, row(depthwise_bias), row(slope_two),
        row(second_norm_gain), row(second_norm_bias), w_res, row(b_res), w_skip, row(b_skip),
    )
    outs = list(finisher(plan, rows)(
        order, offs, window_back, gmoved, from_right, total, narrow, res, skip, gs1))
    outs[11] = outs[11].T
    return tuple(out.reshape(-1) if out.shape[0] == 1 else out for out in outs)


def solution(mesh):
    split = P("items", None, "tm")
    in_specs = (split, split, P("items"), P("items")) + (P(),) * 16 + (split, split)
    out_specs = (split,) * 4 + (P(),) * 16
    return jax.shard_map(
        functools.partial(per_device, mesh), mesh=mesh, in_specs=in_specs, out_specs=out_specs,
        check_vma=False,
    )
```

```python
import functools

import jax
import jax.numpy as jnp
from jax import lax
from jax.experimental import pallas as pl
from jax.experimental.pallas import tpu as pltpu
from jax.sharding import PartitionSpec as P

DILATION_RATE = 16
EPS = 1e-05
LANES = 128
F32 = jnp.float32
BF16 = jnp.bfloat16
MESH = pl.DeviceIdType.MESH
CHUNK = 64
GROUP = 16

B_IN, SLOPE_ONE, GAMMA_ONE, BETA_ONE, TAP, B_DEPTH, SLOPE_TWO, GAMMA_TWO, BETA_TWO, NARROW = (
    0, 1, 2, 3, 4, 7, 8, 9, 10, 11,
)
SUM_ROWS = 16


def halves(value):
    high = value.astype(BF16)
    return high, (value - high.astype(F32)).astype(BF16)


def dot(left, right, over_left, over_right):
    return lax.dot_general(
        left, right, (((over_left,), (over_right,)), ((), ())), preferred_element_type=F32
    )


def fold_rows(value):
    return jnp.sum(value.reshape(value.shape[0] // 8, 8, value.shape[1]), axis=0)


def fold_lanes(value):
    total = value[:, :LANES]
    for start in range(LANES, value.shape[1], LANES):
        total = total + value[:, start : start + LANES]
    return total


def column(row):
    return jnp.broadcast_to(row, (LANES, LANES)).T


def wide(tile, width):
    return jnp.concatenate([tile] * (width // LANES), axis=1)


def rounded(size, step):
    return -(-size // step) * step


class Plan:
    def __init__(self, mesh, items, chans, frames, units):
        self.n_tm = mesh.shape["tm"]
        self.n_it = mesh.shape["items"]
        self.items, self.chans, self.frames, self.units = items, chans, frames, units
        whole = frames * self.n_tm
        self.tail = min(frames, rounded(whole // 32, CHUNK))
        step = 8 * self.n_tm * self.n_it
        self.seg = step
        weight_rows, rows = 2 * chans * units // LANES, chans * units // LANES
        if step >= weight_rows + rows:
            self.weight_segs, self.segs, self.in_start = 0, 1, weight_rows
        else:
            self.weight_segs = -(-weight_rows // step)
            self.segs = self.weight_segs + -(-rows // step)
            self.in_start = self.weight_segs * step
        self.small = rounded(SUM_ROWS * units // LANES, 8 * self.n_tm)
        full = items * frames
        self.parts = 32
        self.caps = tuple(sorted({
            rounded(full * part // 16, GROUP * self.parts) for part in (9, 10, 11, 12, 16)}))
        if items == 8 and self.caps[0] >= 4 * frames:
            self.arrive = (4, 8, 12, 16, 24, 32, 32, 32)
            self.out = (
                12, ((1, 1, 1, 1), (1, 1, 1, 1), (2, 1, 1, 1), (2, 1, 2, 2)))
            self.back = {
                6: (1, 1, 1, 1), 7: (1, 1, 1, 1), 8: (1, 1, 1, 1), 9: (1, 1, 1, 1),
                10: (4, 4, 0, 0)}
        else:
            self.arrive = (self.parts,) * items
            self.out = (self.parts, ())
            self.back = {items + 3: (self.parts, 0, 0, 0)}


def kernel(plan, rows_sent, *refs):
    n_tm, n_it = plan.n_tm, plan.n_it
    items, chans, frames, units = plan.items, plan.chans, plan.frames, plan.units
    wing = DILATION_RATE
    blocks = units // LANES
    (
        order, offs, lens, window, pack, s1_h, s2t_h, packed_h, cr_h, cs_h,
        gain1, gain2, w_in, b_in, slope1, gamma1, beta1, tap_rows, b_depth, slope2, gamma2, beta2,
        w_res, b_res, w_skip, b_skip,
        res_h, skip_h, gs1_h, gmoved_h, from_right_h, total_h, small_h,
        s1, s2t, cr, cs, from_left, staged, gbuf, gpack, out_skip, out_gs1, cat,
        moved_s, mixed_s, mcat, pre_raw, a1, pre1, conv, act2, d2, e2, high, low, grad_a,
        gconv, gp_high, gp_low, gcat, edges, halo_m, edge_act, halo_g, stats, act_sums, coef, out_coef,
        w_t, wg_high, wg_low, wg, cols, x_acc, gw_acc, gb_acc, y_acc, gain_acc, sums,
        gall, rs_it, part, rs_tm, quarter, done, small, small_it, small_tm, small_done,
        in_sem, out_sem, left_send, left_recv, right_send, right_recv,
        halo_send, halo_recv, stat_send, stat_recv, ar_send, ar_recv,
    ) = refs
    size = rows_sent // plan.parts
    out_res = out_gs1
    tm = lax.axis_index("tm")
    it = lax.axis_index("items")
    first, last = tm == 0, tm == n_tm - 1
    base = tm * frames
    whole = frames * n_tm

    def remote(src, dst, send, recv, axis, peer):
        return pltpu.make_async_remote_copy(
            src_ref=src, dst_ref=dst, send_sem=send, recv_sem=recv,
            device_id={axis: peer}, device_id_type=MESH,
        )

    def others(axis, count, mine, act):
        def turn(step, carry):
            act(lax.rem(mine + step, count))
            return carry

        lax.fori_loop(1, count, turn, 0)

    def load(kind):
        src, dst = ((s2t_h, s2t), (s1_h, s1), (cr_h, cr), (cs_h, cs))[kind]
        return pltpu.make_async_copy(src, dst, in_sem.at[kind])

    for kind in range(4):
        load(kind).start()

    barrier = pltpu.get_barrier_semaphore()

    def greet(axis):
        def act(peer):
            pl.semaphore_signal(barrier, inc=1, device_id={axis: peer}, device_id_type=MESH)

        return act

    others("tm", n_tm, tm, greet("tm"))
    others("items", n_it, it, greet("items"))
    pl.semaphore_wait(barrier, n_tm + n_it - 2)

    def to_next(chunk):
        cut = pl.ds(chunk * size, size)
        return remote(
            packed_h.at[cut], from_left.at[cut], left_send.at[chunk], left_recv.at[chunk],
            "tm", jnp.minimum(tm + 1, n_tm - 1),
        )

    def to_previous(chunk):
        cut = pl.ds(chunk * size, size)
        return remote(
            gpack.at[cut], from_right_h.at[cut], right_send.at[chunk], right_recv.at[chunk],
            "tm", jnp.maximum(tm - 1, 0),
        )

    def start_to_next(chunk):
        @pl.when((chunk < plan.parts) & jnp.logical_not(last))
        def _():
            to_next(chunk).start()

    for chunk in range(plan.out[0]):
        start_to_next(chunk)

    def arrived(place):
        def take(chunk, carry):
            @pl.when(jnp.logical_not(first))
            def _():
                to_next(chunk).wait_recv()
                staged[pl.ds(pl.multiple_of(frames + chunk * size, 8), size)] = from_left[
                    pl.ds(pl.multiple_of(chunk * size, 8), size)]

            return carry

        for k in range(items):
            low_end, high_end = (plan.arrive[k - 1] if k else 0), plan.arrive[k]
            if high_end > low_end:
                @pl.when(place == k)
                def _():
                    lax.fori_loop(low_end, high_end, take, 0)

    def send_back(low_end, high_end):
        def put(chunk, carry):
            def turn(block, carry):
                block = chunk * (size // GROUP) + block
                source = pack[block // LANES, block % LANES] * GROUP
                gpack[pl.ds(pl.multiple_of(block * GROUP, GROUP), GROUP)] = gbuf[
                    pl.ds(source, GROUP)]
                return carry

            lax.fori_loop(0, size // GROUP, turn, 0, unroll=True)
            pl.when(jnp.logical_not(first))(to_previous(chunk).start)
            return carry

        lax.fori_loop(low_end, high_end, put, 0)

    def bulk(index, point):
        sent = plan.out[0]
        for k, counts in enumerate(plan.out[1]):
            start = sent + sum(counts[:point])
            sent += sum(counts)
            if counts[point]:
                @pl.when(index == k)
                def _():
                    for chunk in range(start, start + counts[point]):
                        start_to_next(chunk)

        returned = 0
        for k, counts in plan.back.items():
            start = returned + sum(counts[:point])
            returned += sum(counts)
            if counts[point]:
                pl.when(index == k)(functools.partial(send_back, start, start + counts[point]))

    w_high, w_low = halves(w_in[...].T)
    w_t[0:chans] = w_high
    w_t[chans : 2 * chans] = w_low
    w_t[2 * chans :] = w_high
    wg[0:chans] = w_res[...] * gamma2[...]
    wg[chans:] = w_skip[...] * gamma2[...]
    high_part, low_part = halves(wg[...])
    wg_high[...] = high_part
    wg_low[...] = low_part
    cols[0] = column(gain1[...])
    cols[1] = column(gain2[...])
    for side, (weight, bias) in enumerate(((w_res, b_res), (w_skip, b_skip))):
        weight_sum = jnp.sum(wg[side * chans : (side + 1) * chans], axis=1, keepdims=True)
        shift = jnp.sum(weight[...] * beta2[...], axis=1, keepdims=True)
        cols[2 + side] = jnp.broadcast_to(weight_sum, (chans, LANES))
        cols[4 + side] = jnp.broadcast_to(shift, (chans, LANES)) + column(bias[...])
    x_acc[...] = jnp.zeros_like(x_acc)
    gw_acc[...] = jnp.zeros_like(gw_acc)
    gb_acc[...] = jnp.zeros_like(gb_acc)
    y_acc[...] = jnp.zeros_like(y_acc)
    gain_acc[...] = jnp.zeros_like(gain_acc)
    sums[...] = jnp.zeros_like(sums)

    main = (frames - plan.tail) // CHUNK
    chunks = frames // CHUNK

    def by_lanes(act, init, merged):
        if merged:
            for b in range(blocks):
                init = act(b * LANES, init)
            return init
        return lax.fori_loop(0, blocks, lambda b, c: act(pl.multiple_of(b * LANES, LANES), c), init)

    def side_by_side(index, together, parts):
        low_end, high_end = together
        all_due = (index >= low_end) & (index <= high_end)

        @pl.when(all_due)
        def _():
            for _, _, act in parts:
                act(True)

        for first_turn, last_turn, act in parts:
            due = (index >= first_turn) & (index <= last_turn) & jnp.logical_not(all_due)
            pl.when(due)(functools.partial(act, False))

    def by_rows(act, init):
        def at(masked):
            return lambda c, carry: act(pl.multiple_of(c * CHUNK, CHUNK), masked, carry)

        carry = init
        for c in range(chunks):
            carry = act(c * CHUNK, c >= main, carry)
        return carry

    def valid_rows(row, count, length):
        index = lax.broadcasted_iota(jnp.int32, (count, LANES), 0)
        return (index + (base + row)) < length

    def lane_mask(length):
        return (lax.broadcasted_iota(jnp.int32, (8, frames), 1) + base) < length

    def add_sum(row, lanes, value):
        sums[pl.ds(row, 1), pl.ds(lanes, LANES)] += value

    def send_stats(phase, item):
        mine = stats.at[phase, item, tm]
        others("tm", n_tm, tm, lambda peer: remote(
            mine, mine, stat_send.at[phase, item], stat_recv.at[phase, item], "tm", peer).start())

    def wait_stats(phase, item, sem):
        if n_tm > 1:
            block = stats.at[phase, item, pl.ds(0, n_tm - 1)]
            pltpu.make_async_copy(block, block, sem.at[phase, item]).wait()

    def read_stats(phase, item):
        total = stats[phase, item, 0]
        for peer in range(1, n_tm):
            total = total + stats[phase, item, peer]
        total = jnp.sum(total, axis=1, keepdims=True)
        return [total[k : k + 1] for k in range(4)]

    def put_stats(phase, item, rows):
        for k, row in enumerate(rows):
            stats[phase, item, tm, k : k + 1] = row
        for k in range(len(rows), 4):
            stats[phase, item, tm, k : k + 1] = jnp.zeros((1, LANES), F32)

    def halo_copies(kind, place, slot):
        if kind == 0:
            ends, halo = (edges.at[place, 0], edges.at[place, 1]), halo_m
        else:
            ends = (gconv.at[slot, pl.ds(wing, wing)], gconv.at[slot, pl.ds(frames, wing)])
            halo = halo_g
        down = remote(
            ends[0], halo.at[place, 1], halo_send.at[kind, place, 0],
            halo_recv.at[kind, place, 1], "tm", jnp.maximum(tm - 1, 0))
        up = remote(
            ends[1], halo.at[place, 0], halo_send.at[kind, place, 1],
            halo_recv.at[kind, place, 0], "tm", jnp.minimum(tm + 1, n_tm - 1))
        return down, up

    def send_halo(kind, place, slot=None):
        down, up = halo_copies(kind, place, slot)
        pl.when(jnp.logical_not(first))(down.start)
        pl.when(jnp.logical_not(last))(up.start)

    def wait_halo(kind, place, slot=None):
        down, up = halo_copies(kind, place, slot)

        @pl.when(jnp.logical_not(first))
        def _():
            down.wait_send()
            up.wait_recv()

        @pl.when(jnp.logical_not(last))
        def _():
            up.wait_send()
            down.wait_recv()

    def mix(place):
        slot = lax.rem(place, 5)
        item = order[place]
        before = staged[pl.ds(window[place] * GROUP, frames)]
        cat[0:frames] = jnp.where(first, 0.0, before)
        cat[frames:] = s2t[place]
        moved = cat[pl.ds(frames - offs[place], frames), :].T
        moved_s[slot] = moved
        mixed = wide(cols[0], frames) * s1[item] + wide(cols[1], frames) * moved
        mixed = jnp.where(lane_mask(lens[place])[0:1], mixed, 0.0)
        mixed_s[place] = mixed
        for side, row in enumerate((0, frames - wing)):
            near = cat[pl.ds(frames + row - offs[place], wing), :]
            block = 0 if side == 0 else frames - LANES
            turned = s1[item, :, block : block + LANES].T[row - block : row - block + wing]
            ends = gain1[...] * turned + gain2[...] * near
            edges[place, side] = jnp.where(valid_rows(row, wing, lens[place]), ends, 0.0)
        mix_high, mix_low = halves(mixed)
        mcat[slot, 0:chans] = mix_high
        mcat[slot, chans:] = mix_low

    def mix_product(place):
        slot = lax.rem(place, 5)
        left = jnp.concatenate([mcat[slot, 0:chans], mcat[slot]], axis=0)
        pre_raw[...] = dot(left, w_t[...], 0, 0)

    def edge_product(place):
        end_high, end_low = halves(halo_m[place].reshape(2 * wing, chans))
        left = jnp.concatenate([end_high, end_high, end_low], axis=1)
        x = dot(left, w_t[...], 1, 0) + b_in[...]
        half = jnp.tanh(0.5 * x)
        edge_act[...] = jnp.maximum(x, slope1[...] * x) - (1.0 - slope1[...]) * jnp.log(
            0.5 + 0.5 * jnp.abs(half))

    def phase_a(place, merged):
        slot = lax.rem(place, 4)
        length = lens[place]

        def lanes_step(lanes, carry):
            cut = pl.ds(lanes, LANES)
            bias, slope = b_in[:, cut], slope1[:, cut]

            def rows_step(row, masked, carry):
                rows = pl.ds(row, CHUNK)
                x = pre_raw[rows, cut] + bias
                half = jnp.tanh(0.5 * x)
                act = jnp.maximum(x, slope * x) - (1.0 - slope) * jnp.log(
                    0.5 + 0.5 * jnp.abs(half))
                pre1[slot, rows, cut] = x
                a1[slot, pl.ds(row + wing, CHUNK), cut] = act
                if masked:
                    act = jnp.where(valid_rows(row, CHUNK, length), act, 0.0)
                return carry[0] + fold_rows(act), carry[1] + fold_rows(act * act)

            return by_rows(rows_step, carry)

        zero = jnp.zeros((8, LANES), F32)
        carry = by_lanes(lanes_step, (zero, zero), merged)
        put_stats(0, place, [jnp.sum(c, axis=0, keepdims=True) for c in carry])

    def scales(totals, length):
        count = jnp.float32(units) * length.astype(F32)
        mean = totals[0] / count
        inverse = lax.rsqrt(totals[1] / count - mean * mean + EPS)
        return mean, inverse, count

    def before_b(place):
        slot = lax.rem(place, 4)
        length = lens[place]
        mean, inverse, _ = scales(read_stats(0, place), length)
        scale = gamma1[...] * inverse
        shift = beta1[...] - scale * mean
        outside = mean - beta1[...] / scale
        taps = [tap_rows[k : k + 1] for k in range(3)]
        coef[0:1] = taps[0] * scale
        coef[1:2] = taps[1] * scale
        coef[2:3] = taps[2] * scale
        coef[3:4] = b_depth[...] + shift * (taps[0] + taps[1] + taps[2])
        a1[slot, 0:wing] = jnp.where(first, outside, edge_act[0:wing])
        after = (lax.broadcasted_iota(jnp.int32, (wing, units), 0) + (base + frames)) < length
        a1[slot, frames + wing :] = jnp.where(after, edge_act[wing:], outside)


        @pl.when(last)
        def _():
            for row in range(frames - plan.tail, frames, CHUNK):
                keep = wide(valid_rows(row, CHUNK, length).astype(F32), units) > 0.5
                rows = slice(row + wing, row + wing + CHUNK)
                a1[slot, rows] = jnp.where(keep, a1[slot, rows], outside)

    def phase_b(place, merged):
        slot = lax.rem(place, 4)
        pair = lax.rem(place, 2)
        length = lens[place]

        def lanes_step(lanes, carry):
            cut = pl.ds(lanes, LANES)
            slope = slope2[:, cut]
            w0, w1, w2, const = (coef[k : k + 1, cut] for k in range(4))

            def rows_step(row, masked, carry):
                rows = pl.ds(row, CHUNK)
                x = const + w0 * a1[slot, rows, cut]
                x += w1 * a1[slot, pl.ds(row + wing, CHUNK), cut]
                x += w2 * a1[slot, pl.ds(row + 2 * wing, CHUNK), cut]
                half = jnp.tanh(0.5 * x)
                act = jnp.maximum(x, slope * x) - (1.0 - slope) * jnp.log(
                    0.5 + 0.5 * jnp.abs(half))
                conv[pair, rows, cut] = x
                act2[pair, rows, cut] = act
                d2[pair, rows, cut] = (0.5 + 0.5 * slope) + (0.5 - 0.5 * slope) * half
                act_high, act_low = halves(act)
                high[place, rows, cut] = act_high
                low[place, rows, cut] = act_low
                if masked:
                    act = jnp.where(valid_rows(row, CHUNK, length), act, 0.0)
                return carry[0] + fold_rows(act), carry[1] + fold_rows(act * act)

            return by_rows(rows_step, carry)

        zero = jnp.zeros((8, LANES), F32)
        carry = by_lanes(lanes_step, (zero, zero), merged)
        act_sums[0:1] = jnp.sum(carry[0], axis=0, keepdims=True)
        act_sums[1:2] = jnp.sum(carry[1], axis=0, keepdims=True)

    def cotangents(place):
        item = order[place]
        pair = lax.rem(place, 2)
        keep = lane_mask(lens[place])[0:1]
        in_sum = None
        for side, source in enumerate((cr, cs)):
            cot = jnp.where(keep, source[item], 0.0)
            cot_high, cot_low = halves(cot)
            gcat[side * chans : (side + 1) * chans] = cot_high
            gcat[(2 + side) * chans : (3 + side) * chans] = cot_low
            partial = fold_lanes(cot)
            rows = pl.ds(side * chans, chans)
            y_acc[1 + pair, rows] = partial
            gb_acc[rows] += partial
            by_weight = cols[2 + side] * partial
            in_sum = by_weight if in_sum is None else in_sum + by_weight
        act_sums[2:3] = jnp.sum(in_sum, axis=0, keepdims=True)

    def products(place):
        cot_high, cot_low = gcat[0 : 2 * chans], gcat[2 * chans :]
        act_h, act_l = high[place], low[place]
        left = jnp.concatenate([cot_high, cot_high, cot_low], axis=1)
        found = dot(left, jnp.concatenate([act_h, act_l, act_h], axis=0), 1, 0)
        grad_a[...] = found
        cross = jnp.sum(fold_lanes(fold_rows(wg[...] * found)), axis=0, keepdims=True)
        put_stats(1, place, (act_sums[0:1], act_sums[1:2], act_sums[2:3], cross))

    def outputs(place):
        pair = lax.rem(place, 2)
        act_h, act_l = high[place], low[place]
        left = jnp.concatenate([wg_high[...], wg_high[...], wg_low[...]], axis=1)
        raw = dot(left, jnp.concatenate([act_h, act_l, act_h], axis=1), 1, 1)
        keep = lane_mask(lens[place])[0:1]
        inverse, by_mean = out_coef[place, 0:1, 0:1], out_coef[place, 1:2, 0:1]
        out = inverse * raw[0:chans] + wide(cols[4] - by_mean * cols[2], frames)
        out_res[pair] = jnp.where(keep, mixed_s[place] + out, 0.0)
        out = inverse * raw[chans:] + wide(cols[5] - by_mean * cols[3], frames)
        out_skip[pair] = jnp.where(keep, out, 0.0)

    def back_product():
        left = jnp.concatenate([gcat[...], gcat[0 : 2 * chans]], axis=0)
        right = jnp.concatenate([wg_high[...], wg_high[...], wg_low[...]], axis=0)
        e2[...] = dot(left, right, 0, 0)

    def before_c(place):
        length = lens[place]
        totals = read_stats(1, place)
        mean, inverse, count = scales(totals, length)
        sum_e, sum_ea = totals[2], totals[3]
        mean_e = sum_e / count
        mean_ex = inverse * (sum_ea - mean * sum_e) / count
        by_act = -inverse * inverse * mean_ex
        by_one = -inverse * mean_e - by_act * mean
        mean_1, inverse_1, _ = scales(read_stats(0, place), length)
        scale_1 = gamma1[...] * inverse_1
        coef[4:5] = scale_1
        coef[5:6] = beta1[...] - scale_1 * mean_1
        for row, value in ((10, by_act), (11, by_one), (12, inverse), (13, inverse * mean)):
            coef[row : row + 1] = jnp.broadcast_to(value, (1, units))
        out_coef[place, 0:1] = jnp.broadcast_to(inverse, (1, LANES))
        out_coef[place, 1:2] = jnp.broadcast_to(inverse * mean, (1, LANES))

    def phase_c(place, merged):
        slot = lax.rem(place, 4)
        pair = lax.rem(place, 2)
        length = lens[place]
        y_acc[0] += coef[13:14, 0:LANES] * y_acc[1 + pair]
        inverse = coef[12:13, 0:1]
        x_acc[...] += inverse * grad_a[...]
        edge_rows = min(frames, plan.tail + CHUNK)

        def lanes_step(lanes, carry):
            cut = pl.ds(lanes, LANES)
            by_a, by_1, inv_e = (coef[k : k + 1, cut] for k in (10, 11, 12))

            def rows_step(row, masked, carry):
                rows = pl.ds(row, CHUNK)
                middle = pl.ds(row + wing, CHUNK)
                behind = pl.ds(row + 2 * wing, CHUNK)
                act = act2[pair, rows, cut]
                g = inv_e * e2[rows, cut] + by_a * act + by_1
                if masked:
                    g = jnp.where(valid_rows(row, CHUNK, length), g, 0.0)
                gc = g * d2[pair, rows, cut]
                gconv[pair, middle, cut] = gc
                parts = (
                    g * (conv[pair, rows, cut] - act), gc, gc * a1[slot, rows, cut],
                    gc * a1[slot, middle, cut], gc * a1[slot, behind, cut],
                )
                return tuple(c + fold_rows(p) for c, p in zip(carry, parts))

            zero = jnp.zeros((8, LANES), F32)
            found = by_rows(rows_step, (zero,) * 5)
            slope_sum, total, n0, n1, n2 = (jnp.sum(f, axis=0, keepdims=True) for f in found)

            def edge_step(c, carry):
                row = c * CHUNK
                gc = gconv[pair, pl.ds(row + wing, CHUNK), cut]
                inside = valid_rows(row + wing, CHUNK, length)
                return carry + fold_rows(jnp.where(inside, 0.0, gc))

            late = zero
            for c in range((frames - edge_rows) // CHUNK, chunks):
                late = edge_step(c, late)
            late = jnp.sum(late, axis=0, keepdims=True)
            early = jnp.sum(gconv[pair, wing : 2 * wing, cut], axis=0, keepdims=True)
            early = jnp.where(first, early, 0.0)
            scale, shift = coef[4:5, cut], coef[5:6, cut]
            gains, bias = gamma1[:, cut], beta1[:, cut]
            reach = (total - early, total, total - late)
            by_beta = jnp.zeros((1, LANES), F32)
            by_gamma = jnp.zeros((1, LANES), F32)
            for k, (n_k, b_k) in enumerate(zip((n0, n1, n2), reach)):
                tap = tap_rows[k : k + 1, cut]
                n_k = scale * n_k + shift * total
                add_sum(TAP + k, lanes, n_k)
                by_beta += tap * b_k
                by_gamma += tap * (n_k - bias * b_k)
            add_sum(SLOPE_TWO, lanes, slope_sum)
            add_sum(B_DEPTH, lanes, total)
            add_sum(BETA_ONE, lanes, by_beta)
            add_sum(GAMMA_ONE, lanes, by_gamma)
            return carry[0] + gains * by_beta, carry[1] + by_gamma

        zero = jnp.zeros((1, LANES), F32)
        put_stats(2, place, by_lanes(lanes_step, (zero, zero), merged))

    def out_copies(item):
        pair = lax.rem(item, 2)
        return (
            pltpu.make_async_copy(out_res.at[pair], res_h.at[item], out_sem.at[0, item]),
            pltpu.make_async_copy(out_skip.at[pair], skip_h.at[item], out_sem.at[1, item]),
        )

    def gs1_copy(item):
        return pltpu.make_async_copy(
            out_gs1.at[lax.rem(item, 2)], gs1_h.at[item], out_sem.at[2, item])

    def gmoved_copy(item):
        return pltpu.make_async_copy(
            gbuf.at[pl.ds(item * frames, frames)], gmoved_h.at[item], out_sem.at[3, item])

    def before_d(place):
        pair = lax.rem(place, 2)
        length = lens[place]
        totals = read_stats(2, place)
        mean, inverse, count = scales(read_stats(0, place), length)
        mean_e, mean_ex = totals[0] / count, totals[1] / count
        by_act = -inverse * inverse * mean_ex
        by_one = -inverse * mean_e - by_act * mean
        for k in range(3):
            coef[6 + k : 7 + k] = tap_rows[k : k + 1] * gamma1[...] * inverse
        for row, value in ((14, by_act), (15, by_one)):
            coef[row : row + 1] = jnp.broadcast_to(value, (1, units))
        gconv[pair, 0:wing] = jnp.where(first, 0.0, halo_g[place, 0])
        gconv[pair, frames + wing :] = jnp.where(last, 0.0, halo_g[place, 1])

    def phase_d(place, merged):
        slot = lax.rem(place, 4)
        pair = lax.rem(place, 2)
        length = lens[place]

        def lanes_step(lanes, carry):
            cut = pl.ds(lanes, LANES)
            slope = slope1[:, cut]
            by_a, by_1 = coef[14:15, cut], coef[15:16, cut]
            u0, u1, u2 = (coef[6 + k : 7 + k, cut] for k in range(3))

            def rows_step(row, masked, carry):
                rows = pl.ds(row, CHUNK)
                middle = pl.ds(row + wing, CHUNK)
                behind = pl.ds(row + 2 * wing, CHUNK)
                act, x = a1[slot, middle, cut], pre1[slot, rows, cut]
                g = by_a * act + by_1 + u0 * gconv[pair, behind, cut]
                g += u1 * gconv[pair, middle, cut] + u2 * gconv[pair, rows, cut]
                if masked:
                    g = jnp.where(valid_rows(row, CHUNK, length), g, 0.0)
                half = jnp.tanh(0.5 * x)
                gp = g * ((0.5 + 0.5 * slope) + (0.5 - 0.5 * slope) * half)
                gp_h, gp_l = halves(gp)
                gp_high[rows, cut] = gp_h
                gp_low[rows, cut] = gp_l
                return carry[0] + fold_rows(g * (x - act)), carry[1] + fold_rows(gp)

            zero = jnp.zeros((8, LANES), F32)
            slope_sum, bias_sum = by_rows(rows_step, (zero, zero))
            add_sum(SLOPE_ONE, lanes, jnp.sum(slope_sum, axis=0, keepdims=True))
            add_sum(B_IN, lanes, jnp.sum(bias_sum, axis=0, keepdims=True))
            return carry

        by_lanes(lanes_step, 0, merged)

    def weight_product(place):
        slot = lax.rem(place, 5)
        g_h, g_l = gp_high[...], gp_low[...]
        gw_acc[...] += dot(mcat[slot], g_h, 1, 0)
        gw_acc[0:chans] += dot(mcat[slot, 0:chans], g_l, 1, 0)

    def mixture_gradient(place):
        slot = lax.rem(place, 5)
        pair = lax.rem(place, 2)
        item = order[place]
        both = dot(w_t[0 : 2 * chans], gp_high[...], 1, 1)
        g_mixed = both[0:chans] + both[chans:] + dot(w_t[0:chans], gp_low[...], 1, 1)
        g_mixed = jnp.where(lane_mask(lens[place])[0:1], cr[item] + g_mixed, 0.0)
        out_gs1[pair] = wide(cols[0], frames) * g_mixed
        gain_acc[0] += fold_lanes(g_mixed * s1[item])
        gain_acc[1] += fold_lanes(g_mixed * moved_s[slot])
        gbuf[pl.ds(pl.multiple_of(place * frames, 8), frames)] = (
            wide(cols[1], frames) * g_mixed).T

    big, small_part = plan.seg // n_it, plan.seg // n_it // n_tm

    def segment(seg):
        return seg * plan.seg, big, small_part

    def stage_copies(seg, stage):
        start, big, small = segment(seg)
        offset = start // n_it
        send, recv = ar_send.at[seg, stage], ar_recv.at[seg, stage]
        if stage == 0:
            return "items", n_it, it, lambda peer: remote(
                gall.at[pl.ds(start + peer * big, big)], rs_it.at[it, pl.ds(offset, big)],
                send, recv, "items", peer)
        if stage == 1:
            return "tm", n_tm, tm, lambda peer: remote(
                part.at[pl.ds(offset + peer * small, small)],
                rs_tm.at[tm, pl.ds(offset // n_tm, small)], send, recv, "tm", peer)
        if stage == 2:
            mine = quarter.at[pl.ds(offset + tm * small, small)]
            return "tm", n_tm, tm, lambda peer: remote(mine, mine, send, recv, "tm", peer)
        mine = done.at[pl.ds(start + it * big, big)]
        return "items", n_it, it, lambda peer: remote(mine, mine, send, recv, "items", peer)

    def stage_start(seg, stage):
        axis, count, mine, copy = stage_copies(seg, stage)
        others(axis, count, mine, lambda peer: copy(peer).start())

    def stage_wait(seg, stage, sem):
        start, big, small = segment(seg)
        count, rows = ((n_it, big), (n_tm, small), (n_tm, small), (n_it, big))[stage]
        if count > 1:
            block = gall.at[pl.ds(0, (count - 1) * rows)]
            pltpu.make_async_copy(block, block, sem.at[seg, stage]).wait()

    def added(ref, count, rows):
        total = ref[0, rows]
        for peer in range(1, count):
            total = total + ref[peer, rows]
        return total

    def stage_zero(seg):
        start, big, _ = segment(seg)
        rs_it[it, pl.ds(start // n_it, big)] = gall[pl.ds(start + it * big, big)]
        stage_start(seg, 0)

    def stage_one(seg):
        start, big, small = segment(seg)
        offset = start // n_it
        stage_wait(seg, 0, ar_recv)
        part[pl.ds(offset, big)] = added(rs_it, n_it, pl.ds(offset, big))
        rs_tm[tm, pl.ds(offset // n_tm, small)] = part[pl.ds(offset + tm * small, small)]
        stage_start(seg, 1)

    def stage_two(seg):
        start, big, small = segment(seg)
        offset = start // n_it
        stage_wait(seg, 1, ar_recv)
        quarter[pl.ds(offset + tm * small, small)] = added(
            rs_tm, n_tm, pl.ds(offset // n_tm, small))
        stage_start(seg, 2)

    def stage_three(seg):
        start, big, _ = segment(seg)
        offset = start // n_it
        stage_wait(seg, 2, ar_recv)
        done[pl.ds(start + it * big, big)] = quarter[pl.ds(offset, big)]
        stage_start(seg, 3)

    def weights_sum():
        for side, weight in enumerate((w_res, w_skip)):
            rows = slice(side * chans, (side + 1) * chans)
            ones = jnp.sum(gb_acc[rows], axis=1, keepdims=True)
            centred = x_acc[rows] - jnp.sum(y_acc[0, rows], axis=1, keepdims=True)
            grad = gamma2[...] * centred + beta2[...] * ones
            for b in range(blocks):
                gall[b * 2 * chans + side * chans : b * 2 * chans + (side + 1) * chans] = grad[
                    :, b * LANES : (b + 1) * LANES]
            sums[GAMMA_TWO : GAMMA_TWO + 1] += jnp.sum(
                weight[...] * centred, axis=0, keepdims=True)
            sums[BETA_TWO : BETA_TWO + 1] += jnp.sum(weight[...] * ones, axis=0, keepdims=True)
            sums[NARROW : NARROW + 1, (2 + side) * LANES : (3 + side) * LANES] = jnp.sum(
                gb_acc[rows].T, axis=0, keepdims=True)

    def input_weights_sum():
        start = plan.in_start
        grad = gw_acc[0:chans] + gw_acc[chans:]
        for b in range(blocks):
            gall[start + b * chans : start + (b + 1) * chans] = grad[
                :, b * LANES : (b + 1) * LANES]

    def narrow_sums():
        for side in range(2):
            sums[NARROW : NARROW + 1, side * LANES : (side + 1) * LANES] = jnp.sum(
                gain_acc[side].T, axis=0, keepdims=True)
        sums[SLOPE_ONE : SLOPE_ONE + 1] = sums[SLOPE_ONE : SLOPE_ONE + 1] / (1.0 - slope1[...])
        sums[SLOPE_TWO : SLOPE_TWO + 1] = sums[SLOPE_TWO : SLOPE_TWO + 1] / (1.0 - slope2[...])
        sums[GAMMA_ONE : GAMMA_ONE + 1] = sums[GAMMA_ONE : GAMMA_ONE + 1] / gamma1[...]
        for b in range(blocks):
            small[b * SUM_ROWS : (b + 1) * SUM_ROWS] = sums[:, b * LANES : (b + 1) * LANES]
        small_it[it] = small[...]

    narrow = plan.small // n_tm

    def small_copies(stage):
        send, recv = ar_send.at[plan.segs, stage], ar_recv.at[plan.segs, stage]
        if stage == 0:
            return "items", n_it, it, lambda peer: remote(
                small, small_it.at[it], send, recv, "items", peer)
        if stage == 1:
            return "tm", n_tm, tm, lambda peer: remote(
                small.at[pl.ds(peer * narrow, narrow)], small_tm.at[tm], send, recv, "tm", peer)
        mine = small_done.at[pl.ds(tm * narrow, narrow)]
        return "tm", n_tm, tm, lambda peer: remote(mine, mine, send, recv, "tm", peer)

    def small_start(stage):
        axis, count, mine, copy = small_copies(stage)
        others(axis, count, mine, lambda peer: copy(peer).start())

    def small_wait(stage, sem):
        count, rows = ((n_it, plan.small), (n_tm, narrow), (n_tm, narrow))[stage]
        if count > 1:
            block = gall.at[pl.ds(0, (count - 1) * rows)]
            pltpu.make_async_copy(block, block, sem.at[plan.segs, stage]).wait()

    def small_one():
        small_wait(0, ar_recv)
        small_wait(0, ar_send)
        total = small_it[0]
        for peer in range(1, n_it):
            total = total + small_it[peer]
        small[...] = total
        small_tm[tm] = small[pl.ds(tm * narrow, narrow)]
        small_start(1)

    def small_two():
        small_wait(1, ar_recv)
        total = small_tm[0]
        for peer in range(1, n_tm):
            total = total + small_tm[peer]
        small_done[pl.ds(tm * narrow, narrow)] = total
        small_start(2)

    load(0).wait()
    load(1).wait()
    arrived(0)
    mix(0)
    send_halo(0, 0)
    mix_product(0)
    load(2).wait()
    load(3).wait()
    end = items - 1

    def step(index, carry):
        def within(lag, back=0):
            return (index >= lag) & (index <= end + lag - back)

        pl.when(within(6))(lambda: gs1_copy(index - 6).wait())
        pl.when(within(1))(lambda: wait_halo(0, index - 1))
        side_by_side(index, (4, end), (
            (1, end + 1, lambda merged: edge_product(index - 1)),
            (0, end, lambda merged: phase_a(index, merged)),
            (4, end + 3, lambda merged: weight_product(index - 4)),
            (4, end + 3, lambda merged: mixture_gradient(index - 4)),
        ))

        @pl.when(within(0))
        def _():
            send_stats(0, index)

        @pl.when(index == end + 4)
        def _():
            weight_product(index - 4)
            input_weights_sum()
            for seg in range(plan.weight_segs, plan.segs):
                stage_zero(seg)
            mixture_gradient(index - 4)
            stage_one(0)

        @pl.when(within(4))
        def _():
            gs1_copy(index - 4).start()
            gmoved_copy(index - 4).start()

        bulk(index, 0)

        @pl.when(within(1))
        def _():
            wait_stats(0, index - 1, stat_recv)
            before_b(index - 1)

        side_by_side(index, (2, end + 1), (
            (1, end + 1, lambda merged: phase_b(index - 1, merged)),
            (2, end + 2, lambda merged: back_product()),
        ))
        bulk(index, 1)

        @pl.when(within(2))
        def _():
            wait_stats(1, index - 2, stat_recv)
            before_c(index - 2)

        pl.when(within(1))(lambda: cotangents(index - 1))
        side_by_side(index, (2, end + 1), (
            (2, end + 2, lambda merged: phase_c(index - 2, merged)),
            (1, end + 1, lambda merged: products(index - 1)),
        ))

        @pl.when(within(1))
        def _():
            send_stats(1, index - 1)

        @pl.when(within(2))
        def _():
            send_stats(2, index - 2)
            send_halo(1, index - 2, lax.rem(index, 2))

        @pl.when(index == end + 2)
        def _():
            weights_sum()
            for seg in range(plan.weight_segs):
                stage_zero(seg)

        bulk(index, 2)

        @pl.when(within(3))
        def _():
            wait_halo(1, index - 3, lax.rem(index + 1, 2))
            wait_stats(2, index - 3, stat_recv)
            before_d(index - 3)

        @pl.when(index < end)
        def _():
            arrived(index + 1)
            mix(index + 1)
            send_halo(0, index + 1)

        side_by_side(index, (3, end - 1), (
            (3, end + 3, lambda merged: phase_d(index - 3, merged)),
            (0, end - 1, lambda merged: mix_product(index + 1)),
        ))
        bulk(index, 3)
        return carry

    lax.fori_loop(0, items + 4, step, 0)
    narrow_sums()
    small_start(0)

    def stages(acts):
        for act, *given in acts:
            act(*given)

    one, two, three = stage_one, stage_two, stage_three
    if items == 8 and plan.segs == 6:
        due = (
            ((one, 1),), ((one, 2),), ((one, 3),), ((two, 0),), ((one, 4), (two, 1)),
            ((one, 5),), ((two, 2), (small_one,)), ((two, 3),),
        )
        late = (
            (three, 0), (three, 1), (two, 4), (three, 2), (two, 5), (three, 3), (small_two,),
            (three, 4), (three, 5),
        )
    else:
        due = ((),) * items
        late = [(one, seg) for seg in range(1, plan.segs)] + [(small_one,)]
        late += [(two, seg) for seg in range(plan.segs)] + [(small_two,)]
        late += [(three, seg) for seg in range(plan.segs)]

    def turn(place, carry):
        @pl.when(place >= 2)
        def _():
            for copy in out_copies(place - 2):
                copy.wait()

        outputs(place)
        for copy in out_copies(place):
            copy.start()
        for k, acts in enumerate(due):
            if acts:
                pl.when(place == k)(functools.partial(stages, acts))
        start = sum(map(sum, plan.back.values()))
        each = (plan.parts - start) // items
        if each:
            send_back(start + place * each, start + place * each + each)
        return carry

    for place in range(max(0, items - 2), items):
        gs1_copy(place).wait()
    lax.fori_loop(0, items, turn, 0)
    stages(late)
    for seg in range(plan.segs):
        stage_wait(seg, 3, ar_recv)
    small_wait(2, ar_recv)
    total_copy = pltpu.make_async_copy(done, total_h, in_sem.at[0])
    total_copy.start()
    small_copy = pltpu.make_async_copy(small_done, small_h, in_sem.at[1])
    small_copy.start()

    def finish(item, carry):
        for phase in range(3):
            wait_stats(phase, item, stat_send)
        gmoved_copy(item).wait()
        return carry

    def finish_chunk(chunk, carry):
        @pl.when(jnp.logical_not(first))
        def _():
            to_previous(chunk).wait_send()

        @pl.when(jnp.logical_not(last))
        def _():
            to_next(chunk).wait_send()
            to_previous(chunk).wait_recv()

        return carry

    lax.fori_loop(0, items, finish, 0)
    lax.fori_loop(0, plan.parts, finish_chunk, 0)
    for item in range(max(0, items - 2), items):
        for copy in out_copies(item):
            copy.wait()
    for seg in range(plan.segs):
        for stage in range(4):
            stage_wait(seg, stage, ar_send)
    small_wait(1, ar_send)
    small_wait(2, ar_send)
    total_copy.wait()
    small_copy.wait()


def prelude(plan):
    items, frames, chans = plan.items, plan.frames, plan.chans
    rows = items * frames
    groups = rows // GROUP
    table = (rounded(groups, LANES) // LANES, LANES)
    per_item = frames // GROUP

    def body(
        offs_in, lens_in, s2_h, s2t_h, packed_h, pack, order, offs, lens, window, window_back,
        which, s2, s2t, packed, lookup_v, lookup, held, in_sem, out_sem, table_sem, send, recv,
    ):
        n_it = plan.n_it
        it = lax.axis_index("items")
        load = pltpu.make_async_copy(s2_h, s2, in_sem)
        load.start()
        barrier = pltpu.get_barrier_semaphore()

        def peers(act):
            def turn(step, carry):
                act(lax.rem(it + step, n_it))
                return carry

            lax.fori_loop(1, n_it, turn, 0)

        def copy(peer):
            return pltpu.make_async_remote_copy(
                src_ref=held.at[it], dst_ref=held.at[it], send_sem=send, recv_sem=recv,
                device_id={"items": peer}, device_id_type=MESH)

        peers(lambda peer: pl.semaphore_signal(
            barrier, inc=1, device_id={"items": peer}, device_id_type=MESH))
        given = [offs_in[i] for i in range(items)]
        places = []
        for i in range(items):
            rank = jnp.int32(0)
            for j in range(items):
                if j != i:
                    before = given[j] <= given[i] if j < i else given[j] < given[i]
                    rank += jnp.where(before, 1, 0)
            places.append(jnp.where(rank % 2 == 0, rank // 2, items - 1 - rank // 2))
        starts, needs, end = [], [], jnp.int32(0)
        taken = []
        for k in range(items):
            here = [jnp.where(place == k, 1, 0) for place in places]
            item = sum(i * h for i, h in enumerate(here))
            offset = sum(given[i] * h for i, h in enumerate(here))
            taken.append(item)
            order[k] = item
            offs[k] = offset
            lens[k] = sum(lens_in[i] * h for i, h in enumerate(here))
            needs.append((offset + GROUP - 1) // GROUP)
            starts.append(end)
            end = end + needs[k]
            window[k] = end
        held[it] = jnp.full((1, LANES), end, jnp.int32)

        index = (
            lax.broadcasted_iota(jnp.int32, table, 0) * LANES
            + lax.broadcasted_iota(jnp.int32, table, 1))

        def looked_up(index, firsts):
            total, previous = index, jnp.int32(0)
            for k in range(items):
                shift = firsts[k] - starts[k]
                total = total + jnp.where(index >= starts[k], shift - previous, 0)
                previous = shift
            return jnp.minimum(total, groups - 1)

        lookup_v[...] = looked_up(
            index, [(k + 1) * per_item - needs[k] for k in range(items)])
        to_smem = pltpu.make_async_copy(lookup_v, lookup, table_sem)
        to_smem.start()
        load.wait()
        for k in range(items // 2):
            s2t[k * frames : (k + 1) * frames] = s2[taken[k]].T
        pl.semaphore_wait(barrier, n_it - 1)
        peers(lambda peer: copy(peer).start())
        for k in range(items // 2, items):
            s2t[k * frames : (k + 1) * frames] = s2[taken[k]].T
        to_smem.wait()
        own_out = pltpu.make_async_copy(s2t, s2t_h, out_sem.at[0])
        own_out.start()

        def turn(group, carry):
            source = lookup[group // LANES, group % LANES] * GROUP
            packed[pl.ds(pl.multiple_of(group * GROUP, GROUP), GROUP)] = s2t[
                pl.ds(source, GROUP)]
            return carry

        lax.fori_loop(0, groups, turn, 0, unroll=16)
        packed_out = pltpu.make_async_copy(packed, packed_h, out_sem.at[1])
        packed_out.start()

        if n_it > 1:
            block = held.at[pl.ds(0, n_it - 1)]
            pltpu.make_async_copy(block, block, recv).wait()
        most = held[0]
        for peer in range(1, n_it):
            most = jnp.maximum(most, held[peer])
        choice = jnp.zeros((1, LANES), jnp.int32)
        sent = jnp.full((1, LANES), plan.caps[0] // GROUP, jnp.int32)
        for low_cap, cap in zip(plan.caps[:-1], plan.caps[1:]):
            more = most * GROUP > low_cap
            choice += more.astype(jnp.int32)
            sent += jnp.where(more, (cap - low_cap) // GROUP, 0)
        which[0] = jnp.max(choice)
        base = jnp.max(sent) - end
        for k in range(items):
            window_back[k] = base + starts[k]
        back = looked_up(index - base, [jnp.int32(k * per_item) for k in range(items)])
        pack[...] = jnp.where(index < base, 0, back)
        own_out.wait()
        packed_out.wait()
        if n_it > 1:
            pltpu.make_async_copy(block, block, send).wait()

    smem = pl.BlockSpec(memory_space=pltpu.SMEM)
    hbm = pl.BlockSpec(memory_space=pl.ANY)
    short = jax.ShapeDtypeStruct((items,), jnp.int32)
    flat = jax.ShapeDtypeStruct((rows, chans), F32)
    sem = pltpu.SemaphoreType.DMA
    return pl.pallas_call(
        body,
        out_shape=(
            flat, flat, jax.ShapeDtypeStruct(table, jnp.int32), short, short, short, short, short,
            jax.ShapeDtypeStruct((1,), jnp.int32),
        ),
        in_specs=[smem, smem, hbm],
        out_specs=(hbm, hbm, pl.BlockSpec(memory_space=pltpu.VMEM)) + (smem,) * 6,
        scratch_shapes=[
            pltpu.VMEM((items, chans, frames), F32), pltpu.VMEM((rows, chans), F32),
            pltpu.VMEM((rows, chans), F32), pltpu.VMEM(table, jnp.int32),
            pltpu.SMEM(table, jnp.int32), pltpu.VMEM((plan.n_it, 1, LANES), jnp.int32),
            sem, sem((2,)), sem, sem, sem,
        ],
        compiler_params=pltpu.CompilerParams(
            collective_id=0, has_side_effects=True, vmem_limit_bytes=62 * 2**20),
        name="prelude",
    )


def finisher(plan, rows):
    items, frames, chans, units = plan.items, plan.frames, plan.chans, plan.units
    blocks = units // LANES

    def body(
        order, offs, window, gmoved_h, from_right_h, total_h, small_h, res_h, skip_h, gs1_h, *rest
    ):
        outs, scratch = rest[:20], rest[20:]
        cat, gs2, total, small, passed, in_sem, out_sem, pass_sem, total_sem = scratch
        out_res, out_skip, out_gs1, out_gs2 = outs[:4]
        last = lax.axis_index("tm") == plan.n_tm - 1
        def through(kind, item):
            src, dst = ((res_h, out_res), (skip_h, out_skip), (gs1_h, out_gs1))[kind]
            held = passed.at[kind, item]
            return (
                pltpu.make_async_copy(src.at[item], held, pass_sem.at[0, kind, item]),
                pltpu.make_async_copy(held, dst.at[order[item]], pass_sem.at[1, kind, item]),
            )

        def loads(item):
            start = pl.multiple_of(window[item] * GROUP, GROUP)
            return (
                pltpu.make_async_copy(
                    gmoved_h.at[item], cat.at[item, pl.ds(0, frames)], in_sem.at[0, item]),
                pltpu.make_async_copy(
                    from_right_h.at[pl.ds(start, frames)], cat.at[item, pl.ds(frames, frames)],
                    in_sem.at[1, item]),
            )

        def store(item):
            return pltpu.make_async_copy(gs2.at[item], out_gs2.at[order[item]], out_sem.at[item])

        def start(item, carry):
            for copy in loads(item):
                copy.start()
            for kind in range(3):
                through(kind, item)[0].start()
            return carry

        total_copy = pltpu.make_async_copy(total_h, total, total_sem.at[0])
        total_copy.start()
        small_copy = pltpu.make_async_copy(small_h, small, total_sem.at[1])
        small_copy.start()
        lax.fori_loop(0, items, start, 0)

        def turn(item, carry):
            for copy in loads(item):
                copy.wait()
            for kind in range(3):
                arriving, leaving = through(kind, item)
                arriving.wait()
                leaving.start()

            @pl.when(last)
            def _():
                cat[item, frames:] = jnp.zeros((frames, chans), F32)

            gs2[item] = cat[item, pl.ds(offs[item], frames), :].T
            store(item).start()
            return carry

        lax.fori_loop(0, items, turn, 0)
        total_copy.wait()
        small_copy.wait()
        (
            gain_1, gain_2, g_in, gb_in, g_slope1, g_gamma1, g_beta1, g_taps, gb_depth, g_slope2,
            g_gamma2, g_beta2, g_res, gb_res, g_skip, gb_skip,
        ) = outs[4:]
        start_in = plan.in_start
        for b in range(blocks):
            cut = slice(b * LANES, (b + 1) * LANES)
            g_res[:, cut] = total[2 * b * chans : (2 * b + 1) * chans]
            g_skip[:, cut] = total[(2 * b + 1) * chans : (2 * b + 2) * chans]
            g_in[cut] = total[start_in + b * chans : start_in + (b + 1) * chans].T
            sums = small[b * SUM_ROWS : (b + 1) * SUM_ROWS]
            for out, row in (
                (gb_in, B_IN), (g_slope1, SLOPE_ONE), (g_gamma1, GAMMA_ONE), (g_beta1, BETA_ONE),
                (gb_depth, B_DEPTH), (g_slope2, SLOPE_TWO), (g_gamma2, GAMMA_TWO),
                (g_beta2, BETA_TWO),
            ):
                out[:, cut] = sums[row : row + 1]
            g_taps[:, cut] = sums[TAP : TAP + 3]
            (gain_1, gain_2, gb_res, gb_skip)[b][...] = sums[NARROW : NARROW + 1]

        def end(item, carry):
            store(item).wait()
            for kind in range(3):
                through(kind, item)[1].wait()
            return carry

        lax.fori_loop(0, items, end, 0)

    smem = pl.BlockSpec(memory_space=pltpu.SMEM)
    hbm = pl.BlockSpec(memory_space=pl.ANY)
    vmem = pl.BlockSpec(memory_space=pltpu.VMEM)
    big = jax.ShapeDtypeStruct((items, chans, frames), F32)

    def array(*shape):
        return jax.ShapeDtypeStruct(shape, F32)

    narrow, per_unit = array(1, chans), array(1, units)
    sem = pltpu.SemaphoreType.DMA
    return pl.pallas_call(
        body,
        out_shape=(big,) * 4 + (
            narrow, narrow, array(units, chans), per_unit, per_unit, per_unit, per_unit,
            array(3, units), per_unit, per_unit, per_unit, per_unit, array(chans, units), narrow,
            array(chans, units), narrow,
        ),
        in_specs=[smem] * 3 + [hbm] * 7,
        out_specs=(hbm,) * 4 + (vmem,) * 16,
        scratch_shapes=[
            pltpu.VMEM((items, 2 * frames, chans), F32), pltpu.VMEM((items, chans, frames), F32),
            pltpu.VMEM((rows, LANES), F32), pltpu.VMEM((plan.small, LANES), F32),
            pltpu.VMEM((3, items, chans, frames), F32),
            sem((2, items)), sem((items,)), sem((2, 3, items)), sem((2,)),
        ],
        compiler_params=pltpu.CompilerParams(vmem_limit_bytes=62 * 2**20),
        name="finisher",
    )


def per_device(
    mesh, source_one, source_two, offsets, lengths, gain_one, gain_two, w_in, b_in, slope_one,
    first_norm_gain, first_norm_bias, depthwise_weight, depthwise_bias, slope_two,
    second_norm_gain, second_norm_bias, w_res, b_res, w_skip, b_skip, cot_res, cot_skip,
):
    items, chans, frames = source_one.shape
    units = w_in.shape[0]
    plan = Plan(mesh, items, chans, frames, units)
    n_tm, n_it, wing = plan.n_tm, plan.n_it, DILATION_RATE
    full = items * frames
    s2t, packed, pack, order, offs, lens, window, window_back, which = prelude(plan)(
        offsets, lengths, source_two)

    def row(value):
        return value.reshape(1, -1)

    smem = pl.BlockSpec(memory_space=pltpu.SMEM)
    hbm = pl.BlockSpec(memory_space=pl.ANY)
    vmem = pl.BlockSpec(memory_space=pltpu.VMEM)
    rows = plan.segs * plan.seg

    def floats(*shape):
        return pltpu.VMEM(shape, F32)

    def shorts(*shape):
        return pltpu.VMEM(shape, BF16)

    big = jax.ShapeDtypeStruct((items, chans, frames), F32)
    sem = pltpu.SemaphoreType.DMA
    def block(sent, index):
        return pl.pallas_call(
            functools.partial(kernel, plan, sent),
            out_shape=(
                big, big, big, jax.ShapeDtypeStruct((items, frames, chans), F32),
                jax.ShapeDtypeStruct((full + frames, chans), F32),
                jax.ShapeDtypeStruct((rows, LANES), F32),
                jax.ShapeDtypeStruct((plan.small, LANES), F32),
            ),
            in_specs=[smem] * 5 + [hbm] * 5 + [vmem] * 16,
            out_specs=[hbm] * 7,
            scratch_shapes=[
                floats(items, chans, frames), floats(items, frames, chans),
                floats(items, chans, frames), floats(items, chans, frames),
                floats(sent, chans), floats(frames + sent, chans), floats(full, chans),
                floats(sent, chans),
                floats(2, chans, frames), floats(2, chans, frames), floats(2 * frames, chans),
                floats(5, chans, frames), floats(items, chans, frames),
                shorts(5, 2 * chans, frames),
                floats(frames, units), floats(4, frames + 2 * wing, units),
                floats(4, frames, units),
                floats(2, frames, units), floats(2, frames, units), floats(2, frames, units),
                floats(frames, units), shorts(items, frames, units),
                shorts(items, frames, units), floats(2 * chans, units),
                floats(2, frames + 2 * wing, units), shorts(frames, units),
                shorts(frames, units), shorts(4 * chans, frames),
                floats(items, 2, wing, chans), floats(items, 2, wing, chans),
                floats(2 * wing, units), floats(items, 2, wing, units),
                floats(3, items, n_tm, 4, LANES), floats(8, LANES), floats(16, units),
                floats(items, 2, LANES),
                shorts(3 * chans, units), shorts(2 * chans, units), shorts(2 * chans, units),
                floats(2 * chans, units), floats(6, chans, LANES),
                floats(2 * chans, units), floats(2 * chans, units),
                floats(2 * chans, LANES), floats(3, 2 * chans, LANES), floats(2, chans, LANES),
                floats(SUM_ROWS, units),
                floats(rows, LANES), floats(n_it, rows // n_it, LANES),
                floats(rows // n_it, LANES),
                floats(n_tm, rows // n_it // n_tm, LANES), floats(rows // n_it, LANES),
                floats(rows, LANES),
                floats(plan.small, LANES), floats(n_it, plan.small, LANES),
                floats(n_tm, plan.small // n_tm, LANES), floats(plan.small, LANES),
                sem((4,)), sem((4, items)), sem((plan.parts,)), sem((plan.parts,)),
                sem((plan.parts,)), sem((plan.parts,)), sem((2, items, 2)), sem((2, items, 2)),
                sem((3, items)), sem((3, items)), sem((plan.segs + 1, 4)),
                sem((plan.segs + 1, 4)),
            ],
            compiler_params=pltpu.CompilerParams(
                collective_id=1 + index, has_side_effects=True,
                vmem_limit_bytes=63 * 2**20),
            name="tcn_block",
        )

    branches = [block(sent, index) for index, sent in enumerate(plan.caps)]
    res, skip, gs1, gmoved, from_right, total, narrow = lax.switch(
        which[0], branches,
        order, offs, lens, window, pack, source_one, s2t.reshape(items, frames, chans), packed,
        cot_res, cot_skip,
        row(gain_one), row(gain_two), w_in, row(b_in), row(slope_one), row(first_norm_gain),
        row(first_norm_bias), depthwise_weight.T, row(depthwise_bias), row(slope_two),
        row(second_norm_gain), row(second_norm_bias), w_res, row(b_res), w_skip, row(b_skip),
    )
    outs = list(finisher(plan, rows)(
        order, offs, window_back, gmoved, from_right, total, narrow, res, skip, gs1))
    outs[11] = outs[11].T
    return tuple(out.reshape(-1) if out.shape[0] == 1 else out for out in outs)


def solution(mesh):
    split = P("items", None, "tm")
    in_specs = (split, split, P("items"), P("items")) + (P(),) * 16 + (split, split)
    out_specs = (split,) * 4 + (P(),) * 16
    return jax.shard_map(
        functools.partial(per_device, mesh), mesh=mesh, in_specs=in_specs, out_specs=out_specs,
        check_vma=False,
    )
```

```python
import functools

import jax
import jax.numpy as jnp
from jax import lax
from jax.experimental import pallas as pl
from jax.experimental.pallas import tpu as pltpu
from jax.sharding import PartitionSpec as P

DILATION_RATE = 16
EPS = 1e-05
LANES = 128
F32 = jnp.float32
BF16 = jnp.bfloat16
MESH = pl.DeviceIdType.MESH
CHUNK = 64
GROUP = 16

B_IN, SLOPE_ONE, GAMMA_ONE, BETA_ONE, TAP, B_DEPTH, SLOPE_TWO, GAMMA_TWO, BETA_TWO, NARROW = (
    0, 1, 2, 3, 4, 7, 8, 9, 10, 11,
)
SUM_ROWS = 16


def halves(value):
    high = value.astype(BF16)
    return high, (value - high.astype(F32)).astype(BF16)


def dot(left, right, over_left, over_right):
    return lax.dot_general(
        left, right, (((over_left,), (over_right,)), ((), ())), preferred_element_type=F32
    )


def fold_rows(value):
    return jnp.sum(value.reshape(value.shape[0] // 8, 8, value.shape[1]), axis=0)


def fold_lanes(value):
    total = value[:, :LANES]
    for start in range(LANES, value.shape[1], LANES):
        total = total + value[:, start : start + LANES]
    return total


def column(row):
    return jnp.broadcast_to(row, (LANES, LANES)).T


def wide(tile, width):
    return jnp.concatenate([tile] * (width // LANES), axis=1)


def rounded(size, step):
    return -(-size // step) * step


class Plan:
    def __init__(self, mesh, items, chans, frames, units):
        self.n_tm = mesh.shape["tm"]
        self.n_it = mesh.shape["items"]
        self.items, self.chans, self.frames, self.units = items, chans, frames, units
        whole = frames * self.n_tm
        self.tail = min(frames, rounded(whole // 32, CHUNK))
        step = 8 * self.n_tm * self.n_it
        self.seg = step
        weight_rows, rows = 2 * chans * units // LANES, chans * units // LANES
        if step >= weight_rows + rows:
            self.weight_segs, self.segs, self.in_start = 0, 1, weight_rows
        else:
            self.weight_segs = -(-weight_rows // step)
            self.segs = self.weight_segs + -(-rows // step)
            self.in_start = self.weight_segs * step
        self.small = rounded(SUM_ROWS * units // LANES, 8 * self.n_tm)
        full = items * frames
        self.parts = 32
        self.caps = tuple(sorted({
            rounded(full * part // 16, GROUP * self.parts) for part in (9, 10, 11, 12, 16)}))
        if items == 8 and self.caps[0] >= 5 * frames:
            self.arrive = (4, 8, 12, 16, 23, 29, 32, 32)
            self.out = (
                12, ((1, 1, 1, 1), (1, 1, 1, 1), (2, 1, 1, 1), (2, 1, 2, 2)))
            self.back = {
                6: (2, 1, 2, 1), 7: (1, 1, 1, 1), 8: (1, 1, 1, 1), 9: (1, 1, 1, 1),
                10: (4, 2, 0, 0)}
        else:
            self.arrive = (self.parts,) * items
            self.out = (self.parts, ())
            self.back = {items + 3: (self.parts, 0, 0, 0)}


def kernel(plan, rows_sent, *refs):
    n_tm, n_it = plan.n_tm, plan.n_it
    items, chans, frames, units = plan.items, plan.chans, plan.frames, plan.units
    wing = DILATION_RATE
    blocks = units // LANES
    (
        order, offs, lens, window, pack, s1_h, s2t_h, packed_h, cr_h, cs_h,
        gain1, gain2, w_in, b_in, slope1, gamma1, beta1, tap_rows, b_depth, slope2, gamma2, beta2,
        w_res, b_res, w_skip, b_skip,
        res_h, skip_h, gs1_h, gmoved_h, from_right_h, total_h, small_h,
        s1, s2t, cr, cs, from_left, staged, gbuf, gpack, out_skip, out_gs1, cat,
        moved_s, mixed_s, mcat, pre_raw, a1, pre1, conv, act2, d2, e2, high, low, grad_a,
        gconv, gp_high, gp_low, gcat, edges, halo_m, edge_act, halo_g, stats, turn_stats, act_sums, coef, out_coef,
        w_t, wg_high, wg_low, wg, cols, x_acc, gw_acc, gb_acc, y_acc, gain_acc, sums,
        gall, rs_it, part, rs_tm, quarter, done, small, small_it, small_tm, small_done,
        in_sem, out_sem, left_send, left_recv, right_send, right_recv,
        halo_send, halo_recv, stat_send, stat_recv, ar_send, ar_recv,
    ) = refs
    size = rows_sent // plan.parts
    out_res = out_gs1
    tm = lax.axis_index("tm")
    it = lax.axis_index("items")
    first, last = tm == 0, tm == n_tm - 1
    base = tm * frames
    whole = frames * n_tm

    def remote(src, dst, send, recv, axis, peer):
        return pltpu.make_async_remote_copy(
            src_ref=src, dst_ref=dst, send_sem=send, recv_sem=recv,
            device_id={axis: peer}, device_id_type=MESH,
        )

    def others(axis, count, mine, act):
        def turn(step, carry):
            act(lax.rem(mine + step, count))
            return carry

        lax.fori_loop(1, count, turn, 0)

    def load(kind):
        src, dst = ((s2t_h, s2t), (s1_h, s1), (cr_h, cr), (cs_h, cs))[kind]
        return pltpu.make_async_copy(src, dst, in_sem.at[kind])

    for kind in range(4):
        load(kind).start()

    barrier = pltpu.get_barrier_semaphore()

    def greet(axis):
        def act(peer):
            pl.semaphore_signal(barrier, inc=1, device_id={axis: peer}, device_id_type=MESH)

        return act

    others("tm", n_tm, tm, greet("tm"))
    others("items", n_it, it, greet("items"))
    pl.semaphore_wait(barrier, n_tm + n_it - 2)

    def to_next(chunk):
        cut = pl.ds(chunk * size, size)
        return remote(
            packed_h.at[cut], from_left.at[cut], left_send.at[chunk], left_recv.at[chunk],
            "tm", jnp.minimum(tm + 1, n_tm - 1),
        )

    def to_previous(chunk):
        cut = pl.ds(chunk * size, size)
        return remote(
            gpack.at[cut], from_right_h.at[cut], right_send.at[chunk], right_recv.at[chunk],
            "tm", jnp.maximum(tm - 1, 0),
        )

    def start_to_next(chunk):
        @pl.when((chunk < plan.parts) & jnp.logical_not(last))
        def _():
            to_next(chunk).start()

    for chunk in range(plan.out[0]):
        start_to_next(chunk)

    def arrived(place):
        def take(chunk, carry):
            @pl.when(jnp.logical_not(first))
            def _():
                to_next(chunk).wait_recv()
                staged[pl.ds(pl.multiple_of(frames + chunk * size, 8), size)] = from_left[
                    pl.ds(pl.multiple_of(chunk * size, 8), size)]

            return carry

        for k in range(items):
            low_end, high_end = (plan.arrive[k - 1] if k else 0), plan.arrive[k]
            if high_end > low_end:
                @pl.when(place == k)
                def _():
                    lax.fori_loop(low_end, high_end, take, 0)

    def send_back(low_end, high_end):
        def put(chunk, carry):
            def turn(block, carry):
                block = chunk * (size // GROUP) + block
                source = pack[block // LANES, block % LANES] * GROUP
                gpack[pl.ds(pl.multiple_of(block * GROUP, GROUP), GROUP)] = gbuf[
                    pl.ds(source, GROUP)]
                return carry

            lax.fori_loop(0, size // GROUP, turn, 0, unroll=True)
            pl.when(jnp.logical_not(first))(to_previous(chunk).start)
            return carry

        lax.fori_loop(low_end, high_end, put, 0)

    def bulk(index, point):
        sent = plan.out[0]
        for k, counts in enumerate(plan.out[1]):
            start = sent + sum(counts[:point])
            sent += sum(counts)
            if counts[point]:
                @pl.when(index == k)
                def _():
                    for chunk in range(start, start + counts[point]):
                        start_to_next(chunk)

        returned = 0
        for k, counts in plan.back.items():
            start = returned + sum(counts[:point])
            returned += sum(counts)
            if counts[point]:
                pl.when(index == k)(functools.partial(send_back, start, start + counts[point]))

    w_high, w_low = halves(w_in[...].T)
    w_t[0:chans] = w_high
    w_t[chans : 2 * chans] = w_low
    w_t[2 * chans :] = w_high
    wg[0:chans] = w_res[...] * gamma2[...]
    wg[chans:] = w_skip[...] * gamma2[...]
    high_part, low_part = halves(wg[...])
    wg_high[...] = high_part
    wg_low[...] = low_part
    cols[0] = column(gain1[...])
    cols[1] = column(gain2[...])
    for side, (weight, bias) in enumerate(((w_res, b_res), (w_skip, b_skip))):
        weight_sum = jnp.sum(wg[side * chans : (side + 1) * chans], axis=1, keepdims=True)
        shift = jnp.sum(weight[...] * beta2[...], axis=1, keepdims=True)
        cols[2 + side] = jnp.broadcast_to(weight_sum, (chans, LANES))
        cols[4 + side] = jnp.broadcast_to(shift, (chans, LANES)) + column(bias[...])
    x_acc[...] = jnp.zeros_like(x_acc)
    gw_acc[...] = jnp.zeros_like(gw_acc)
    gb_acc[...] = jnp.zeros_like(gb_acc)
    y_acc[...] = jnp.zeros_like(y_acc)
    gain_acc[...] = jnp.zeros_like(gain_acc)
    sums[...] = jnp.zeros_like(sums)
    turn_stats[1, tm] = jnp.zeros((8, LANES), F32)
    turn_stats[items + 1, tm] = jnp.zeros((8, LANES), F32)

    main = (frames - plan.tail) // CHUNK
    chunks = frames // CHUNK

    def by_lanes(act, init, merged):
        if merged:
            for b in range(blocks):
                init = act(b * LANES, init)
            return init
        return lax.fori_loop(0, blocks, lambda b, c: act(pl.multiple_of(b * LANES, LANES), c), init)

    def side_by_side(index, together, parts):
        low_end, high_end = together
        all_due = (index >= low_end) & (index <= high_end)

        @pl.when(all_due)
        def _():
            for _, _, act in parts:
                act(True)

        for first_turn, last_turn, act in parts:
            due = (index >= first_turn) & (index <= last_turn) & jnp.logical_not(all_due)
            pl.when(due)(functools.partial(act, False))

    def by_rows(act, init):
        def at(masked):
            return lambda c, carry: act(pl.multiple_of(c * CHUNK, CHUNK), masked, carry)

        carry = init
        for c in range(chunks):
            carry = act(c * CHUNK, c >= main, carry)
        return carry

    def valid_rows(row, count, length):
        index = lax.broadcasted_iota(jnp.int32, (count, LANES), 0)
        return (index + (base + row)) < length

    def lane_mask(length):
        return (lax.broadcasted_iota(jnp.int32, (8, frames), 1) + base) < length

    def add_sum(row, lanes, value):
        sums[pl.ds(row, 1), pl.ds(lanes, LANES)] += value

    def sums_of(kind):
        return stats if kind == 0 else turn_stats

    def send_stats(kind, index):
        mine = sums_of(kind).at[index, tm]
        others("tm", n_tm, tm, lambda peer: remote(
            mine, mine, stat_send.at[kind, index], stat_recv.at[kind, index], "tm", peer).start())

    def wait_stats(kind, index, sem):
        if n_tm > 1:
            block = sums_of(kind).at[index, pl.ds(0, n_tm - 1)]
            pltpu.make_async_copy(block, block, sem.at[kind, index]).wait()

    def read_stats(phase, item):
        if phase == 0:
            found = [stats[item, peer] for peer in range(n_tm)]
        else:
            rows = slice(4 * phase - 4, 4 * phase)
            found = [turn_stats[item + phase, peer, rows] for peer in range(n_tm)]
        total = found[0]
        for more in found[1:]:
            total = total + more
        total = jnp.sum(total, axis=1, keepdims=True)
        return [total[k : k + 1] for k in range(4)]

    def put_stats(phase, item, rows):
        for k in range(4):
            row = rows[k] if k < len(rows) else jnp.zeros((1, LANES), F32)
            if phase == 0:
                stats[item, tm, k : k + 1] = row
            else:
                at = 4 * phase - 4 + k
                turn_stats[item + phase, tm, at : at + 1] = row

    def halo_copies(kind, place, slot):
        if kind == 0:
            ends, halo = (edges.at[place, 0], edges.at[place, 1]), halo_m
        else:
            ends = (gconv.at[slot, pl.ds(wing, wing)], gconv.at[slot, pl.ds(frames, wing)])
            halo = halo_g
        down = remote(
            ends[0], halo.at[place, 1], halo_send.at[kind, place, 0],
            halo_recv.at[kind, place, 1], "tm", jnp.maximum(tm - 1, 0))
        up = remote(
            ends[1], halo.at[place, 0], halo_send.at[kind, place, 1],
            halo_recv.at[kind, place, 0], "tm", jnp.minimum(tm + 1, n_tm - 1))
        return down, up

    def send_halo(kind, place, slot=None):
        down, up = halo_copies(kind, place, slot)
        pl.when(jnp.logical_not(first))(down.start)
        pl.when(jnp.logical_not(last))(up.start)

    def wait_halo(kind, place, slot=None):
        down, up = halo_copies(kind, place, slot)

        @pl.when(jnp.logical_not(first))
        def _():
            down.wait_send()
            up.wait_recv()

        @pl.when(jnp.logical_not(last))
        def _():
            up.wait_send()
            down.wait_recv()

    def mix(place):
        slot = lax.rem(place, 5)
        item = order[place]
        before = staged[pl.ds(window[place] * GROUP, frames)]
        cat[0:frames] = jnp.where(first, 0.0, before)
        cat[frames:] = s2t[place]
        moved = cat[pl.ds(frames - offs[place], frames), :].T
        moved_s[slot] = moved
        mixed = wide(cols[0], frames) * s1[item] + wide(cols[1], frames) * moved
        mixed = jnp.where(lane_mask(lens[place])[0:1], mixed, 0.0)
        mixed_s[place] = mixed
        for side, row in enumerate((0, frames - wing)):
            near = cat[pl.ds(frames + row - offs[place], wing), :]
            block = 0 if side == 0 else frames - LANES
            turned = s1[item, :, block : block + LANES].T[row - block : row - block + wing]
            ends = gain1[...] * turned + gain2[...] * near
            edges[place, side] = jnp.where(valid_rows(row, wing, lens[place]), ends, 0.0)
        mix_high, mix_low = halves(mixed)
        mcat[slot, 0:chans] = mix_high
        mcat[slot, chans:] = mix_low

    def mix_product(place):
        slot = lax.rem(place, 5)
        left = jnp.concatenate([mcat[slot, 0:chans], mcat[slot]], axis=0)
        pre_raw[...] = dot(left, w_t[...], 0, 0)

    def edge_product(place):
        end_high, end_low = halves(halo_m[place].reshape(2 * wing, chans))
        left = jnp.concatenate([end_high, end_high, end_low], axis=1)
        x = dot(left, w_t[...], 1, 0) + b_in[...]
        half = jnp.tanh(0.5 * x)
        edge_act[...] = jnp.maximum(x, slope1[...] * x) - (1.0 - slope1[...]) * jnp.log(
            0.5 + 0.5 * jnp.abs(half))

    def phase_a(place, merged):
        slot = lax.rem(place, 4)
        length = lens[place]

        def lanes_step(lanes, carry):
            cut = pl.ds(lanes, LANES)
            bias, slope = b_in[:, cut], slope1[:, cut]

            def rows_step(row, masked, carry):
                rows = pl.ds(row, CHUNK)
                x = pre_raw[rows, cut] + bias
                half = jnp.tanh(0.5 * x)
                act = jnp.maximum(x, slope * x) - (1.0 - slope) * jnp.log(
                    0.5 + 0.5 * jnp.abs(half))
                pre1[slot, rows, cut] = x
                a1[slot, pl.ds(row + wing, CHUNK), cut] = act
                if masked:
                    act = jnp.where(valid_rows(row, CHUNK, length), act, 0.0)
                return carry[0] + fold_rows(act), carry[1] + fold_rows(act * act)

            return by_rows(rows_step, carry)

        zero = jnp.zeros((8, LANES), F32)
        carry = by_lanes(lanes_step, (zero, zero), merged)
        put_stats(0, place, [jnp.sum(c, axis=0, keepdims=True) for c in carry])

    def scales(totals, length):
        count = jnp.float32(units) * length.astype(F32)
        mean = totals[0] / count
        inverse = lax.rsqrt(totals[1] / count - mean * mean + EPS)
        return mean, inverse, count

    def before_b(place):
        slot = lax.rem(place, 4)
        length = lens[place]
        mean, inverse, _ = scales(read_stats(0, place), length)
        scale = gamma1[...] * inverse
        shift = beta1[...] - scale * mean
        outside = mean - beta1[...] / scale
        taps = [tap_rows[k : k + 1] for k in range(3)]
        coef[0:1] = taps[0] * scale
        coef[1:2] = taps[1] * scale
        coef[2:3] = taps[2] * scale
        coef[3:4] = b_depth[...] + shift * (taps[0] + taps[1] + taps[2])
        a1[slot, 0:wing] = jnp.where(first, outside, edge_act[0:wing])
        after = (lax.broadcasted_iota(jnp.int32, (wing, units), 0) + (base + frames)) < length
        a1[slot, frames + wing :] = jnp.where(after, edge_act[wing:], outside)


        @pl.when(last)
        def _():
            for row in range(frames - plan.tail, frames, CHUNK):
                keep = wide(valid_rows(row, CHUNK, length).astype(F32), units) > 0.5
                rows = slice(row + wing, row + wing + CHUNK)
                a1[slot, rows] = jnp.where(keep, a1[slot, rows], outside)

    def phase_b(place, merged):
        slot = lax.rem(place, 4)
        pair = lax.rem(place, 2)
        length = lens[place]

        def lanes_step(lanes, carry):
            cut = pl.ds(lanes, LANES)
            slope = slope2[:, cut]
            w0, w1, w2, const = (coef[k : k + 1, cut] for k in range(4))

            def rows_step(row, masked, carry):
                rows = pl.ds(row, CHUNK)
                x = const + w0 * a1[slot, rows, cut]
                x += w1 * a1[slot, pl.ds(row + wing, CHUNK), cut]
                x += w2 * a1[slot, pl.ds(row + 2 * wing, CHUNK), cut]
                half = jnp.tanh(0.5 * x)
                act = jnp.maximum(x, slope * x) - (1.0 - slope) * jnp.log(
                    0.5 + 0.5 * jnp.abs(half))
                conv[pair, rows, cut] = x
                act2[pair, rows, cut] = act
                d2[pair, rows, cut] = (0.5 + 0.5 * slope) + (0.5 - 0.5 * slope) * half
                act_high, act_low = halves(act)
                high[place, rows, cut] = act_high
                low[place, rows, cut] = act_low
                if masked:
                    act = jnp.where(valid_rows(row, CHUNK, length), act, 0.0)
                return carry[0] + fold_rows(act), carry[1] + fold_rows(act * act)

            return by_rows(rows_step, carry)

        zero = jnp.zeros((8, LANES), F32)
        carry = by_lanes(lanes_step, (zero, zero), merged)
        act_sums[0:1] = jnp.sum(carry[0], axis=0, keepdims=True)
        act_sums[1:2] = jnp.sum(carry[1], axis=0, keepdims=True)

    def cotangents(place):
        item = order[place]
        pair = lax.rem(place, 2)
        keep = lane_mask(lens[place])[0:1]
        in_sum = None
        for side, source in enumerate((cr, cs)):
            cot = jnp.where(keep, source[item], 0.0)
            cot_high, cot_low = halves(cot)
            gcat[side * chans : (side + 1) * chans] = cot_high
            gcat[(2 + side) * chans : (3 + side) * chans] = cot_low
            partial = fold_lanes(cot)
            rows = pl.ds(side * chans, chans)
            y_acc[1 + pair, rows] = partial
            gb_acc[rows] += partial
            by_weight = cols[2 + side] * partial
            in_sum = by_weight if in_sum is None else in_sum + by_weight
        act_sums[2:3] = jnp.sum(in_sum, axis=0, keepdims=True)

    def products(place):
        cot_high, cot_low = gcat[0 : 2 * chans], gcat[2 * chans :]
        act_h, act_l = high[place], low[place]
        left = jnp.concatenate([cot_high, cot_high, cot_low], axis=1)
        found = dot(left, jnp.concatenate([act_h, act_l, act_h], axis=0), 1, 0)
        grad_a[...] = found
        cross = jnp.sum(fold_lanes(fold_rows(wg[...] * found)), axis=0, keepdims=True)
        put_stats(1, place, (act_sums[0:1], act_sums[1:2], act_sums[2:3], cross))

    def outputs(place):
        pair = lax.rem(place, 2)
        act_h, act_l = high[place], low[place]
        left = jnp.concatenate([wg_high[...], wg_high[...], wg_low[...]], axis=1)
        raw = dot(left, jnp.concatenate([act_h, act_l, act_h], axis=1), 1, 1)
        keep = lane_mask(lens[place])[0:1]
        inverse, by_mean = out_coef[place, 0:1, 0:1], out_coef[place, 1:2, 0:1]
        out = inverse * raw[0:chans] + wide(cols[4] - by_mean * cols[2], frames)
        out_res[pair] = jnp.where(keep, mixed_s[place] + out, 0.0)
        out = inverse * raw[chans:] + wide(cols[5] - by_mean * cols[3], frames)
        out_skip[pair] = jnp.where(keep, out, 0.0)

    def back_product():
        left = jnp.concatenate([gcat[...], gcat[0 : 2 * chans]], axis=0)
        right = jnp.concatenate([wg_high[...], wg_high[...], wg_low[...]], axis=0)
        e2[...] = dot(left, right, 0, 0)

    def before_c(place):
        length = lens[place]
        totals = read_stats(1, place)
        mean, inverse, count = scales(totals, length)
        sum_e, sum_ea = totals[2], totals[3]
        mean_e = sum_e / count
        mean_ex = inverse * (sum_ea - mean * sum_e) / count
        by_act = -inverse * inverse * mean_ex
        by_one = -inverse * mean_e - by_act * mean
        mean_1, inverse_1, _ = scales(read_stats(0, place), length)
        scale_1 = gamma1[...] * inverse_1
        coef[4:5] = scale_1
        coef[5:6] = beta1[...] - scale_1 * mean_1
        for row, value in ((10, by_act), (11, by_one), (12, inverse), (13, inverse * mean)):
            coef[row : row + 1] = jnp.broadcast_to(value, (1, units))
        out_coef[place, 0:1] = jnp.broadcast_to(inverse, (1, LANES))
        out_coef[place, 1:2] = jnp.broadcast_to(inverse * mean, (1, LANES))

    def phase_c(place, merged):
        slot = lax.rem(place, 4)
        pair = lax.rem(place, 2)
        length = lens[place]
        y_acc[0] += coef[13:14, 0:LANES] * y_acc[1 + pair]
        inverse = coef[12:13, 0:1]
        x_acc[...] += inverse * grad_a[...]
        edge_rows = min(frames, plan.tail + CHUNK)

        def lanes_step(lanes, carry):
            cut = pl.ds(lanes, LANES)
            by_a, by_1, inv_e = (coef[k : k + 1, cut] for k in (10, 11, 12))

            def rows_step(row, masked, carry):
                rows = pl.ds(row, CHUNK)
                middle = pl.ds(row + wing, CHUNK)
                behind = pl.ds(row + 2 * wing, CHUNK)
                act = act2[pair, rows, cut]
                g = inv_e * e2[rows, cut] + by_a * act + by_1
                if masked:
                    g = jnp.where(valid_rows(row, CHUNK, length), g, 0.0)
                gc = g * d2[pair, rows, cut]
                gconv[pair, middle, cut] = gc
                parts = (
                    g * (conv[pair, rows, cut] - act), gc, gc * a1[slot, rows, cut],
                    gc * a1[slot, middle, cut], gc * a1[slot, behind, cut],
                )
                return tuple(c + fold_rows(p) for c, p in zip(carry, parts))

            zero = jnp.zeros((8, LANES), F32)
            found = by_rows(rows_step, (zero,) * 5)
            slope_sum, total, n0, n1, n2 = (jnp.sum(f, axis=0, keepdims=True) for f in found)

            def edge_step(c, carry):
                row = c * CHUNK
                gc = gconv[pair, pl.ds(row + wing, CHUNK), cut]
                inside = valid_rows(row + wing, CHUNK, length)
                return carry + fold_rows(jnp.where(inside, 0.0, gc))

            late = zero
            for c in range((frames - edge_rows) // CHUNK, chunks):
                late = edge_step(c, late)
            late = jnp.sum(late, axis=0, keepdims=True)
            early = jnp.sum(gconv[pair, wing : 2 * wing, cut], axis=0, keepdims=True)
            early = jnp.where(first, early, 0.0)
            scale, shift = coef[4:5, cut], coef[5:6, cut]
            gains, bias = gamma1[:, cut], beta1[:, cut]
            reach = (total - early, total, total - late)
            by_beta = jnp.zeros((1, LANES), F32)
            by_gamma = jnp.zeros((1, LANES), F32)
            for k, (n_k, b_k) in enumerate(zip((n0, n1, n2), reach)):
                tap = tap_rows[k : k + 1, cut]
                n_k = scale * n_k + shift * total
                add_sum(TAP + k, lanes, n_k)
                by_beta += tap * b_k
                by_gamma += tap * (n_k - bias * b_k)
            add_sum(SLOPE_TWO, lanes, slope_sum)
            add_sum(B_DEPTH, lanes, total)
            add_sum(BETA_ONE, lanes, by_beta)
            add_sum(GAMMA_ONE, lanes, by_gamma)
            return carry[0] + gains * by_beta, carry[1] + by_gamma

        zero = jnp.zeros((1, LANES), F32)
        put_stats(2, place, by_lanes(lanes_step, (zero, zero), merged))

    def out_copies(item):
        pair = lax.rem(item, 2)
        return (
            pltpu.make_async_copy(out_res.at[pair], res_h.at[item], out_sem.at[0, item]),
            pltpu.make_async_copy(out_skip.at[pair], skip_h.at[item], out_sem.at[1, item]),
        )

    def gs1_copy(item):
        return pltpu.make_async_copy(
            out_gs1.at[lax.rem(item, 2)], gs1_h.at[item], out_sem.at[2, item])

    def gmoved_copy(item):
        return pltpu.make_async_copy(
            gbuf.at[pl.ds(item * frames, frames)], gmoved_h.at[item], out_sem.at[3, item])

    def before_d(place):
        pair = lax.rem(place, 2)
        length = lens[place]
        totals = read_stats(2, place)
        mean, inverse, count = scales(read_stats(0, place), length)
        mean_e, mean_ex = totals[0] / count, totals[1] / count
        by_act = -inverse * inverse * mean_ex
        by_one = -inverse * mean_e - by_act * mean
        for k in range(3):
            coef[6 + k : 7 + k] = tap_rows[k : k + 1] * gamma1[...] * inverse
        for row, value in ((14, by_act), (15, by_one)):
            coef[row : row + 1] = jnp.broadcast_to(value, (1, units))
        gconv[pair, 0:wing] = jnp.where(first, 0.0, halo_g[place, 0])
        gconv[pair, frames + wing :] = jnp.where(last, 0.0, halo_g[place, 1])

    def phase_d(place, merged):
        slot = lax.rem(place, 4)
        pair = lax.rem(place, 2)
        length = lens[place]

        def lanes_step(lanes, carry):
            cut = pl.ds(lanes, LANES)
            slope = slope1[:, cut]
            by_a, by_1 = coef[14:15, cut], coef[15:16, cut]
            u0, u1, u2 = (coef[6 + k : 7 + k, cut] for k in range(3))

            def rows_step(row, masked, carry):
                rows = pl.ds(row, CHUNK)
                middle = pl.ds(row + wing, CHUNK)
                behind = pl.ds(row + 2 * wing, CHUNK)
                act, x = a1[slot, middle, cut], pre1[slot, rows, cut]
                g = by_a * act + by_1 + u0 * gconv[pair, behind, cut]
                g += u1 * gconv[pair, middle, cut] + u2 * gconv[pair, rows, cut]
                if masked:
                    g = jnp.where(valid_rows(row, CHUNK, length), g, 0.0)
                half = jnp.tanh(0.5 * x)
                gp = g * ((0.5 + 0.5 * slope) + (0.5 - 0.5 * slope) * half)
                gp_h, gp_l = halves(gp)
                gp_high[rows, cut] = gp_h
                gp_low[rows, cut] = gp_l
                return carry[0] + fold_rows(g * (x - act)), carry[1] + fold_rows(gp)

            zero = jnp.zeros((8, LANES), F32)
            slope_sum, bias_sum = by_rows(rows_step, (zero, zero))
            add_sum(SLOPE_ONE, lanes, jnp.sum(slope_sum, axis=0, keepdims=True))
            add_sum(B_IN, lanes, jnp.sum(bias_sum, axis=0, keepdims=True))
            return carry

        by_lanes(lanes_step, 0, merged)

    def weight_product(place):
        slot = lax.rem(place, 5)
        g_h, g_l = gp_high[...], gp_low[...]
        gw_acc[...] += dot(mcat[slot], g_h, 1, 0)
        gw_acc[0:chans] += dot(mcat[slot, 0:chans], g_l, 1, 0)

    def mixture_gradient(place):
        slot = lax.rem(place, 5)
        pair = lax.rem(place, 2)
        item = order[place]
        both = dot(w_t[0 : 2 * chans], gp_high[...], 1, 1)
        g_mixed = both[0:chans] + both[chans:] + dot(w_t[0:chans], gp_low[...], 1, 1)
        g_mixed = jnp.where(lane_mask(lens[place])[0:1], cr[item] + g_mixed, 0.0)
        out_gs1[pair] = wide(cols[0], frames) * g_mixed
        gain_acc[0] += fold_lanes(g_mixed * s1[item])
        gain_acc[1] += fold_lanes(g_mixed * moved_s[slot])
        gbuf[pl.ds(pl.multiple_of(place * frames, 8), frames)] = (
            wide(cols[1], frames) * g_mixed).T

    big, small_part = plan.seg // n_it, plan.seg // n_it // n_tm

    def segment(seg):
        return seg * plan.seg, big, small_part

    def stage_copies(seg, stage):
        start, big, small = segment(seg)
        offset = start // n_it
        send, recv = ar_send.at[seg, stage], ar_recv.at[seg, stage]
        if stage == 0:
            return "items", n_it, it, lambda peer: remote(
                gall.at[pl.ds(start + peer * big, big)], rs_it.at[it, pl.ds(offset, big)],
                send, recv, "items", peer)
        if stage == 1:
            return "tm", n_tm, tm, lambda peer: remote(
                part.at[pl.ds(offset + peer * small, small)],
                rs_tm.at[tm, pl.ds(offset // n_tm, small)], send, recv, "tm", peer)
        if stage == 2:
            mine = quarter.at[pl.ds(offset + tm * small, small)]
            return "tm", n_tm, tm, lambda peer: remote(mine, mine, send, recv, "tm", peer)
        mine = done.at[pl.ds(start + it * big, big)]
        return "items", n_it, it, lambda peer: remote(mine, mine, send, recv, "items", peer)

    def stage_start(seg, stage):
        axis, count, mine, copy = stage_copies(seg, stage)
        others(axis, count, mine, lambda peer: copy(peer).start())

    def stage_wait(seg, stage, sem):
        start, big, small = segment(seg)
        count, rows = ((n_it, big), (n_tm, small), (n_tm, small), (n_it, big))[stage]
        if count > 1:
            block = gall.at[pl.ds(0, (count - 1) * rows)]
            pltpu.make_async_copy(block, block, sem.at[seg, stage]).wait()

    def added(ref, count, rows):
        total = ref[0, rows]
        for peer in range(1, count):
            total = total + ref[peer, rows]
        return total

    def stage_zero(seg):
        start, big, _ = segment(seg)
        rs_it[it, pl.ds(start // n_it, big)] = gall[pl.ds(start + it * big, big)]
        stage_start(seg, 0)

    def stage_one(seg):
        start, big, small = segment(seg)
        offset = start // n_it
        stage_wait(seg, 0, ar_recv)
        part[pl.ds(offset, big)] = added(rs_it, n_it, pl.ds(offset, big))
        rs_tm[tm, pl.ds(offset // n_tm, small)] = part[pl.ds(offset + tm * small, small)]
        stage_start(seg, 1)

    def stage_two(seg):
        start, big, small = segment(seg)
        offset = start // n_it
        stage_wait(seg, 1, ar_recv)
        quarter[pl.ds(offset + tm * small, small)] = added(
            rs_tm, n_tm, pl.ds(offset // n_tm, small))
        stage_start(seg, 2)

    def stage_three(seg):
        start, big, _ = segment(seg)
        offset = start // n_it
        stage_wait(seg, 2, ar_recv)
        done[pl.ds(start + it * big, big)] = quarter[pl.ds(offset, big)]
        stage_start(seg, 3)

    def weights_sum():
        for side, weight in enumerate((w_res, w_skip)):
            rows = slice(side * chans, (side + 1) * chans)
            ones = jnp.sum(gb_acc[rows], axis=1, keepdims=True)
            centred = x_acc[rows] - jnp.sum(y_acc[0, rows], axis=1, keepdims=True)
            grad = gamma2[...] * centred + beta2[...] * ones
            for b in range(blocks):
                gall[b * 2 * chans + side * chans : b * 2 * chans + (side + 1) * chans] = grad[
                    :, b * LANES : (b + 1) * LANES]
            sums[GAMMA_TWO : GAMMA_TWO + 1] += jnp.sum(
                weight[...] * centred, axis=0, keepdims=True)
            sums[BETA_TWO : BETA_TWO + 1] += jnp.sum(weight[...] * ones, axis=0, keepdims=True)
            sums[NARROW : NARROW + 1, (2 + side) * LANES : (3 + side) * LANES] = jnp.sum(
                gb_acc[rows].T, axis=0, keepdims=True)

    def input_weights_sum():
        start = plan.in_start
        grad = gw_acc[0:chans] + gw_acc[chans:]
        for b in range(blocks):
            gall[start + b * chans : start + (b + 1) * chans] = grad[
                :, b * LANES : (b + 1) * LANES]

    def narrow_sums():
        for side in range(2):
            sums[NARROW : NARROW + 1, side * LANES : (side + 1) * LANES] = jnp.sum(
                gain_acc[side].T, axis=0, keepdims=True)
        sums[SLOPE_ONE : SLOPE_ONE + 1] = sums[SLOPE_ONE : SLOPE_ONE + 1] / (1.0 - slope1[...])
        sums[SLOPE_TWO : SLOPE_TWO + 1] = sums[SLOPE_TWO : SLOPE_TWO + 1] / (1.0 - slope2[...])
        sums[GAMMA_ONE : GAMMA_ONE + 1] = sums[GAMMA_ONE : GAMMA_ONE + 1] / gamma1[...]
        for b in range(blocks):
            small[b * SUM_ROWS : (b + 1) * SUM_ROWS] = sums[:, b * LANES : (b + 1) * LANES]
        small_it[it] = small[...]

    narrow = plan.small // n_tm

    def small_copies(stage):
        send, recv = ar_send.at[plan.segs, stage], ar_recv.at[plan.segs, stage]
        if stage == 0:
            return "items", n_it, it, lambda peer: remote(
                small, small_it.at[it], send, recv, "items", peer)
        if stage == 1:
            return "tm", n_tm, tm, lambda peer: remote(
                small.at[pl.ds(peer * narrow, narrow)], small_tm.at[tm], send, recv, "tm", peer)
        mine = small_done.at[pl.ds(tm * narrow, narrow)]
        return "tm", n_tm, tm, lambda peer: remote(mine, mine, send, recv, "tm", peer)

    def small_start(stage):
        axis, count, mine, copy = small_copies(stage)
        others(axis, count, mine, lambda peer: copy(peer).start())

    def small_wait(stage, sem):
        count, rows = ((n_it, plan.small), (n_tm, narrow), (n_tm, narrow))[stage]
        if count > 1:
            block = gall.at[pl.ds(0, (count - 1) * rows)]
            pltpu.make_async_copy(block, block, sem.at[plan.segs, stage]).wait()

    def small_one():
        small_wait(0, ar_recv)
        small_wait(0, ar_send)
        total = small_it[0]
        for peer in range(1, n_it):
            total = total + small_it[peer]
        small[...] = total
        small_tm[tm] = small[pl.ds(tm * narrow, narrow)]
        small_start(1)

    def small_two():
        small_wait(1, ar_recv)
        total = small_tm[0]
        for peer in range(1, n_tm):
            total = total + small_tm[peer]
        small_done[pl.ds(tm * narrow, narrow)] = total
        small_start(2)

    load(0).wait()
    load(1).wait()
    arrived(0)
    mix(0)
    send_halo(0, 0)
    mix_product(0)
    load(2).wait()
    load(3).wait()
    end = items - 1

    def step(index, carry):
        def within(lag, back=0):
            return (index >= lag) & (index <= end + lag - back)

        pl.when(within(6))(lambda: gs1_copy(index - 6).wait())
        pl.when(within(1))(lambda: wait_halo(0, index - 1))
        side_by_side(index, (4, end), (
            (1, end + 1, lambda merged: edge_product(index - 1)),
            (0, end, lambda merged: phase_a(index, merged)),
            (4, end + 3, lambda merged: weight_product(index - 4)),
            (4, end + 3, lambda merged: mixture_gradient(index - 4)),
        ))

        @pl.when(within(0))
        def _():
            send_stats(0, index)

        @pl.when(index == end + 4)
        def _():
            weight_product(index - 4)
            input_weights_sum()
            for seg in range(plan.weight_segs, plan.segs):
                stage_zero(seg)
            mixture_gradient(index - 4)
            stage_one(0)

        @pl.when(within(4))
        def _():
            gs1_copy(index - 4).start()
            gmoved_copy(index - 4).start()

        bulk(index, 0)

        @pl.when(within(1))
        def _():
            wait_stats(0, index - 1, stat_recv)
            before_b(index - 1)

        side_by_side(index, (2, end + 1), (
            (1, end + 1, lambda merged: phase_b(index - 1, merged)),
            (2, end + 2, lambda merged: back_product()),
        ))
        bulk(index, 1)

        @pl.when(within(2))
        def _():
            wait_stats(1, index - 1, stat_recv)
            before_c(index - 2)

        pl.when(within(1))(lambda: cotangents(index - 1))
        side_by_side(index, (2, end + 1), (
            (2, end + 2, lambda merged: phase_c(index - 2, merged)),
            (1, end + 1, lambda merged: products(index - 1)),
        ))

        pl.when((index >= 1) & (index <= end + 2))(lambda: send_stats(1, index))

        @pl.when(within(2))
        def _():
            send_halo(1, index - 2, lax.rem(index, 2))

        @pl.when(index == end + 2)
        def _():
            weights_sum()
            for seg in range(plan.weight_segs):
                stage_zero(seg)

        bulk(index, 2)

        @pl.when(within(3))
        def _():
            wait_halo(1, index - 3, lax.rem(index + 1, 2))
            pl.when(index == end + 3)(lambda: wait_stats(1, index - 1, stat_recv))
            before_d(index - 3)

        @pl.when(index < end)
        def _():
            arrived(index + 1)
            mix(index + 1)
            send_halo(0, index + 1)

        side_by_side(index, (3, end - 1), (
            (3, end + 3, lambda merged: phase_d(index - 3, merged)),
            (0, end - 1, lambda merged: mix_product(index + 1)),
        ))
        bulk(index, 3)
        return carry

    lax.fori_loop(0, items + 4, step, 0)
    narrow_sums()
    small_start(0)

    def stages(acts):
        for act, *given in acts:
            act(*given)

    one, two, three = stage_one, stage_two, stage_three
    if items == 8 and plan.segs == 6:
        due = (
            ((one, 1),), ((one, 2),), ((one, 3),), ((two, 0),), ((one, 4), (two, 1)),
            ((one, 5),), ((two, 2), (small_one,)), ((two, 3),),
        )
        late = (
            (three, 0), (three, 1), (two, 4), (three, 2), (two, 5), (three, 3), (small_two,),
            (three, 4), (three, 5),
        )
    else:
        due = ((),) * items
        late = [(one, seg) for seg in range(1, plan.segs)] + [(small_one,)]
        late += [(two, seg) for seg in range(plan.segs)] + [(small_two,)]
        late += [(three, seg) for seg in range(plan.segs)]

    def turn(place, carry):
        @pl.when(place >= 2)
        def _():
            for copy in out_copies(place - 2):
                copy.wait()

        outputs(place)
        for copy in out_copies(place):
            copy.start()
        for k, acts in enumerate(due):
            if acts:
                pl.when(place == k)(functools.partial(stages, acts))
        start = sum(map(sum, plan.back.values()))
        each = (plan.parts - start) // items
        if each:
            send_back(start + place * each, start + place * each + each)
        return carry

    for place in range(max(0, items - 2), items):
        gs1_copy(place).wait()
    lax.fori_loop(0, items, turn, 0)
    stages(late)
    for seg in range(plan.segs):
        stage_wait(seg, 3, ar_recv)
    small_wait(2, ar_recv)
    total_copy = pltpu.make_async_copy(done, total_h, in_sem.at[0])
    total_copy.start()
    small_copy = pltpu.make_async_copy(small_done, small_h, in_sem.at[1])
    small_copy.start()

    def finish(item, carry):
        wait_stats(0, item, stat_send)
        wait_stats(1, item + 1, stat_send)
        gmoved_copy(item).wait()
        return carry

    def finish_chunk(chunk, carry):
        @pl.when(jnp.logical_not(first))
        def _():
            to_previous(chunk).wait_send()

        @pl.when(jnp.logical_not(last))
        def _():
            to_next(chunk).wait_send()
            to_previous(chunk).wait_recv()

        return carry

    lax.fori_loop(0, items, finish, 0)
    wait_stats(1, items + 1, stat_send)
    lax.fori_loop(0, plan.parts, finish_chunk, 0)
    for item in range(max(0, items - 2), items):
        for copy in out_copies(item):
            copy.wait()
    for seg in range(plan.segs):
        for stage in range(4):
            stage_wait(seg, stage, ar_send)
    small_wait(1, ar_send)
    small_wait(2, ar_send)
    total_copy.wait()
    small_copy.wait()


def prelude(plan):
    items, frames, chans = plan.items, plan.frames, plan.chans
    rows = items * frames
    groups = rows // GROUP
    table = (rounded(groups, LANES) // LANES, LANES)
    per_item = frames // GROUP

    def body(
        offs_in, lens_in, s2_h, s2t_h, packed_h, pack, order, offs, lens, window, window_back,
        which, s2, s2t, packed, lookup_v, lookup, held, in_sem, out_sem, table_sem, send, recv,
    ):
        n_it = plan.n_it
        it = lax.axis_index("items")
        load = pltpu.make_async_copy(s2_h, s2, in_sem)
        load.start()
        barrier = pltpu.get_barrier_semaphore()

        def peers(act):
            def turn(step, carry):
                act(lax.rem(it + step, n_it))
                return carry

            lax.fori_loop(1, n_it, turn, 0)

        def copy(peer):
            return pltpu.make_async_remote_copy(
                src_ref=held.at[it], dst_ref=held.at[it], send_sem=send, recv_sem=recv,
                device_id={"items": peer}, device_id_type=MESH)

        peers(lambda peer: pl.semaphore_signal(
            barrier, inc=1, device_id={"items": peer}, device_id_type=MESH))
        given = [offs_in[i] for i in range(items)]
        places = []
        for i in range(items):
            rank = jnp.int32(0)
            for j in range(items):
                if j != i:
                    before = given[j] <= given[i] if j < i else given[j] < given[i]
                    rank += jnp.where(before, 1, 0)
            places.append(jnp.where(rank % 2 == 0, rank // 2, items - 1 - rank // 2))
        starts, needs, end = [], [], jnp.int32(0)
        taken = []
        for k in range(items):
            here = [jnp.where(place == k, 1, 0) for place in places]
            item = sum(i * h for i, h in enumerate(here))
            offset = sum(given[i] * h for i, h in enumerate(here))
            taken.append(item)
            order[k] = item
            offs[k] = offset
            lens[k] = sum(lens_in[i] * h for i, h in enumerate(here))
            needs.append((offset + GROUP - 1) // GROUP)
            starts.append(end)
            end = end + needs[k]
            window[k] = end
        held[it] = jnp.full((1, LANES), end, jnp.int32)

        index = (
            lax.broadcasted_iota(jnp.int32, table, 0) * LANES
            + lax.broadcasted_iota(jnp.int32, table, 1))

        def looked_up(index, firsts):
            total, previous = index, jnp.int32(0)
            for k in range(items):
                shift = firsts[k] - starts[k]
                total = total + jnp.where(index >= starts[k], shift - previous, 0)
                previous = shift
            return jnp.minimum(total, groups - 1)

        lookup_v[...] = looked_up(
            index, [(k + 1) * per_item - needs[k] for k in range(items)])
        to_smem = pltpu.make_async_copy(lookup_v, lookup, table_sem)
        to_smem.start()
        load.wait()
        for k in range(items // 2):
            s2t[k * frames : (k + 1) * frames] = s2[taken[k]].T
        pl.semaphore_wait(barrier, n_it - 1)
        peers(lambda peer: copy(peer).start())
        for k in range(items // 2, items):
            s2t[k * frames : (k + 1) * frames] = s2[taken[k]].T
        to_smem.wait()
        own_out = pltpu.make_async_copy(s2t, s2t_h, out_sem.at[0])
        own_out.start()

        def turn(group, carry):
            source = lookup[group // LANES, group % LANES] * GROUP
            packed[pl.ds(pl.multiple_of(group * GROUP, GROUP), GROUP)] = s2t[
                pl.ds(source, GROUP)]
            return carry

        lax.fori_loop(0, groups, turn, 0, unroll=16)
        packed_out = pltpu.make_async_copy(packed, packed_h, out_sem.at[1])
        packed_out.start()

        if n_it > 1:
            block = held.at[pl.ds(0, n_it - 1)]
            pltpu.make_async_copy(block, block, recv).wait()
        most = held[0]
        for peer in range(1, n_it):
            most = jnp.maximum(most, held[peer])
        choice = jnp.zeros((1, LANES), jnp.int32)
        sent = jnp.full((1, LANES), plan.caps[0] // GROUP, jnp.int32)
        for low_cap, cap in zip(plan.caps[:-1], plan.caps[1:]):
            more = most * GROUP > low_cap
            choice += more.astype(jnp.int32)
            sent += jnp.where(more, (cap - low_cap) // GROUP, 0)
        which[0] = jnp.max(choice)
        base = jnp.max(sent) - end
        for k in range(items):
            window_back[k] = base + starts[k]
        back = looked_up(index - base, [jnp.int32(k * per_item) for k in range(items)])
        pack[...] = jnp.where(index < base, 0, back)
        own_out.wait()
        packed_out.wait()
        if n_it > 1:
            pltpu.make_async_copy(block, block, send).wait()

    smem = pl.BlockSpec(memory_space=pltpu.SMEM)
    hbm = pl.BlockSpec(memory_space=pl.ANY)
    short = jax.ShapeDtypeStruct((items,), jnp.int32)
    flat = jax.ShapeDtypeStruct((rows, chans), F32)
    sem = pltpu.SemaphoreType.DMA
    return pl.pallas_call(
        body,
        out_shape=(
            flat, flat, jax.ShapeDtypeStruct(table, jnp.int32), short, short, short, short, short,
            jax.ShapeDtypeStruct((1,), jnp.int32),
        ),
        in_specs=[smem, smem, hbm],
        out_specs=(hbm, hbm, pl.BlockSpec(memory_space=pltpu.VMEM)) + (smem,) * 6,
        scratch_shapes=[
            pltpu.VMEM((items, chans, frames), F32), pltpu.VMEM((rows, chans), F32),
            pltpu.VMEM((rows, chans), F32), pltpu.VMEM(table, jnp.int32),
            pltpu.SMEM(table, jnp.int32), pltpu.VMEM((plan.n_it, 1, LANES), jnp.int32),
            sem, sem((2,)), sem, sem, sem,
        ],
        compiler_params=pltpu.CompilerParams(
            collective_id=0, has_side_effects=True, vmem_limit_bytes=62 * 2**20),
        name="prelude",
    )


def finisher(plan, rows):
    items, frames, chans, units = plan.items, plan.frames, plan.chans, plan.units
    blocks = units // LANES

    def body(
        order, offs, window, gmoved_h, from_right_h, total_h, small_h, res_h, skip_h, gs1_h, *rest
    ):
        outs, scratch = rest[:20], rest[20:]
        cat, gs2, total, small, passed, in_sem, out_sem, pass_sem, total_sem = scratch
        out_res, out_skip, out_gs1, out_gs2 = outs[:4]
        last = lax.axis_index("tm") == plan.n_tm - 1
        def through(kind, item):
            src, dst = ((res_h, out_res), (skip_h, out_skip), (gs1_h, out_gs1))[kind]
            held = passed.at[kind, item]
            return (
                pltpu.make_async_copy(src.at[item], held, pass_sem.at[0, kind, item]),
                pltpu.make_async_copy(held, dst.at[order[item]], pass_sem.at[1, kind, item]),
            )

        def loads(item):
            start = pl.multiple_of(window[item] * GROUP, GROUP)
            return (
                pltpu.make_async_copy(
                    gmoved_h.at[item], cat.at[item, pl.ds(0, frames)], in_sem.at[0, item]),
                pltpu.make_async_copy(
                    from_right_h.at[pl.ds(start, frames)], cat.at[item, pl.ds(frames, frames)],
                    in_sem.at[1, item]),
            )

        def store(item):
            return pltpu.make_async_copy(gs2.at[item], out_gs2.at[order[item]], out_sem.at[item])

        def start(item, carry):
            for copy in loads(item):
                copy.start()
            for kind in range(3):
                through(kind, item)[0].start()
            return carry

        total_copy = pltpu.make_async_copy(total_h, total, total_sem.at[0])
        total_copy.start()
        small_copy = pltpu.make_async_copy(small_h, small, total_sem.at[1])
        small_copy.start()
        lax.fori_loop(0, items, start, 0)

        def turn(item, carry):
            for copy in loads(item):
                copy.wait()
            for kind in range(3):
                arriving, leaving = through(kind, item)
                arriving.wait()
                leaving.start()

            @pl.when(last)
            def _():
                cat[item, frames:] = jnp.zeros((frames, chans), F32)

            gs2[item] = cat[item, pl.ds(offs[item], frames), :].T
            store(item).start()
            return carry

        lax.fori_loop(0, items, turn, 0)
        total_copy.wait()
        small_copy.wait()
        (
            gain_1, gain_2, g_in, gb_in, g_slope1, g_gamma1, g_beta1, g_taps, gb_depth, g_slope2,
            g_gamma2, g_beta2, g_res, gb_res, g_skip, gb_skip,
        ) = outs[4:]
        start_in = plan.in_start
        for b in range(blocks):
            cut = slice(b * LANES, (b + 1) * LANES)
            g_res[:, cut] = total[2 * b * chans : (2 * b + 1) * chans]
            g_skip[:, cut] = total[(2 * b + 1) * chans : (2 * b + 2) * chans]
            g_in[cut] = total[start_in + b * chans : start_in + (b + 1) * chans].T
            sums = small[b * SUM_ROWS : (b + 1) * SUM_ROWS]
            for out, row in (
                (gb_in, B_IN), (g_slope1, SLOPE_ONE), (g_gamma1, GAMMA_ONE), (g_beta1, BETA_ONE),
                (gb_depth, B_DEPTH), (g_slope2, SLOPE_TWO), (g_gamma2, GAMMA_TWO),
                (g_beta2, BETA_TWO),
            ):
                out[:, cut] = sums[row : row + 1]
            g_taps[:, cut] = sums[TAP : TAP + 3]
            (gain_1, gain_2, gb_res, gb_skip)[b][...] = sums[NARROW : NARROW + 1]

        def end(item, carry):
            store(item).wait()
            for kind in range(3):
                through(kind, item)[1].wait()
            return carry

        lax.fori_loop(0, items, end, 0)

    smem = pl.BlockSpec(memory_space=pltpu.SMEM)
    hbm = pl.BlockSpec(memory_space=pl.ANY)
    vmem = pl.BlockSpec(memory_space=pltpu.VMEM)
    big = jax.ShapeDtypeStruct((items, chans, frames), F32)

    def array(*shape):
        return jax.ShapeDtypeStruct(shape, F32)

    narrow, per_unit = array(1, chans), array(1, units)
    sem = pltpu.SemaphoreType.DMA
    return pl.pallas_call(
        body,
        out_shape=(big,) * 4 + (
            narrow, narrow, array(units, chans), per_unit, per_unit, per_unit, per_unit,
            array(3, units), per_unit, per_unit, per_unit, per_unit, array(chans, units), narrow,
            array(chans, units), narrow,
        ),
        in_specs=[smem] * 3 + [hbm] * 7,
        out_specs=(hbm,) * 4 + (vmem,) * 16,
        scratch_shapes=[
            pltpu.VMEM((items, 2 * frames, chans), F32), pltpu.VMEM((items, chans, frames), F32),
            pltpu.VMEM((rows, LANES), F32), pltpu.VMEM((plan.small, LANES), F32),
            pltpu.VMEM((3, items, chans, frames), F32),
            sem((2, items)), sem((items,)), sem((2, 3, items)), sem((2,)),
        ],
        compiler_params=pltpu.CompilerParams(vmem_limit_bytes=62 * 2**20),
        name="finisher",
    )


def per_device(
    mesh, source_one, source_two, offsets, lengths, gain_one, gain_two, w_in, b_in, slope_one,
    first_norm_gain, first_norm_bias, depthwise_weight, depthwise_bias, slope_two,
    second_norm_gain, second_norm_bias, w_res, b_res, w_skip, b_skip, cot_res, cot_skip,
):
    items, chans, frames = source_one.shape
    units = w_in.shape[0]
    plan = Plan(mesh, items, chans, frames, units)
    n_tm, n_it, wing = plan.n_tm, plan.n_it, DILATION_RATE
    full = items * frames
    s2t, packed, pack, order, offs, lens, window, window_back, which = prelude(plan)(
        offsets, lengths, source_two)

    def row(value):
        return value.reshape(1, -1)

    smem = pl.BlockSpec(memory_space=pltpu.SMEM)
    hbm = pl.BlockSpec(memory_space=pl.ANY)
    vmem = pl.BlockSpec(memory_space=pltpu.VMEM)
    rows = plan.segs * plan.seg

    def floats(*shape):
        return pltpu.VMEM(shape, F32)

    def shorts(*shape):
        return pltpu.VMEM(shape, BF16)

    big = jax.ShapeDtypeStruct((items, chans, frames), F32)
    sem = pltpu.SemaphoreType.DMA
    def block(sent, index):
        return pl.pallas_call(
            functools.partial(kernel, plan, sent),
            out_shape=(
                big, big, big, jax.ShapeDtypeStruct((items, frames, chans), F32),
                jax.ShapeDtypeStruct((full + frames, chans), F32),
                jax.ShapeDtypeStruct((rows, LANES), F32),
                jax.ShapeDtypeStruct((plan.small, LANES), F32),
            ),
            in_specs=[smem] * 5 + [hbm] * 5 + [vmem] * 16,
            out_specs=[hbm] * 7,
            scratch_shapes=[
                floats(items, chans, frames), floats(items, frames, chans),
                floats(items, chans, frames), floats(items, chans, frames),
                floats(sent, chans), floats(frames + sent, chans), floats(full, chans),
                floats(sent, chans),
                floats(2, chans, frames), floats(2, chans, frames), floats(2 * frames, chans),
                floats(5, chans, frames), floats(items, chans, frames),
                shorts(5, 2 * chans, frames),
                floats(frames, units), floats(4, frames + 2 * wing, units),
                floats(4, frames, units),
                floats(2, frames, units), floats(2, frames, units), floats(2, frames, units),
                floats(frames, units), shorts(items, frames, units),
                shorts(items, frames, units), floats(2 * chans, units),
                floats(2, frames + 2 * wing, units), shorts(frames, units),
                shorts(frames, units), shorts(4 * chans, frames),
                floats(items, 2, wing, chans), floats(items, 2, wing, chans),
                floats(2 * wing, units), floats(items, 2, wing, units),
                floats(items, n_tm, 4, LANES), floats(items + 2, n_tm, 8, LANES), floats(8, LANES), floats(16, units),
                floats(items, 2, LANES),
                shorts(3 * chans, units), shorts(2 * chans, units), shorts(2 * chans, units),
                floats(2 * chans, units), floats(6, chans, LANES),
                floats(2 * chans, units), floats(2 * chans, units),
                floats(2 * chans, LANES), floats(3, 2 * chans, LANES), floats(2, chans, LANES),
                floats(SUM_ROWS, units),
                floats(rows, LANES), floats(n_it, rows // n_it, LANES),
                floats(rows // n_it, LANES),
                floats(n_tm, rows // n_it // n_tm, LANES), floats(rows // n_it, LANES),
                floats(rows, LANES),
                floats(plan.small, LANES), floats(n_it, plan.small, LANES),
                floats(n_tm, plan.small // n_tm, LANES), floats(plan.small, LANES),
                sem((4,)), sem((4, items)), sem((plan.parts,)), sem((plan.parts,)),
                sem((plan.parts,)), sem((plan.parts,)), sem((2, items, 2)), sem((2, items, 2)),
                sem((2, items + 2)), sem((2, items + 2)), sem((plan.segs + 1, 4)),
                sem((plan.segs + 1, 4)),
            ],
            compiler_params=pltpu.CompilerParams(
                collective_id=1 + index, has_side_effects=True,
                vmem_limit_bytes=63 * 2**20),
            name="tcn_block",
        )

    branches = [block(sent, index) for index, sent in enumerate(plan.caps)]
    res, skip, gs1, gmoved, from_right, total, narrow = lax.switch(
        which[0], branches,
        order, offs, lens, window, pack, source_one, s2t.reshape(items, frames, chans), packed,
        cot_res, cot_skip,
        row(gain_one), row(gain_two), w_in, row(b_in), row(slope_one), row(first_norm_gain),
        row(first_norm_bias), depthwise_weight.T, row(depthwise_bias), row(slope_two),
        row(second_norm_gain), row(second_norm_bias), w_res, row(b_res), w_skip, row(b_skip),
    )
    outs = list(finisher(plan, rows)(
        order, offs, window_back, gmoved, from_right, total, narrow, res, skip, gs1))
    outs[11] = outs[11].T
    return tuple(out.reshape(-1) if out.shape[0] == 1 else out for out in outs)


def solution(mesh):
    split = P("items", None, "tm")
    in_specs = (split, split, P("items"), P("items")) + (P(),) * 16 + (split, split)
    out_specs = (split,) * 4 + (P(),) * 16
    return jax.shard_map(
        functools.partial(per_device, mesh), mesh=mesh, in_specs=in_specs, out_specs=out_specs,
        check_vma=False,
    )
```

```python
import functools

import jax
import jax.numpy as jnp
from jax import lax
from jax.experimental import pallas as pl
from jax.experimental.pallas import tpu as pltpu
from jax.sharding import PartitionSpec as P

DILATION_RATE = 16
EPS = 1e-05
LANES = 128
F32 = jnp.float32
BF16 = jnp.bfloat16
MESH = pl.DeviceIdType.MESH
CHUNK = 64
GROUP = 16

B_IN, SLOPE_ONE, GAMMA_ONE, BETA_ONE, TAP, B_DEPTH, SLOPE_TWO, GAMMA_TWO, BETA_TWO, NARROW = (
    0, 1, 2, 3, 4, 7, 8, 9, 10, 11,
)
SUM_ROWS = 16


def halves(value):
    high = value.astype(BF16)
    return high, (value - high.astype(F32)).astype(BF16)


def dot(left, right, over_left, over_right):
    return lax.dot_general(
        left, right, (((over_left,), (over_right,)), ((), ())), preferred_element_type=F32
    )


def fold_rows(value):
    return jnp.sum(value.reshape(value.shape[0] // 8, 8, value.shape[1]), axis=0)


def fold_lanes(value):
    total = value[:, :LANES]
    for start in range(LANES, value.shape[1], LANES):
        total = total + value[:, start : start + LANES]
    return total


def column(row):
    return jnp.broadcast_to(row, (LANES, LANES)).T


def wide(tile, width):
    return jnp.concatenate([tile] * (width // LANES), axis=1)


def rounded(size, step):
    return -(-size // step) * step


class Plan:
    def __init__(self, mesh, items, chans, frames, units):
        self.n_tm = mesh.shape["tm"]
        self.n_it = mesh.shape["items"]
        self.items, self.chans, self.frames, self.units = items, chans, frames, units
        whole = frames * self.n_tm
        self.tail = min(frames, rounded(whole // 32, CHUNK))
        step = 8 * self.n_tm * self.n_it
        self.seg = step
        weight_rows, rows = 2 * chans * units // LANES, chans * units // LANES
        if step >= weight_rows + rows:
            self.weight_segs, self.segs, self.in_start = 0, 1, weight_rows
        else:
            self.weight_segs = -(-weight_rows // step)
            self.segs = self.weight_segs + -(-rows // step)
            self.in_start = self.weight_segs * step
        self.small = rounded(SUM_ROWS * units // LANES, 8 * self.n_tm)
        full = items * frames
        self.parts = 32
        self.caps = tuple(sorted({
            rounded(full * part // 16, GROUP * self.parts) for part in (9, 10, 11, 12, 16)}))
        if items == 8 and self.caps[0] >= 5 * frames:
            self.arrive = (4, 8, 12, 16, 23, 29, 32, 32)
            self.out = (
                12, ((1, 1, 1, 1), (1, 1, 1, 1), (2, 1, 1, 1), (2, 1, 2, 2)))
            self.back = {
                6: (2, 1, 2, 1), 7: (1, 1, 1, 1), 8: (1, 1, 1, 1), 9: (1, 1, 1, 1),
                10: (4, 2, 0, 0)}
        else:
            self.arrive = (self.parts,) * items
            self.out = (self.parts, ())
            self.back = {items + 3: (self.parts, 0, 0, 0)}


def kernel(plan, rows_sent, *refs):
    n_tm, n_it = plan.n_tm, plan.n_it
    items, chans, frames, units = plan.items, plan.chans, plan.frames, plan.units
    wing = DILATION_RATE
    blocks = units // LANES
    (
        order, offs, lens, window, pack, s1_h, s2t_h, packed_h, cr_h, cs_h,
        gain1, gain2, w_in, b_in, slope1, gamma1, beta1, tap_rows, b_depth, slope2, gamma2, beta2,
        w_res, b_res, w_skip, b_skip,
        res_h, skip_h, gs1_h, gmoved_h, from_right_h, total_h, small_h,
        s1, s2t, cr, cs, from_left, staged, gbuf, gpack, out_skip, out_gs1, cat,
        moved_s, mixed_s, mcat, pre_raw, a1, pre1, conv, act2, d2, e2, high, low, grad_a,
        gconv, gp_high, gp_low, gcat, edges, halo_m, edge_act, halo_g, stats, turn_stats, act_sums, coef, out_coef,
        w_t, wg_high, wg_low, wg, cols, x_acc, gw_acc, gb_acc, y_acc, gain_acc, sums,
        gall, rs_it, part, rs_tm, quarter, done, small, small_it, small_tm, small_done,
        in_sem, out_sem, left_send, left_recv, right_send, right_recv,
        halo_send, halo_recv, stat_send, stat_recv, ar_send, ar_recv,
    ) = refs
    size = rows_sent // plan.parts
    out_res = out_gs1
    tm = lax.axis_index("tm")
    it = lax.axis_index("items")
    first, last = tm == 0, tm == n_tm - 1
    base = tm * frames
    whole = frames * n_tm

    def remote(src, dst, send, recv, axis, peer):
        return pltpu.make_async_remote_copy(
            src_ref=src, dst_ref=dst, send_sem=send, recv_sem=recv,
            device_id={axis: peer}, device_id_type=MESH,
        )

    def others(axis, count, mine, act):
        def turn(step, carry):
            act(lax.rem(mine + step, count))
            return carry

        lax.fori_loop(1, count, turn, 0)

    def load(kind):
        src, dst = ((s2t_h, s2t), (s1_h, s1), (cr_h, cr), (cs_h, cs))[kind]
        return pltpu.make_async_copy(src, dst, in_sem.at[kind])

    for kind in range(4):
        load(kind).start()

    barrier = pltpu.get_barrier_semaphore()

    def greet(axis):
        def act(peer):
            pl.semaphore_signal(barrier, inc=1, device_id={axis: peer}, device_id_type=MESH)

        return act

    others("tm", n_tm, tm, greet("tm"))
    others("items", n_it, it, greet("items"))
    pl.semaphore_wait(barrier, n_tm + n_it - 2)

    def to_next(chunk):
        cut = pl.ds(chunk * size, size)
        return remote(
            packed_h.at[cut], from_left.at[cut], left_send.at[chunk], left_recv.at[chunk],
            "tm", jnp.minimum(tm + 1, n_tm - 1),
        )

    def to_previous(chunk):
        cut = pl.ds(chunk * size, size)
        return remote(
            gpack.at[cut], from_right_h.at[cut], right_send.at[chunk], right_recv.at[chunk],
            "tm", jnp.maximum(tm - 1, 0),
        )

    def start_to_next(chunk):
        @pl.when((chunk < plan.parts) & jnp.logical_not(last))
        def _():
            to_next(chunk).start()

    for chunk in range(plan.out[0]):
        start_to_next(chunk)

    def arrived(place):
        def take(chunk, carry):
            @pl.when(jnp.logical_not(first))
            def _():
                to_next(chunk).wait_recv()
                staged[pl.ds(pl.multiple_of(frames + chunk * size, 8), size)] = from_left[
                    pl.ds(pl.multiple_of(chunk * size, 8), size)]

            return carry

        for k in range(items):
            low_end, high_end = (plan.arrive[k - 1] if k else 0), plan.arrive[k]
            if high_end > low_end:
                @pl.when(place == k)
                def _():
                    lax.fori_loop(low_end, high_end, take, 0)

    def send_back(low_end, high_end):
        def put(chunk, carry):
            def turn(block, carry):
                block = chunk * (size // GROUP) + block
                source = pack[block // LANES, block % LANES] * GROUP
                gpack[pl.ds(pl.multiple_of(block * GROUP, GROUP), GROUP)] = gbuf[
                    pl.ds(source, GROUP)]
                return carry

            lax.fori_loop(0, size // GROUP, turn, 0, unroll=True)
            pl.when(jnp.logical_not(first))(to_previous(chunk).start)
            return carry

        lax.fori_loop(low_end, high_end, put, 0)

    def bulk(index, point):
        sent = plan.out[0]
        for k, counts in enumerate(plan.out[1]):
            start = sent + sum(counts[:point])
            sent += sum(counts)
            if counts[point]:
                @pl.when(index == k)
                def _():
                    for chunk in range(start, start + counts[point]):
                        start_to_next(chunk)

        returned = 0
        for k, counts in plan.back.items():
            start = returned + sum(counts[:point])
            returned += sum(counts)
            if counts[point]:
                pl.when(index == k)(functools.partial(send_back, start, start + counts[point]))

    w_high, w_low = halves(w_in[...].T)
    w_t[0:chans] = w_high
    w_t[chans : 2 * chans] = w_low
    w_t[2 * chans :] = w_high
    wg[0:chans] = w_res[...] * gamma2[...]
    wg[chans:] = w_skip[...] * gamma2[...]
    high_part, low_part = halves(wg[...])
    wg_high[...] = high_part
    wg_low[...] = low_part
    cols[0] = column(gain1[...])
    cols[1] = column(gain2[...])
    for side, (weight, bias) in enumerate(((w_res, b_res), (w_skip, b_skip))):
        weight_sum = jnp.sum(wg[side * chans : (side + 1) * chans], axis=1, keepdims=True)
        shift = jnp.sum(weight[...] * beta2[...], axis=1, keepdims=True)
        cols[2 + side] = jnp.broadcast_to(weight_sum, (chans, LANES))
        cols[4 + side] = jnp.broadcast_to(shift, (chans, LANES)) + column(bias[...])
    x_acc[...] = jnp.zeros_like(x_acc)
    gw_acc[...] = jnp.zeros_like(gw_acc)
    gb_acc[...] = jnp.zeros_like(gb_acc)
    y_acc[...] = jnp.zeros_like(y_acc)
    gain_acc[...] = jnp.zeros_like(gain_acc)
    sums[...] = jnp.zeros_like(sums)
    turn_stats[1, tm] = jnp.zeros((8, LANES), F32)
    turn_stats[items + 1, tm] = jnp.zeros((8, LANES), F32)

    main = (frames - plan.tail) // CHUNK
    chunks = frames // CHUNK

    def by_lanes(act, init, merged):
        if merged:
            for b in range(blocks):
                init = act(b * LANES, init)
            return init
        return lax.fori_loop(0, blocks, lambda b, c: act(pl.multiple_of(b * LANES, LANES), c), init)

    def side_by_side(index, together, parts):
        low_end, high_end = together
        all_due = (index >= low_end) & (index <= high_end)

        @pl.when(all_due)
        def _():
            for _, _, act in parts:
                act(True)

        for first_turn, last_turn, act in parts:
            due = (index >= first_turn) & (index <= last_turn) & jnp.logical_not(all_due)
            pl.when(due)(functools.partial(act, False))

    def by_rows(act, init):
        def at(masked):
            return lambda c, carry: act(pl.multiple_of(c * CHUNK, CHUNK), masked, carry)

        carry = init
        for c in range(chunks):
            carry = act(c * CHUNK, c >= main, carry)
        return carry

    def valid_rows(row, count, length):
        index = lax.broadcasted_iota(jnp.int32, (count, LANES), 0)
        return (index + (base + row)) < length

    def lane_mask(length):
        return (lax.broadcasted_iota(jnp.int32, (8, frames), 1) + base) < length

    def add_sum(row, lanes, value):
        sums[pl.ds(row, 1), pl.ds(lanes, LANES)] += value

    def sums_of(kind):
        return stats if kind == 0 else turn_stats

    def send_stats(kind, index):
        mine = sums_of(kind).at[index, tm]
        others("tm", n_tm, tm, lambda peer: remote(
            mine, mine, stat_send.at[kind, index], stat_recv.at[kind, index], "tm", peer).start())

    def wait_stats(kind, index, sem):
        if n_tm > 1:
            block = sums_of(kind).at[index, pl.ds(0, n_tm - 1)]
            pltpu.make_async_copy(block, block, sem.at[kind, index]).wait()

    def read_stats(phase, item):
        if phase == 0:
            found = [stats[item, peer] for peer in range(n_tm)]
        else:
            rows = slice(4 * phase - 4, 4 * phase)
            found = [turn_stats[item + phase, peer, rows] for peer in range(n_tm)]
        total = found[0]
        for more in found[1:]:
            total = total + more
        total = jnp.sum(total, axis=1, keepdims=True)
        return [total[k : k + 1] for k in range(4)]

    def put_stats(phase, item, rows):
        for k in range(4):
            row = rows[k] if k < len(rows) else jnp.zeros((1, LANES), F32)
            if phase == 0:
                stats[item, tm, k : k + 1] = row
            else:
                at = 4 * phase - 4 + k
                turn_stats[item + phase, tm, at : at + 1] = row

    def halo_copies(kind, place, slot):
        if kind == 0:
            ends, halo = (edges.at[place, 0], edges.at[place, 1]), halo_m
        else:
            ends = (gconv.at[slot, pl.ds(wing, wing)], gconv.at[slot, pl.ds(frames, wing)])
            halo = halo_g
        down = remote(
            ends[0], halo.at[place, 1], halo_send.at[kind, place, 0],
            halo_recv.at[kind, place, 1], "tm", jnp.maximum(tm - 1, 0))
        up = remote(
            ends[1], halo.at[place, 0], halo_send.at[kind, place, 1],
            halo_recv.at[kind, place, 0], "tm", jnp.minimum(tm + 1, n_tm - 1))
        return down, up

    def send_halo(kind, place, slot=None):
        down, up = halo_copies(kind, place, slot)
        pl.when(jnp.logical_not(first))(down.start)
        pl.when(jnp.logical_not(last))(up.start)

    def wait_halo(kind, place, slot=None):
        down, up = halo_copies(kind, place, slot)

        @pl.when(jnp.logical_not(first))
        def _():
            down.wait_send()
            up.wait_recv()

        @pl.when(jnp.logical_not(last))
        def _():
            up.wait_send()
            down.wait_recv()

    def mix(place):
        slot = lax.rem(place, 5)
        item = order[place]
        before = staged[pl.ds(window[place] * GROUP, frames)]
        cat[0:frames] = jnp.where(first, 0.0, before)
        cat[frames:] = s2t[place]
        moved = cat[pl.ds(frames - offs[place], frames), :].T
        moved_s[slot] = moved
        mixed = wide(cols[0], frames) * s1[item] + wide(cols[1], frames) * moved
        mixed = jnp.where(lane_mask(lens[place])[0:1], mixed, 0.0)
        mixed_s[place] = mixed
        for side, row in enumerate((0, frames - wing)):
            near = cat[pl.ds(frames + row - offs[place], wing), :]
            block = 0 if side == 0 else frames - LANES
            turned = s1[item, :, block : block + LANES].T[row - block : row - block + wing]
            ends = gain1[...] * turned + gain2[...] * near
            edges[place, side] = jnp.where(valid_rows(row, wing, lens[place]), ends, 0.0)
        mix_high, mix_low = halves(mixed)
        mcat[slot, 0:chans] = mix_high
        mcat[slot, chans:] = mix_low

    def mix_product(place):
        slot = lax.rem(place, 5)
        left = jnp.concatenate([mcat[slot, 0:chans], mcat[slot]], axis=0)
        pre_raw[...] = dot(left, w_t[...], 0, 0)

    def edge_product(place):
        end_high, end_low = halves(halo_m[place].reshape(2 * wing, chans))
        left = jnp.concatenate([end_high, end_high, end_low], axis=1)
        x = dot(left, w_t[...], 1, 0) + b_in[...]
        half = jnp.tanh(0.5 * x)
        edge_act[...] = jnp.maximum(x, slope1[...] * x) - (1.0 - slope1[...]) * jnp.log(
            0.5 + 0.5 * jnp.abs(half))

    def phase_a(place, merged):
        slot = lax.rem(place, 4)
        length = lens[place]

        def lanes_step(lanes, carry):
            cut = pl.ds(lanes, LANES)
            bias, slope = b_in[:, cut], slope1[:, cut]

            def rows_step(row, masked, carry):
                rows = pl.ds(row, CHUNK)
                x = pre_raw[rows, cut] + bias
                half = jnp.tanh(0.5 * x)
                act = jnp.maximum(x, slope * x) - (1.0 - slope) * jnp.log(
                    0.5 + 0.5 * jnp.abs(half))
                pre1[slot, rows, cut] = x
                a1[slot, pl.ds(row + wing, CHUNK), cut] = act
                if masked:
                    act = jnp.where(valid_rows(row, CHUNK, length), act, 0.0)
                return carry[0] + fold_rows(act), carry[1] + fold_rows(act * act)

            return by_rows(rows_step, carry)

        zero = jnp.zeros((8, LANES), F32)
        carry = by_lanes(lanes_step, (zero, zero), merged)
        put_stats(0, place, [jnp.sum(c, axis=0, keepdims=True) for c in carry])

    def scales(totals, length):
        count = jnp.float32(units) * length.astype(F32)
        mean = totals[0] / count
        inverse = lax.rsqrt(totals[1] / count - mean * mean + EPS)
        return mean, inverse, count

    def before_b(place):
        slot = lax.rem(place, 4)
        length = lens[place]
        mean, inverse, _ = scales(read_stats(0, place), length)
        scale = gamma1[...] * inverse
        shift = beta1[...] - scale * mean
        outside = mean - beta1[...] / scale
        taps = [tap_rows[k : k + 1] for k in range(3)]
        coef[0:1] = taps[0] * scale
        coef[1:2] = taps[1] * scale
        coef[2:3] = taps[2] * scale
        coef[3:4] = b_depth[...] + shift * (taps[0] + taps[1] + taps[2])
        a1[slot, 0:wing] = jnp.where(first, outside, edge_act[0:wing])
        after = (lax.broadcasted_iota(jnp.int32, (wing, units), 0) + (base + frames)) < length
        a1[slot, frames + wing :] = jnp.where(after, edge_act[wing:], outside)


        @pl.when(last)
        def _():
            for row in range(frames - plan.tail, frames, CHUNK):
                keep = wide(valid_rows(row, CHUNK, length).astype(F32), units) > 0.5
                rows = slice(row + wing, row + wing + CHUNK)
                a1[slot, rows] = jnp.where(keep, a1[slot, rows], outside)

    def phase_b(place, merged):
        slot = lax.rem(place, 4)
        pair = lax.rem(place, 2)
        length = lens[place]

        def lanes_step(lanes, carry):
            cut = pl.ds(lanes, LANES)
            slope = slope2[:, cut]
            w0, w1, w2, const = (coef[k : k + 1, cut] for k in range(4))

            def rows_step(row, masked, carry):
                rows = pl.ds(row, CHUNK)
                x = const + w0 * a1[slot, rows, cut]
                x += w1 * a1[slot, pl.ds(row + wing, CHUNK), cut]
                x += w2 * a1[slot, pl.ds(row + 2 * wing, CHUNK), cut]
                half = jnp.tanh(0.5 * x)
                act = jnp.maximum(x, slope * x) - (1.0 - slope) * jnp.log(
                    0.5 + 0.5 * jnp.abs(half))
                conv[pair, rows, cut] = x
                act2[pair, rows, cut] = act
                d2[pair, rows, cut] = (0.5 + 0.5 * slope) + (0.5 - 0.5 * slope) * half
                act_high, act_low = halves(act)
                high[place, rows, cut] = act_high
                low[place, rows, cut] = act_low
                if masked:
                    act = jnp.where(valid_rows(row, CHUNK, length), act, 0.0)
                return carry[0] + fold_rows(act), carry[1] + fold_rows(act * act)

            return by_rows(rows_step, carry)

        zero = jnp.zeros((8, LANES), F32)
        carry = by_lanes(lanes_step, (zero, zero), merged)
        act_sums[0:1] = jnp.sum(carry[0], axis=0, keepdims=True)
        act_sums[1:2] = jnp.sum(carry[1], axis=0, keepdims=True)

    def cotangents(place):
        item = order[place]
        pair = lax.rem(place, 2)
        keep = lane_mask(lens[place])[0:1]
        in_sum = None
        for side, source in enumerate((cr, cs)):
            cot = jnp.where(keep, source[item], 0.0)
            cot_high, cot_low = halves(cot)
            gcat[side * chans : (side + 1) * chans] = cot_high
            gcat[(2 + side) * chans : (3 + side) * chans] = cot_low
            partial = fold_lanes(cot)
            rows = pl.ds(side * chans, chans)
            y_acc[1 + pair, rows] = partial
            gb_acc[rows] += partial
            by_weight = cols[2 + side] * partial
            in_sum = by_weight if in_sum is None else in_sum + by_weight
        act_sums[2:3] = jnp.sum(in_sum, axis=0, keepdims=True)

    def products(place):
        cot_high, cot_low = gcat[0 : 2 * chans], gcat[2 * chans :]
        act_h, act_l = high[place], low[place]
        left = jnp.concatenate([cot_high, cot_high, cot_low], axis=1)
        found = dot(left, jnp.concatenate([act_h, act_l, act_h], axis=0), 1, 0)
        grad_a[...] = found
        cross = jnp.sum(fold_lanes(fold_rows(wg[...] * found)), axis=0, keepdims=True)
        put_stats(1, place, (act_sums[0:1], act_sums[1:2], act_sums[2:3], cross))

    def outputs(place):
        pair = lax.rem(place, 2)
        act_h, act_l = high[place], low[place]
        left = jnp.concatenate([wg_high[...], wg_high[...], wg_low[...]], axis=1)
        raw = dot(left, jnp.concatenate([act_h, act_l, act_h], axis=1), 1, 1)
        keep = lane_mask(lens[place])[0:1]
        inverse, by_mean = out_coef[place, 0:1, 0:1], out_coef[place, 1:2, 0:1]
        out = inverse * raw[0:chans] + wide(cols[4] - by_mean * cols[2], frames)
        out_res[pair] = jnp.where(keep, mixed_s[place] + out, 0.0)
        out = inverse * raw[chans:] + wide(cols[5] - by_mean * cols[3], frames)
        out_skip[pair] = jnp.where(keep, out, 0.0)

    def back_product():
        left = jnp.concatenate([gcat[...], gcat[0 : 2 * chans]], axis=0)
        right = jnp.concatenate([wg_high[...], wg_high[...], wg_low[...]], axis=0)
        e2[...] = dot(left, right, 0, 0)

    def before_c(place):
        length = lens[place]
        totals = read_stats(1, place)
        mean, inverse, count = scales(totals, length)
        sum_e, sum_ea = totals[2], totals[3]
        mean_e = sum_e / count
        mean_ex = inverse * (sum_ea - mean * sum_e) / count
        by_act = -inverse * inverse * mean_ex
        by_one = -inverse * mean_e - by_act * mean
        mean_1, inverse_1, _ = scales(read_stats(0, place), length)
        scale_1 = gamma1[...] * inverse_1
        coef[4:5] = scale_1
        coef[5:6] = beta1[...] - scale_1 * mean_1
        for row, value in ((10, by_act), (11, by_one), (12, inverse), (13, inverse * mean)):
            coef[row : row + 1] = jnp.broadcast_to(value, (1, units))
        out_coef[place, 0:1] = jnp.broadcast_to(inverse, (1, LANES))
        out_coef[place, 1:2] = jnp.broadcast_to(inverse * mean, (1, LANES))

    def phase_c(place, merged):
        slot = lax.rem(place, 4)
        pair = lax.rem(place, 2)
        length = lens[place]
        y_acc[0] += coef[13:14, 0:LANES] * y_acc[1 + pair]
        inverse = coef[12:13, 0:1]
        x_acc[...] += inverse * grad_a[...]
        edge_rows = min(frames, plan.tail + CHUNK)

        def lanes_step(lanes, carry):
            cut = pl.ds(lanes, LANES)
            by_a, by_1, inv_e = (coef[k : k + 1, cut] for k in (10, 11, 12))

            def rows_step(row, masked, carry):
                rows = pl.ds(row, CHUNK)
                middle = pl.ds(row + wing, CHUNK)
                behind = pl.ds(row + 2 * wing, CHUNK)
                act = act2[pair, rows, cut]
                g = inv_e * e2[rows, cut] + by_a * act + by_1
                if masked:
                    g = jnp.where(valid_rows(row, CHUNK, length), g, 0.0)
                gc = g * d2[pair, rows, cut]
                gconv[pair, middle, cut] = gc
                parts = (
                    g * (conv[pair, rows, cut] - act), gc, gc * a1[slot, rows, cut],
                    gc * a1[slot, middle, cut], gc * a1[slot, behind, cut],
                )
                return tuple(c + fold_rows(p) for c, p in zip(carry, parts))

            zero = jnp.zeros((8, LANES), F32)
            found = by_rows(rows_step, (zero,) * 5)
            slope_sum, total, n0, n1, n2 = (jnp.sum(f, axis=0, keepdims=True) for f in found)

            def edge_step(c, carry):
                row = c * CHUNK
                gc = gconv[pair, pl.ds(row + wing, CHUNK), cut]
                inside = valid_rows(row + wing, CHUNK, length)
                return carry + fold_rows(jnp.where(inside, 0.0, gc))

            late = zero
            for c in range((frames - edge_rows) // CHUNK, chunks):
                late = edge_step(c, late)
            late = jnp.sum(late, axis=0, keepdims=True)
            early = jnp.sum(gconv[pair, wing : 2 * wing, cut], axis=0, keepdims=True)
            early = jnp.where(first, early, 0.0)
            scale, shift = coef[4:5, cut], coef[5:6, cut]
            gains, bias = gamma1[:, cut], beta1[:, cut]
            reach = (total - early, total, total - late)
            by_beta = jnp.zeros((1, LANES), F32)
            by_gamma = jnp.zeros((1, LANES), F32)
            for k, (n_k, b_k) in enumerate(zip((n0, n1, n2), reach)):
                tap = tap_rows[k : k + 1, cut]
                n_k = scale * n_k + shift * total
                add_sum(TAP + k, lanes, n_k)
                by_beta += tap * b_k
                by_gamma += tap * (n_k - bias * b_k)
            add_sum(SLOPE_TWO, lanes, slope_sum)
            add_sum(B_DEPTH, lanes, total)
            add_sum(BETA_ONE, lanes, by_beta)
            add_sum(GAMMA_ONE, lanes, by_gamma)
            return carry[0] + gains * by_beta, carry[1] + by_gamma

        zero = jnp.zeros((1, LANES), F32)
        put_stats(2, place, by_lanes(lanes_step, (zero, zero), merged))

    def out_copies(item):
        pair = lax.rem(item, 2)
        return (
            pltpu.make_async_copy(out_res.at[pair], res_h.at[item], out_sem.at[0, item]),
            pltpu.make_async_copy(out_skip.at[pair], skip_h.at[item], out_sem.at[1, item]),
        )

    def gs1_copy(item):
        return pltpu.make_async_copy(
            out_gs1.at[lax.rem(item, 2)], gs1_h.at[item], out_sem.at[2, item])

    def gmoved_copy(item):
        return pltpu.make_async_copy(
            gbuf.at[pl.ds(item * frames, frames)], gmoved_h.at[item], out_sem.at[3, item])

    def before_d(place):
        pair = lax.rem(place, 2)
        length = lens[place]
        totals = read_stats(2, place)
        mean, inverse, count = scales(read_stats(0, place), length)
        mean_e, mean_ex = totals[0] / count, totals[1] / count
        by_act = -inverse * inverse * mean_ex
        by_one = -inverse * mean_e - by_act * mean
        for k in range(3):
            coef[6 + k : 7 + k] = tap_rows[k : k + 1] * gamma1[...] * inverse
        for row, value in ((14, by_act), (15, by_one)):
            coef[row : row + 1] = jnp.broadcast_to(value, (1, units))
        gconv[pair, 0:wing] = jnp.where(first, 0.0, halo_g[place, 0])
        gconv[pair, frames + wing :] = jnp.where(last, 0.0, halo_g[place, 1])

    def phase_d(place, merged):
        slot = lax.rem(place, 4)
        pair = lax.rem(place, 2)
        length = lens[place]

        def lanes_step(lanes, carry):
            cut = pl.ds(lanes, LANES)
            slope = slope1[:, cut]
            by_a, by_1 = coef[14:15, cut], coef[15:16, cut]
            u0, u1, u2 = (coef[6 + k : 7 + k, cut] for k in range(3))

            def rows_step(row, masked, carry):
                rows = pl.ds(row, CHUNK)
                middle = pl.ds(row + wing, CHUNK)
                behind = pl.ds(row + 2 * wing, CHUNK)
                act, x = a1[slot, middle, cut], pre1[slot, rows, cut]
                g = by_a * act + by_1 + u0 * gconv[pair, behind, cut]
                g += u1 * gconv[pair, middle, cut] + u2 * gconv[pair, rows, cut]
                if masked:
                    g = jnp.where(valid_rows(row, CHUNK, length), g, 0.0)
                half = jnp.tanh(0.5 * x)
                gp = g * ((0.5 + 0.5 * slope) + (0.5 - 0.5 * slope) * half)
                gp_h, gp_l = halves(gp)
                gp_high[rows, cut] = gp_h
                gp_low[rows, cut] = gp_l
                return carry[0] + fold_rows(g * (x - act)), carry[1] + fold_rows(gp)

            zero = jnp.zeros((8, LANES), F32)
            slope_sum, bias_sum = by_rows(rows_step, (zero, zero))
            add_sum(SLOPE_ONE, lanes, jnp.sum(slope_sum, axis=0, keepdims=True))
            add_sum(B_IN, lanes, jnp.sum(bias_sum, axis=0, keepdims=True))
            return carry

        by_lanes(lanes_step, 0, merged)

    def weight_product(place):
        slot = lax.rem(place, 5)
        g_h, g_l = gp_high[...], gp_low[...]
        gw_acc[...] += dot(mcat[slot], g_h, 1, 0)
        gw_acc[0:chans] += dot(mcat[slot, 0:chans], g_l, 1, 0)

    def mixture_gradient(place):
        slot = lax.rem(place, 5)
        pair = lax.rem(place, 2)
        item = order[place]
        both = dot(w_t[0 : 2 * chans], gp_high[...], 1, 1)
        g_mixed = both[0:chans] + both[chans:] + dot(w_t[0:chans], gp_low[...], 1, 1)
        g_mixed = jnp.where(lane_mask(lens[place])[0:1], cr[item] + g_mixed, 0.0)
        out_gs1[pair] = wide(cols[0], frames) * g_mixed
        gain_acc[0] += fold_lanes(g_mixed * s1[item])
        gain_acc[1] += fold_lanes(g_mixed * moved_s[slot])
        gbuf[pl.ds(pl.multiple_of(place * frames, 8), frames)] = (
            wide(cols[1], frames) * g_mixed).T

    big, small_part = plan.seg // n_it, plan.seg // n_it // n_tm

    def segment(seg):
        return seg * plan.seg, big, small_part

    def stage_copies(seg, stage):
        start, big, small = segment(seg)
        offset = start // n_it
        send, recv = ar_send.at[seg, stage], ar_recv.at[seg, stage]
        if stage == 0:
            return "items", n_it, it, lambda peer: remote(
                gall.at[pl.ds(start + peer * big, big)], rs_it.at[it, pl.ds(offset, big)],
                send, recv, "items", peer)
        if stage == 1:
            return "tm", n_tm, tm, lambda peer: remote(
                part.at[pl.ds(offset + peer * small, small)],
                rs_tm.at[tm, pl.ds(offset // n_tm, small)], send, recv, "tm", peer)
        if stage == 2:
            mine = quarter.at[pl.ds(offset + tm * small, small)]
            return "tm", n_tm, tm, lambda peer: remote(mine, mine, send, recv, "tm", peer)
        mine = done.at[pl.ds(start + it * big, big)]
        return "items", n_it, it, lambda peer: remote(mine, mine, send, recv, "items", peer)

    def stage_start(seg, stage):
        axis, count, mine, copy = stage_copies(seg, stage)
        others(axis, count, mine, lambda peer: copy(peer).start())

    def stage_wait(seg, stage, sem):
        start, big, small = segment(seg)
        count, rows = ((n_it, big), (n_tm, small), (n_tm, small), (n_it, big))[stage]
        if count > 1:
            block = gall.at[pl.ds(0, (count - 1) * rows)]
            pltpu.make_async_copy(block, block, sem.at[seg, stage]).wait()

    def added(ref, count, rows):
        total = ref[0, rows]
        for peer in range(1, count):
            total = total + ref[peer, rows]
        return total

    def stage_zero(seg):
        start, big, _ = segment(seg)
        rs_it[it, pl.ds(start // n_it, big)] = gall[pl.ds(start + it * big, big)]
        stage_start(seg, 0)

    def stage_one(seg):
        start, big, small = segment(seg)
        offset = start // n_it
        stage_wait(seg, 0, ar_recv)
        part[pl.ds(offset, big)] = added(rs_it, n_it, pl.ds(offset, big))
        rs_tm[tm, pl.ds(offset // n_tm, small)] = part[pl.ds(offset + tm * small, small)]
        stage_start(seg, 1)

    def stage_two(seg):
        start, big, small = segment(seg)
        offset = start // n_it
        stage_wait(seg, 1, ar_recv)
        quarter[pl.ds(offset + tm * small, small)] = added(
            rs_tm, n_tm, pl.ds(offset // n_tm, small))
        stage_start(seg, 2)

    def stage_three(seg):
        start, big, _ = segment(seg)
        offset = start // n_it
        stage_wait(seg, 2, ar_recv)
        done[pl.ds(start + it * big, big)] = quarter[pl.ds(offset, big)]
        stage_start(seg, 3)

    def weights_sum():
        for side, weight in enumerate((w_res, w_skip)):
            rows = slice(side * chans, (side + 1) * chans)
            ones = jnp.sum(gb_acc[rows], axis=1, keepdims=True)
            centred = x_acc[rows] - jnp.sum(y_acc[0, rows], axis=1, keepdims=True)
            grad = gamma2[...] * centred + beta2[...] * ones
            for b in range(blocks):
                gall[b * 2 * chans + side * chans : b * 2 * chans + (side + 1) * chans] = grad[
                    :, b * LANES : (b + 1) * LANES]
            sums[GAMMA_TWO : GAMMA_TWO + 1] += jnp.sum(
                weight[...] * centred, axis=0, keepdims=True)
            sums[BETA_TWO : BETA_TWO + 1] += jnp.sum(weight[...] * ones, axis=0, keepdims=True)
            sums[NARROW : NARROW + 1, (2 + side) * LANES : (3 + side) * LANES] = jnp.sum(
                gb_acc[rows].T, axis=0, keepdims=True)

    def input_weights_sum():
        start = plan.in_start
        grad = gw_acc[0:chans] + gw_acc[chans:]
        for b in range(blocks):
            gall[start + b * chans : start + (b + 1) * chans] = grad[
                :, b * LANES : (b + 1) * LANES]

    def narrow_sums():
        for side in range(2):
            sums[NARROW : NARROW + 1, side * LANES : (side + 1) * LANES] = jnp.sum(
                gain_acc[side].T, axis=0, keepdims=True)
        sums[SLOPE_ONE : SLOPE_ONE + 1] = sums[SLOPE_ONE : SLOPE_ONE + 1] / (1.0 - slope1[...])
        sums[SLOPE_TWO : SLOPE_TWO + 1] = sums[SLOPE_TWO : SLOPE_TWO + 1] / (1.0 - slope2[...])
        sums[GAMMA_ONE : GAMMA_ONE + 1] = sums[GAMMA_ONE : GAMMA_ONE + 1] / gamma1[...]
        for b in range(blocks):
            small[b * SUM_ROWS : (b + 1) * SUM_ROWS] = sums[:, b * LANES : (b + 1) * LANES]
        small_it[it] = small[...]

    narrow = plan.small // n_tm

    def small_copies(stage):
        send, recv = ar_send.at[plan.segs, stage], ar_recv.at[plan.segs, stage]
        if stage == 0:
            return "items", n_it, it, lambda peer: remote(
                small, small_it.at[it], send, recv, "items", peer)
        if stage == 1:
            return "tm", n_tm, tm, lambda peer: remote(
                small.at[pl.ds(peer * narrow, narrow)], small_tm.at[tm], send, recv, "tm", peer)
        mine = small_done.at[pl.ds(tm * narrow, narrow)]
        return "tm", n_tm, tm, lambda peer: remote(mine, mine, send, recv, "tm", peer)

    def small_start(stage):
        axis, count, mine, copy = small_copies(stage)
        others(axis, count, mine, lambda peer: copy(peer).start())

    def small_wait(stage, sem):
        count, rows = ((n_it, plan.small), (n_tm, narrow), (n_tm, narrow))[stage]
        if count > 1:
            block = gall.at[pl.ds(0, (count - 1) * rows)]
            pltpu.make_async_copy(block, block, sem.at[plan.segs, stage]).wait()

    def small_one():
        small_wait(0, ar_recv)
        small_wait(0, ar_send)
        total = small_it[0]
        for peer in range(1, n_it):
            total = total + small_it[peer]
        small[...] = total
        small_tm[tm] = small[pl.ds(tm * narrow, narrow)]
        small_start(1)

    def small_two():
        small_wait(1, ar_recv)
        total = small_tm[0]
        for peer in range(1, n_tm):
            total = total + small_tm[peer]
        small_done[pl.ds(tm * narrow, narrow)] = total
        small_start(2)

    load(0).wait()
    load(1).wait()
    arrived(0)
    mix(0)
    send_halo(0, 0)
    mix_product(0)
    load(2).wait()
    load(3).wait()
    end = items - 1

    def step(index, carry):
        def within(lag, back=0):
            return (index >= lag) & (index <= end + lag - back)

        pl.when(within(6))(lambda: gs1_copy(index - 6).wait())
        pl.when(within(1))(lambda: wait_halo(0, index - 1))
        side_by_side(index, (4, end), (
            (1, end + 1, lambda merged: edge_product(index - 1)),
            (0, end, lambda merged: phase_a(index, merged)),
            (4, end + 3, lambda merged: weight_product(index - 4)),
            (4, end + 3, lambda merged: mixture_gradient(index - 4)),
        ))

        @pl.when(within(0))
        def _():
            send_stats(0, index)

        @pl.when(index == end + 4)
        def _():
            weight_product(index - 4)
            input_weights_sum()
            for seg in range(plan.weight_segs, plan.segs):
                stage_zero(seg)
            mixture_gradient(index - 4)
            stage_one(0)

        @pl.when(within(4))
        def _():
            gs1_copy(index - 4).start()
            gmoved_copy(index - 4).start()

        bulk(index, 0)

        @pl.when(within(1))
        def _():
            wait_stats(0, index - 1, stat_recv)
            before_b(index - 1)

        side_by_side(index, (2, end + 1), (
            (1, end + 1, lambda merged: phase_b(index - 1, merged)),
            (2, end + 2, lambda merged: back_product()),
        ))
        bulk(index, 1)

        @pl.when(within(2))
        def _():
            wait_stats(1, index - 1, stat_recv)
            before_c(index - 2)

        pl.when(within(1))(lambda: cotangents(index - 1))
        side_by_side(index, (2, end + 1), (
            (2, end + 2, lambda merged: phase_c(index - 2, merged)),
            (1, end + 1, lambda merged: products(index - 1)),
        ))

        pl.when((index >= 1) & (index <= end + 2))(lambda: send_stats(1, index))

        @pl.when(within(2))
        def _():
            send_halo(1, index - 2, lax.rem(index, 2))

        @pl.when(index == end + 2)
        def _():
            weights_sum()
            for seg in range(plan.weight_segs):
                stage_zero(seg)

        bulk(index, 2)

        @pl.when(within(3))
        def _():
            wait_halo(1, index - 3, lax.rem(index + 1, 2))
            pl.when(index == end + 3)(lambda: wait_stats(1, index - 1, stat_recv))
            before_d(index - 3)

        @pl.when(index < end)
        def _():
            arrived(index + 1)
            mix(index + 1)
            send_halo(0, index + 1)

        side_by_side(index, (3, end - 1), (
            (3, end + 3, lambda merged: phase_d(index - 3, merged)),
            (0, end - 1, lambda merged: mix_product(index + 1)),
        ))
        bulk(index, 3)
        return carry

    lax.fori_loop(0, items + 4, step, 0)
    narrow_sums()
    small_start(0)

    def stages(acts):
        for act, *given in acts:
            act(*given)

    one, two, three = stage_one, stage_two, stage_three
    if items == 8 and plan.segs == 6:
        due = (
            ((one, 1),), ((one, 2),), ((one, 3),), ((two, 0),), ((one, 4), (two, 1)),
            ((one, 5),), ((two, 2), (small_one,)), ((two, 3),),
        )
        late = (
            (three, 0), (three, 1), (two, 4), (three, 2), (two, 5), (three, 3), (small_two,),
            (three, 4), (three, 5),
        )
    else:
        due = ((),) * items
        late = [(one, seg) for seg in range(1, plan.segs)] + [(small_one,)]
        late += [(two, seg) for seg in range(plan.segs)] + [(small_two,)]
        late += [(three, seg) for seg in range(plan.segs)]

    def turn(place, carry):
        @pl.when(place >= 2)
        def _():
            for copy in out_copies(place - 2):
                copy.wait()

        outputs(place)
        for copy in out_copies(place):
            copy.start()
        for k, acts in enumerate(due):
            if acts:
                pl.when(place == k)(functools.partial(stages, acts))
        start = sum(map(sum, plan.back.values()))
        each = (plan.parts - start) // items
        if each:
            send_back(start + place * each, start + place * each + each)
        return carry

    for place in range(max(0, items - 2), items):
        gs1_copy(place).wait()
    lax.fori_loop(0, items, turn, 0)
    stages(late)
    for seg in range(plan.segs):
        stage_wait(seg, 3, ar_recv)
    small_wait(2, ar_recv)
    total_copy = pltpu.make_async_copy(done, total_h, in_sem.at[0])
    total_copy.start()
    small_copy = pltpu.make_async_copy(small_done, small_h, in_sem.at[1])
    small_copy.start()

    def finish(item, carry):
        wait_stats(0, item, stat_send)
        wait_stats(1, item + 1, stat_send)
        gmoved_copy(item).wait()
        return carry

    def finish_chunk(chunk, carry):
        @pl.when(jnp.logical_not(first))
        def _():
            to_previous(chunk).wait_send()

        @pl.when(jnp.logical_not(last))
        def _():
            to_next(chunk).wait_send()
            to_previous(chunk).wait_recv()

        return carry

    lax.fori_loop(0, items, finish, 0)
    wait_stats(1, items + 1, stat_send)
    lax.fori_loop(0, plan.parts, finish_chunk, 0)
    for item in range(max(0, items - 2), items):
        for copy in out_copies(item):
            copy.wait()
    for seg in range(plan.segs):
        for stage in range(4):
            stage_wait(seg, stage, ar_send)
    small_wait(1, ar_send)
    small_wait(2, ar_send)
    total_copy.wait()
    small_copy.wait()


def prelude(plan):
    items, frames, chans = plan.items, plan.frames, plan.chans
    rows = items * frames
    groups = rows // GROUP
    table = (rounded(groups, LANES) // LANES, LANES)
    per_item = frames // GROUP

    def body(
        offs_in, lens_in, s2_h, s2t_h, packed_h, pack, order, offs, lens, window, window_back,
        which, s2, s2t, packed, lookup_v, lookup, held, in_sem, out_sem, table_sem, send, recv,
    ):
        n_it = plan.n_it
        it = lax.axis_index("items")
        load = pltpu.make_async_copy(s2_h, s2, in_sem)
        load.start()
        barrier = pltpu.get_barrier_semaphore()

        def peers(act):
            def turn(step, carry):
                act(lax.rem(it + step, n_it))
                return carry

            lax.fori_loop(1, n_it, turn, 0)

        def copy(peer):
            return pltpu.make_async_remote_copy(
                src_ref=held.at[it], dst_ref=held.at[it], send_sem=send, recv_sem=recv,
                device_id={"items": peer}, device_id_type=MESH)

        peers(lambda peer: pl.semaphore_signal(
            barrier, inc=1, device_id={"items": peer}, device_id_type=MESH))
        given = [offs_in[i] for i in range(items)]
        places = []
        for i in range(items):
            rank = jnp.int32(0)
            for j in range(items):
                if j != i:
                    before = given[j] <= given[i] if j < i else given[j] < given[i]
                    rank += jnp.where(before, 1, 0)
            places.append(jnp.where(rank % 2 == 0, rank // 2, items - 1 - rank // 2))
        starts, needs, end = [], [], jnp.int32(0)
        taken = []
        for k in range(items):
            here = [jnp.where(place == k, 1, 0) for place in places]
            item = sum(i * h for i, h in enumerate(here))
            offset = sum(given[i] * h for i, h in enumerate(here))
            taken.append(item)
            order[k] = item
            offs[k] = offset
            lens[k] = sum(lens_in[i] * h for i, h in enumerate(here))
            needs.append((offset + GROUP - 1) // GROUP)
            starts.append(end)
            end = end + needs[k]
            window[k] = end
        held[it] = jnp.full((1, LANES), end, jnp.int32)

        index = (
            lax.broadcasted_iota(jnp.int32, table, 0) * LANES
            + lax.broadcasted_iota(jnp.int32, table, 1))

        def looked_up(index, firsts):
            total, previous = index, jnp.int32(0)
            for k in range(items):
                shift = firsts[k] - starts[k]
                total = total + jnp.where(index >= starts[k], shift - previous, 0)
                previous = shift
            return jnp.minimum(total, groups - 1)

        lookup_v[...] = looked_up(
            index, [(k + 1) * per_item - needs[k] for k in range(items)])
        to_smem = pltpu.make_async_copy(lookup_v, lookup, table_sem)
        to_smem.start()
        load.wait()
        for k in range(items // 2):
            s2t[k * frames : (k + 1) * frames] = s2[taken[k]].T
        middle = items // 2 * frames
        first_out = pltpu.make_async_copy(
            s2t.at[pl.ds(0, middle)], s2t_h.at[pl.ds(0, middle)], out_sem.at[2])
        first_out.start()
        pl.semaphore_wait(barrier, n_it - 1)
        peers(lambda peer: copy(peer).start())
        for k in range(items // 2, items):
            s2t[k * frames : (k + 1) * frames] = s2[taken[k]].T
        to_smem.wait()
        own_out = pltpu.make_async_copy(
            s2t.at[pl.ds(middle, rows - middle)], s2t_h.at[pl.ds(middle, rows - middle)],
            out_sem.at[0])
        own_out.start()

        def turn(group, carry):
            source = lookup[group // LANES, group % LANES] * GROUP
            packed[pl.ds(pl.multiple_of(group * GROUP, GROUP), GROUP)] = s2t[
                pl.ds(source, GROUP)]
            return carry

        half = groups // 2
        lax.fori_loop(0, half, turn, 0, unroll=16)
        cut = pl.ds(0, half * GROUP)
        early_out = pltpu.make_async_copy(packed.at[cut], packed_h.at[cut], out_sem.at[3])
        early_out.start()
        lax.fori_loop(half, groups, turn, 0, unroll=16)
        cut = pl.ds(half * GROUP, rows - half * GROUP)
        packed_out = pltpu.make_async_copy(packed.at[cut], packed_h.at[cut], out_sem.at[1])
        packed_out.start()

        if n_it > 1:
            block = held.at[pl.ds(0, n_it - 1)]
            pltpu.make_async_copy(block, block, recv).wait()
        most = held[0]
        for peer in range(1, n_it):
            most = jnp.maximum(most, held[peer])
        choice = jnp.zeros((1, LANES), jnp.int32)
        sent = jnp.full((1, LANES), plan.caps[0] // GROUP, jnp.int32)
        for low_cap, cap in zip(plan.caps[:-1], plan.caps[1:]):
            more = most * GROUP > low_cap
            choice += more.astype(jnp.int32)
            sent += jnp.where(more, (cap - low_cap) // GROUP, 0)
        which[0] = jnp.max(choice)
        base = jnp.max(sent) - end
        for k in range(items):
            window_back[k] = base + starts[k]
        back = looked_up(index - base, [jnp.int32(k * per_item) for k in range(items)])
        pack[...] = jnp.where(index < base, 0, back)
        first_out.wait()
        own_out.wait()
        early_out.wait()
        packed_out.wait()
        if n_it > 1:
            pltpu.make_async_copy(block, block, send).wait()

    smem = pl.BlockSpec(memory_space=pltpu.SMEM)
    hbm = pl.BlockSpec(memory_space=pl.ANY)
    short = jax.ShapeDtypeStruct((items,), jnp.int32)
    flat = jax.ShapeDtypeStruct((rows, chans), F32)
    sem = pltpu.SemaphoreType.DMA
    return pl.pallas_call(
        body,
        out_shape=(
            flat, flat, jax.ShapeDtypeStruct(table, jnp.int32), short, short, short, short, short,
            jax.ShapeDtypeStruct((1,), jnp.int32),
        ),
        in_specs=[smem, smem, hbm],
        out_specs=(hbm, hbm, pl.BlockSpec(memory_space=pltpu.VMEM)) + (smem,) * 6,
        scratch_shapes=[
            pltpu.VMEM((items, chans, frames), F32), pltpu.VMEM((rows, chans), F32),
            pltpu.VMEM((rows, chans), F32), pltpu.VMEM(table, jnp.int32),
            pltpu.SMEM(table, jnp.int32), pltpu.VMEM((plan.n_it, 1, LANES), jnp.int32),
            sem, sem((4,)), sem, sem, sem,
        ],
        compiler_params=pltpu.CompilerParams(
            collective_id=0, has_side_effects=True, vmem_limit_bytes=62 * 2**20),
        name="prelude",
    )


def finisher(plan, rows):
    items, frames, chans, units = plan.items, plan.frames, plan.chans, plan.units
    blocks = units // LANES

    def body(
        order, offs, window, gmoved_h, from_right_h, total_h, small_h, res_h, skip_h, gs1_h, *rest
    ):
        outs, scratch = rest[:20], rest[20:]
        cat, gs2, total, small, passed, in_sem, out_sem, pass_sem, total_sem = scratch
        out_res, out_skip, out_gs1, out_gs2 = outs[:4]
        last = lax.axis_index("tm") == plan.n_tm - 1
        def through(kind, item):
            src, dst = ((res_h, out_res), (skip_h, out_skip), (gs1_h, out_gs1))[kind]
            held = passed.at[kind, item]
            return (
                pltpu.make_async_copy(src.at[item], held, pass_sem.at[0, kind, item]),
                pltpu.make_async_copy(held, dst.at[order[item]], pass_sem.at[1, kind, item]),
            )

        def loads(item):
            start = pl.multiple_of(window[item] * GROUP, GROUP)
            return (
                pltpu.make_async_copy(
                    gmoved_h.at[item], cat.at[item, pl.ds(0, frames)], in_sem.at[0, item]),
                pltpu.make_async_copy(
                    from_right_h.at[pl.ds(start, frames)], cat.at[item, pl.ds(frames, frames)],
                    in_sem.at[1, item]),
            )

        def store(item):
            return pltpu.make_async_copy(gs2.at[item], out_gs2.at[order[item]], out_sem.at[item])

        def start(item, carry):
            for copy in loads(item):
                copy.start()
            for kind in range(3):
                through(kind, item)[0].start()
            return carry

        total_copy = pltpu.make_async_copy(total_h, total, total_sem.at[0])
        total_copy.start()
        small_copy = pltpu.make_async_copy(small_h, small, total_sem.at[1])
        small_copy.start()
        lax.fori_loop(0, items, start, 0)

        def turn(item, carry):
            for copy in loads(item):
                copy.wait()
            for kind in range(3):
                arriving, leaving = through(kind, item)
                arriving.wait()
                leaving.start()

            @pl.when(last)
            def _():
                cat[item, frames:] = jnp.zeros((frames, chans), F32)

            gs2[item] = cat[item, pl.ds(offs[item], frames), :].T
            store(item).start()
            return carry

        lax.fori_loop(0, items, turn, 0)
        total_copy.wait()
        small_copy.wait()
        (
            gain_1, gain_2, g_in, gb_in, g_slope1, g_gamma1, g_beta1, g_taps, gb_depth, g_slope2,
            g_gamma2, g_beta2, g_res, gb_res, g_skip, gb_skip,
        ) = outs[4:]
        start_in = plan.in_start
        for b in range(blocks):
            cut = slice(b * LANES, (b + 1) * LANES)
            g_res[:, cut] = total[2 * b * chans : (2 * b + 1) * chans]
            g_skip[:, cut] = total[(2 * b + 1) * chans : (2 * b + 2) * chans]
            g_in[cut] = total[start_in + b * chans : start_in + (b + 1) * chans].T
            sums = small[b * SUM_ROWS : (b + 1) * SUM_ROWS]
            for out, row in (
                (gb_in, B_IN), (g_slope1, SLOPE_ONE), (g_gamma1, GAMMA_ONE), (g_beta1, BETA_ONE),
                (gb_depth, B_DEPTH), (g_slope2, SLOPE_TWO), (g_gamma2, GAMMA_TWO),
                (g_beta2, BETA_TWO),
            ):
                out[:, cut] = sums[row : row + 1]
            g_taps[:, cut] = sums[TAP : TAP + 3]
            (gain_1, gain_2, gb_res, gb_skip)[b][...] = sums[NARROW : NARROW + 1]

        def end(item, carry):
            store(item).wait()
            for kind in range(3):
                through(kind, item)[1].wait()
            return carry

        lax.fori_loop(0, items, end, 0)

    smem = pl.BlockSpec(memory_space=pltpu.SMEM)
    hbm = pl.BlockSpec(memory_space=pl.ANY)
    vmem = pl.BlockSpec(memory_space=pltpu.VMEM)
    big = jax.ShapeDtypeStruct((items, chans, frames), F32)

    def array(*shape):
        return jax.ShapeDtypeStruct(shape, F32)

    narrow, per_unit = array(1, chans), array(1, units)
    sem = pltpu.SemaphoreType.DMA
    return pl.pallas_call(
        body,
        out_shape=(big,) * 4 + (
            narrow, narrow, array(units, chans), per_unit, per_unit, per_unit, per_unit,
            array(3, units), per_unit, per_unit, per_unit, per_unit, array(chans, units), narrow,
            array(chans, units), narrow,
        ),
        in_specs=[smem] * 3 + [hbm] * 7,
        out_specs=(hbm,) * 4 + (vmem,) * 16,
        scratch_shapes=[
            pltpu.VMEM((items, 2 * frames, chans), F32), pltpu.VMEM((items, chans, frames), F32),
            pltpu.VMEM((rows, LANES), F32), pltpu.VMEM((plan.small, LANES), F32),
            pltpu.VMEM((3, items, chans, frames), F32),
            sem((2, items)), sem((items,)), sem((2, 3, items)), sem((2,)),
        ],
        compiler_params=pltpu.CompilerParams(vmem_limit_bytes=62 * 2**20),
        name="finisher",
    )


def per_device(
    mesh, source_one, source_two, offsets, lengths, gain_one, gain_two, w_in, b_in, slope_one,
    first_norm_gain, first_norm_bias, depthwise_weight, depthwise_bias, slope_two,
    second_norm_gain, second_norm_bias, w_res, b_res, w_skip, b_skip, cot_res, cot_skip,
):
    items, chans, frames = source_one.shape
    units = w_in.shape[0]
    plan = Plan(mesh, items, chans, frames, units)
    n_tm, n_it, wing = plan.n_tm, plan.n_it, DILATION_RATE
    full = items * frames
    s2t, packed, pack, order, offs, lens, window, window_back, which = prelude(plan)(
        offsets, lengths, source_two)

    def row(value):
        return value.reshape(1, -1)

    smem = pl.BlockSpec(memory_space=pltpu.SMEM)
    hbm = pl.BlockSpec(memory_space=pl.ANY)
    vmem = pl.BlockSpec(memory_space=pltpu.VMEM)
    rows = plan.segs * plan.seg

    def floats(*shape):
        return pltpu.VMEM(shape, F32)

    def shorts(*shape):
        return pltpu.VMEM(shape, BF16)

    big = jax.ShapeDtypeStruct((items, chans, frames), F32)
    sem = pltpu.SemaphoreType.DMA
    def block(sent, index):
        return pl.pallas_call(
            functools.partial(kernel, plan, sent),
            out_shape=(
                big, big, big, jax.ShapeDtypeStruct((items, frames, chans), F32),
                jax.ShapeDtypeStruct((full + frames, chans), F32),
                jax.ShapeDtypeStruct((rows, LANES), F32),
                jax.ShapeDtypeStruct((plan.small, LANES), F32),
            ),
            in_specs=[smem] * 5 + [hbm] * 5 + [vmem] * 16,
            out_specs=[hbm] * 7,
            scratch_shapes=[
                floats(items, chans, frames), floats(items, frames, chans),
                floats(items, chans, frames), floats(items, chans, frames),
                floats(sent, chans), floats(frames + sent, chans), floats(full, chans),
                floats(sent, chans),
                floats(2, chans, frames), floats(2, chans, frames), floats(2 * frames, chans),
                floats(5, chans, frames), floats(items, chans, frames),
                shorts(5, 2 * chans, frames),
                floats(frames, units), floats(4, frames + 2 * wing, units),
                floats(4, frames, units),
                floats(2, frames, units), floats(2, frames, units), floats(2, frames, units),
                floats(frames, units), shorts(items, frames, units),
                shorts(items, frames, units), floats(2 * chans, units),
                floats(2, frames + 2 * wing, units), shorts(frames, units),
                shorts(frames, units), shorts(4 * chans, frames),
                floats(items, 2, wing, chans), floats(items, 2, wing, chans),
                floats(2 * wing, units), floats(items, 2, wing, units),
                floats(items, n_tm, 4, LANES), floats(items + 2, n_tm, 8, LANES), floats(8, LANES), floats(16, units),
                floats(items, 2, LANES),
                shorts(3 * chans, units), shorts(2 * chans, units), shorts(2 * chans, units),
                floats(2 * chans, units), floats(6, chans, LANES),
                floats(2 * chans, units), floats(2 * chans, units),
                floats(2 * chans, LANES), floats(3, 2 * chans, LANES), floats(2, chans, LANES),
                floats(SUM_ROWS, units),
                floats(rows, LANES), floats(n_it, rows // n_it, LANES),
                floats(rows // n_it, LANES),
                floats(n_tm, rows // n_it // n_tm, LANES), floats(rows // n_it, LANES),
                floats(rows, LANES),
                floats(plan.small, LANES), floats(n_it, plan.small, LANES),
                floats(n_tm, plan.small // n_tm, LANES), floats(plan.small, LANES),
                sem((4,)), sem((4, items)), sem((plan.parts,)), sem((plan.parts,)),
                sem((plan.parts,)), sem((plan.parts,)), sem((2, items, 2)), sem((2, items, 2)),
                sem((2, items + 2)), sem((2, items + 2)), sem((plan.segs + 1, 4)),
                sem((plan.segs + 1, 4)),
            ],
            compiler_params=pltpu.CompilerParams(
                collective_id=1 + index, has_side_effects=True,
                vmem_limit_bytes=63 * 2**20),
            name="tcn_block",
        )

    branches = [block(sent, index) for index, sent in enumerate(plan.caps)]
    res, skip, gs1, gmoved, from_right, total, narrow = lax.switch(
        which[0], branches,
        order, offs, lens, window, pack, source_one, s2t.reshape(items, frames, chans), packed,
        cot_res, cot_skip,
        row(gain_one), row(gain_two), w_in, row(b_in), row(slope_one), row(first_norm_gain),
        row(first_norm_bias), depthwise_weight.T, row(depthwise_bias), row(slope_two),
        row(second_norm_gain), row(second_norm_bias), w_res, row(b_res), w_skip, row(b_skip),
    )
    outs = list(finisher(plan, rows)(
        order, offs, window_back, gmoved, from_right, total, narrow, res, skip, gs1))
    outs[11] = outs[11].T
    return tuple(out.reshape(-1) if out.shape[0] == 1 else out for out in outs)


def solution(mesh):
    split = P("items", None, "tm")
    in_specs = (split, split, P("items"), P("items")) + (P(),) * 16 + (split, split)
    out_specs = (split,) * 4 + (P(),) * 16
    return jax.shard_map(
        functools.partial(per_device, mesh), mesh=mesh, in_specs=in_specs, out_specs=out_specs,
        check_vma=False,
    )
```
